1024 devices in a mesh: shot: 4 (over x_hi), gx: 32 (over z, x_lo, core), gy: 8 (over y).
Axes of the slice: x: 8 (x_hi: 4, x_lo: 2; x = x_hi * 2 + x_lo), y: 8, z: 8, core: 2. Of those that a mesh axis runs over, the one named last changes fastest.
Arguments:
- p_adjoint: float32 [4, 128, 128, 128], P('shot', 'gx', 'gy'), may hold values from -6 to 6
- q_adjoint: float32 [4, 128, 128, 128], P('shot', 'gx', 'gy'), may hold values from -6 to 6
- p_previous: float32 [4, 128, 128, 128], P('shot', 'gx', 'gy'), may hold values from -6 to 6
- q_previous: float32 [4, 128, 128, 128], P('shot', 'gx', 'gy'), may hold values from -6 to 6
- forward_p: float32 [4, 2, 128, 128, 128], P('shot', None, 'gx', 'gy'), may hold values from -6 to 6
- courant: float32 [128, 128, 128], P('gx', 'gy'), may hold values from 0.04 to 0.12
- epsilon: float32 [128, 128, 128], P('gx', 'gy'), may hold values from 0.12 to 0.3
- delta_field: float32 [128, 128, 128], P('gx', 'gy'), may hold values from -0.08 to 0.1
- tilt_angle: float32 [128, 128, 128], P('gx', 'gy'), may hold values from -3.140625 to 3.140625
- azimuth: float32 [128, 128, 128], P('gx', 'gy'), may hold values from -3.140625 to 3.140625
- receiver_cells: int32 [4, 2048], P('shot'), may hold values from 0 to 16383
- receiver_values: float32 [4, 2, 2048], P('shot'), may hold values from -6 to 6
- boundary_cells: int32 [2048], replicated, may hold values from 0 to 2097151
- boundary_force: float32 [4, 2, 2048], P('shot'), may hold values from -6 to 6
- source_cells: int32 [4], P('shot'), may hold values from 0 to 16383
Outputs:
- p_final: float32 [4, 128, 128, 128], P('shot', 'gx', 'gy')
- q_final: float32 [4, 128, 128, 128], P('shot', 'gx', 'gy')
- grad_epsilon: float32 [128, 128, 128], P('gx', 'gy')
- grad_delta: float32 [128, 128, 128], P('gx', 'gy')
The draws below stay inside these ranges and needn't reach their ends.
Inputs may be any that keep to these rules, and one draw needn't show every extreme that they name: `receiver_cells`: x * 128 + y of a receiver at depth index 0. `boundary_cells`: (x * 128 + y) * 128 + z of a boundary layer cell; a cell may repeat. `source_cells`: x * 128 + y of the shot's source.
All inputs are finite; a program needn't handle non-finite values.
Results may differ from the reference program's by a relative error of at most 0.0003.
Values sent between devices are 32-bit elements; how exact they have to be, the bound alone decides.
No kernel may reach another device: no remote copies, remote signals or barrier semaphores. Data moves between devices by JAX's collectives and lax.ppermute only.
A program may use at most 32 MiB of HBM per device.

```python
import jax
import jax.numpy as jnp
from jax import lax

RECV = 2048
DRM = 2048
ITERS = 2
TAPER = 32
SHOTS = 4
NX = 128
NY = 128
NZ = 128


def set_ends(entries, rng, least, high):
    extent = entries.shape
    index_at = [jax.random.randint(jax.random.fold_in(rng, axis), (), 0, extent[axis]) for axis in range(len(extent))]
    entries = entries.at[tuple(index_at)].set(least)
    longest = extent.index(max(extent))
    index_at[longest] = (index_at[longest] + 1) % extent[longest]
    return entries.at[tuple(index_at)].set(high)


def block_scale(own_key, dims, cuts, least, high):
    def one(position, shards_of):
        heights = jax.random.uniform(jax.random.fold_in(jax.random.fold_in(own_key, 6), position), (shards_of,), jnp.float32, least / len(cuts), high / len(cuts))
        return jnp.repeat(jnp.exp(heights), dims[position] // shards_of).reshape((-1,) + (1,) * (len(dims) - position - 1))

    level = one(*cuts[0])
    for cut in cuts[1:]:
        level = level * one(*cut)
    return level


def gaussian(stream_key, shape, width, limit, split=(), kind=jnp.bfloat16):
    result = jax.random.normal(stream_key, shape, jnp.float32) * width
    if len(split) > 0:
        result = block_scale(stream_key, shape, split, -0.22, 0.18) * result
    return jnp.clip(result, min=-limit, max=limit).astype(kind)


def setup_inputs(seed: int = 0) -> dict:
    key_list = jax.random.split(jax.random.key(seed), 16)
    return {
        "p_adjoint": gaussian(key_list[0], (SHOTS, NX, NY, NZ), 1.0, 6.0, ((0, 4), (1, 32), (2, 8)), jnp.float32),
        "q_adjoint": gaussian(key_list[1], (SHOTS, NX, NY, NZ), 1.0, 6.0, ((0, 4), (1, 32), (2, 8)), jnp.float32),
        "p_previous": gaussian(key_list[2], (SHOTS, NX, NY, NZ), 1.0, 6.0, ((0, 4), (1, 32), (2, 8)), jnp.float32),
        "q_previous": gaussian(key_list[3], (SHOTS, NX, NY, NZ), 1.0, 6.0, ((0, 4), (1, 32), (2, 8)), jnp.float32),
        "forward_p": gaussian(key_list[4], (SHOTS, ITERS, NX, NY, NZ), 1.0, 6.0, ((0, 4), (2, 32), (3, 8)), jnp.float32),
        "courant": jnp.clip(0.04 + 0.08 * jax.random.uniform(key_list[5], (NX, NY, NZ), jnp.float32) ** block_scale(key_list[5], (NX, NY, NZ), ((0, 32), (1, 8)), -0.2, 0.2), 0.04, 0.12),
        "epsilon": jnp.clip(0.12 + 0.18 * jax.random.uniform(key_list[6], (NX, NY, NZ), jnp.float32) ** block_scale(key_list[6], (NX, NY, NZ), ((0, 32), (1, 8)), -0.2, 0.2), 0.12, 0.3),
        "delta_field": jnp.clip(-0.08 + 0.18 * jax.random.uniform(key_list[7], (NX, NY, NZ), jnp.float32) ** block_scale(key_list[7], (NX, NY, NZ), ((0, 32), (1, 8)), -0.2, 0.2), -0.08, 0.1),
        "tilt_angle": jnp.clip(jax.random.uniform(key_list[8], (NX, NY, NZ), jnp.float32, -3.140625, 3.140625), -3.140625, 3.140625),
        "azimuth": jnp.clip(jax.random.uniform(key_list[9], (NX, NY, NZ), jnp.float32, -3.140625, 3.140625), -3.140625, 3.140625),
        "receiver_cells": set_ends(jax.random.randint(key_list[10], (SHOTS, RECV), 0, NX * NY), jax.random.fold_in(key_list[10], 1), 0, (NX * NY) - 1).astype(jnp.int32),
        "receiver_values": gaussian(key_list[11], (SHOTS, ITERS, RECV), 1.0, 6.0, ((0, 4),), jnp.float32),
        "boundary_cells": set_ends(jax.random.randint(key_list[12], (DRM,), 0, NX * NY * NZ), jax.random.fold_in(key_list[12], 1), 0, (NX * NY * NZ) - 1).astype(jnp.int32),
        "boundary_force": gaussian(key_list[13], (SHOTS, ITERS, DRM), 1.0, 6.0, ((0, 4),), jnp.float32),
        "source_cells": set_ends(jax.random.randint(key_list[14], (SHOTS,), 0, NX * NY), jax.random.fold_in(key_list[14], 1), 0, (NX * NY) - 1).astype(jnp.int32),
    }


FIRST_WEIGHTS = (1.0 / 12.0, -2.0 / 3.0, 0.0, 2.0 / 3.0, -1.0 / 12.0)
SECOND_WEIGHTS = (-1.0 / 12.0, 4.0 / 3.0, -2.5, 4.0 / 3.0, -1.0 / 12.0)
AXIS_PAIRS = ((0, 0), (1, 1), (2, 2), (0, 1), (0, 2), (1, 2))

def depth_table(weights, length):
    rows = jnp.arange(length, dtype=jnp.int32)[:, None]
    cols = jnp.arange(length, dtype=jnp.int32)[None, :]
    offset = rows - cols
    table = jnp.zeros((length, length), jnp.float32)
    for number in range(5):
        if weights[number] != 0.0:
            table = table + jnp.where(offset == number - 2, jnp.float32(weights[number]), jnp.float32(0.0))
    return table

def stencil(field, along, weights):
    if along == field.ndim - 1:
        table = depth_table(weights, field.shape[along])
        return jnp.dot(field, table, precision=lax.Precision.HIGHEST, preferred_element_type=jnp.float32)
    length = field.shape[along] - 4
    summed = None
    for offset in range(5):
        if weights[offset] != 0.0:
            piece_term = weights[offset] * lax.slice_in_dim(field, offset, offset + length, axis=along)
            summed = piece_term if summed is None else summed + piece_term
    return summed

def trimmed(field, alongs):
    for along in alongs:
        field = lax.slice_in_dim(field, 2, field.shape[along] - 2, axis=along)
    return field

def pair_part(field, first_axis, second_axis):
    base_axis = field.ndim - 3
    if first_axis == second_axis:
        others = [base_axis + other for other in range(2) if other != first_axis]
        return trimmed(stencil(field, base_axis + first_axis, SECOND_WEIGHTS), others)
    remaining = 3 - first_axis - second_axis
    inner_part = stencil(field, base_axis + first_axis, FIRST_WEIGHTS)
    outer_part = stencil(inner_part, base_axis + second_axis, FIRST_WEIGHTS)
    alongs = [base_axis + remaining] if remaining < 2 else []
    return 2.0 * trimmed(outer_part, alongs)

def laplace(field):
    return pair_part(field, 0, 0) + pair_part(field, 1, 1) + pair_part(field, 2, 2)

def axis_products(tilt_angle, azimuth):
    sine = jnp.sin(tilt_angle)
    normal = (sine * jnp.cos(azimuth), sine * jnp.sin(azimuth), jnp.cos(tilt_angle))
    return [normal[first_axis] * normal[second_axis] for first_axis, second_axis in AXIS_PAIRS]

def axial_forward(field, products):
    summed = None
    for number, pair in enumerate(AXIS_PAIRS):
        piece_term = products[number] * pair_part(field, pair[0], pair[1])
        summed = piece_term if summed is None else summed + piece_term
    return summed

def axial_adjoint(field, products):
    summed = None
    for number, pair in enumerate(AXIS_PAIRS):
        piece_term = pair_part(products[number] * field, pair[0], pair[1])
        summed = piece_term if summed is None else summed + piece_term
    return summed

def pad_plane(field):
    return jnp.pad(field, [(0, 0)] * (field.ndim - 3) + [(2, 2), (2, 2), (0, 0)])

def inject(field, cell_x, cell_y, cell_z, values, start_x, start_y):
    shot_count, size_x, size_y, size_z = field.shape
    local_x = cell_x - start_x
    local_y = cell_y - start_y
    inside = (local_x >= 0) & (local_x < size_x) & (local_y >= 0) & (local_y < size_y)
    beyond = size_x * size_y * size_z
    flat = jnp.where(inside, (local_x * size_y + local_y) * size_z + cell_z, beyond).astype(jnp.int32)
    rows = jnp.broadcast_to(jnp.arange(shot_count, dtype=jnp.int32)[:, None], flat.shape)
    return field.reshape(shot_count, -1).at[rows, flat].add(values, mode='drop').reshape(field.shape)

def source_taper(source_cells, start_x, start_y, size_x, size_y, width_y, radius):
    source_x = source_cells // width_y
    source_y = source_cells % width_y
    coord_x = start_x + jnp.arange(size_x, dtype=jnp.int32)
    coord_y = start_y + jnp.arange(size_y, dtype=jnp.int32)
    offset_x = coord_x[None, :, None] - source_x[:, None, None]
    offset_y = coord_y[None, None, :] - source_y[:, None, None]
    squared = (offset_x * offset_x + offset_y * offset_y).astype(jnp.float32)
    return jnp.minimum(squared / float(radius * radius), 1.0)[..., None]

def reference(p_adjoint, q_adjoint, p_previous, q_previous, forward_p, courant, epsilon, delta_field, tilt_angle, azimuth, receiver_cells, receiver_values, boundary_cells, boundary_force, source_cells):
    padded_angles = pad_plane(jnp.stack([tilt_angle, azimuth]))
    pad_products = axis_products(padded_angles[0], padded_angles[1])
    inner_products = axis_products(tilt_angle, azimuth)
    p_weight = courant * (1.0 + 2.0 * epsilon)
    q_weight = courant * (1.0 + 2.0 * delta_field)
    twice = 2.0 * courant
    bound_x = (boundary_cells // (NY * NZ))[None, :]
    bound_y = (boundary_cells // NZ % NY)[None, :]
    bound_z = (boundary_cells % NZ)[None, :]
    anchor = jnp.zeros((), jnp.int32)

    def one_shot(inputs):
        p_now, q_now, p_old, q_old, stored, recv_cell, recv_value, force_value, source_cell = inputs
        p_now, q_now, p_old, q_old = (p_now[None], q_now[None], p_old[None], q_old[None])
        recv_cell = recv_cell[None]
        recv_x = recv_cell // NY
        recv_y = recv_cell % NY
        recv_z = jnp.zeros_like(recv_cell)
        taper = source_taper(source_cell[None], anchor, anchor, NX, NY, NY, TAPER)
        grad_e = jnp.zeros((NX, NY, NZ), jnp.float32)
        grad_d = jnp.zeros((NX, NY, NZ), jnp.float32)
        illum = jnp.zeros((NX, NY, NZ), jnp.float32)
        for step in range(ITERS):
            snapshot = stored[step][None]
            forward_pad = pad_plane(snapshot)
            image = twice * (laplace(forward_pad) - axial_forward(forward_pad, inner_products))
            grad_e = grad_e + lax.optimization_barrier(jnp.sum(taper * p_now * image, axis=0))
            grad_d = grad_d + lax.optimization_barrier(jnp.sum(taper * q_now * image, axis=0))
            illum = illum + lax.optimization_barrier(jnp.sum(snapshot * snapshot, axis=0))
            source_pad = pad_plane(p_weight * p_now + q_weight * q_now)
            mix_pad = pad_plane(courant * (p_now + q_now))
            p_next = 2.0 * p_now - p_old + laplace(source_pad) - axial_adjoint(source_pad, pad_products)
            p_next = inject(p_next, recv_x, recv_y, recv_z, recv_value[step][None], anchor, anchor)
            p_next = inject(p_next, bound_x, bound_y, bound_z, force_value[step][None], anchor, anchor)
            q_next = 2.0 * q_now - q_old + axial_adjoint(mix_pad, pad_products)
            p_old, q_old, p_now, q_now = (p_now, q_now, p_next, q_next)
        return (p_now[0], q_now[0], grad_e, grad_d, illum)
    p_final, q_final, grad_e, grad_d, illum = lax.map(one_shot, (p_adjoint, q_adjoint, p_previous, q_previous, forward_p, receiver_cells, receiver_values, boundary_force, source_cells))
    scale = jnp.sqrt(lax.optimization_barrier(jnp.sum(illum, axis=0)) + 1.0)
    return (p_final, q_final, lax.optimization_barrier(jnp.sum(grad_e, axis=0)) / scale, lax.optimization_barrier(jnp.sum(grad_d, axis=0)) / scale)
```

```python
import functools

import jax
import jax.numpy as jnp
from jax import lax
from jax.experimental import pallas as pl
from jax.experimental.pallas import tpu as pltpu
from jax.sharding import PartitionSpec as P

TAPER = 32
WIDE = 5
NARROW = 7
PAIRS = ((0, 0), (1, 1), (2, 2), (0, 1), (0, 2), (1, 2))


def call(kernel, outs, args, scratch=(), smem=(), flops=2_000_000):
    specs = [
        pl.BlockSpec(memory_space=pltpu.SMEM if i in smem else pltpu.VMEM) for i in range(len(args))
    ]
    shapes = [jax.ShapeDtypeStruct(shape, jnp.float32) for shape in outs]
    return pl.pallas_call(
        kernel,
        out_shape=shapes,
        in_specs=specs,
        out_specs=[pl.BlockSpec(memory_space=pltpu.VMEM)] * len(outs),
        scratch_shapes=list(scratch),
        compiler_params=pltpu.CompilerParams(vmem_limit_bytes=24 * 1024 * 1024),
        cost_estimate=pl.CostEstimate(flops=flops, bytes_accessed=2_000_000, transcendentals=0),
    )(*args)


def row_mask(shape, below):
    return lax.broadcasted_iota(jnp.int32, shape, len(shape) - 2) < below


def shift_y(tiles, step, keep=3):
    if step > 0:
        rolled = [pltpu.roll(tile, 8 - step, 1) for tile in tiles]
        mask = row_mask(tiles[0].shape, 8 - step)
        return [jnp.where(mask, rolled[i], rolled[(i + 1) % 3]) for i in range(keep)]
    rolled = [pltpu.roll(tile, -step, 1) for tile in tiles]
    mask = row_mask(tiles[0].shape, -step)
    return [jnp.where(mask, rolled[(i + 2) % 3], rolled[i]) for i in range(keep)]


def shift_z(tile, step):
    lane = lax.broadcasted_iota(jnp.int32, tile.shape, 2)
    rolled = pltpu.roll(tile, (-step) % 128, 2)
    inside = lane < 128 - step if step > 0 else lane >= -step
    return jnp.where(inside, rolled, 0.0)


def second(far_low, low, here, high, far_high):
    return (4.0 / 3.0) * (low + high) - (1.0 / 12.0) * (far_low + far_high) - 2.5 * here


def first(far_low, low, high, far_high):
    return (2.0 / 3.0) * (high - low) - (1.0 / 12.0) * (far_high - far_low)


def second_x(tile, count):
    return second(*[tile[i : i + count] for i in range(5)])


def first_x(tile, count):
    return first(*[tile[i : i + count] for i in (0, 1, 3, 4)])


def first_y(tiles, keep):
    low2, low1, high1, high2 = [shift_y(tiles, step, keep) for step in (-2, -1, 1, 2)]
    return [first(low2[i], low1[i], high1[i], high2[i]) for i in range(keep)]


def both(parts_second, parts_first):
    near_even = (4.0 / 3.0) * parts_second
    near_odd = (2.0 / 3.0) * parts_first
    far_even = (-1.0 / 12.0) * parts_second
    far_odd = (1.0 / 12.0) * parts_first
    return (far_even + far_odd, near_even - near_odd, near_even + near_odd, far_even - far_odd)


def adjoint(products, source, count, keep, plus):
    mid = slice(2, 2 + count)
    aa = []
    for axis in range(3):
        scaled = [products[axis][i] * source[i] for i in range(3)]
        aa.append(scaled if plus else [source[i] - scaled[i] for i in range(3)])
    factor = 2.0 if plus else -2.0
    doubled = [factor * tile for tile in source]
    n01 = [products[3][i] * doubled[i] for i in range(3)]
    n02 = [products[4][i] * doubled[i] for i in range(keep)]
    n12 = [products[5][i][mid] * doubled[i][mid] for i in range(3)]
    out = [second_x(aa[0][i], count) for i in range(keep)]
    second_y = [tile[mid] for tile in aa[1]]
    cross_y = [first_x(tile, count) for tile in n01]
    mixed = [both(second_y[i], cross_y[i]) for i in range(3)]
    out = [out[i] - 2.5 * second_y[i] for i in range(keep)]
    for number, step in enumerate((-2, -1, 1, 2)):
        moved = shift_y([mixed[i][number] for i in range(3)], step, keep)
        out = [out[i] + moved[i] for i in range(keep)]
    along_y = first_y(n12, keep)
    for i in range(keep):
        second_z = aa[2][i][mid]
        cross_z = first_x(n02[i], count) + along_y[i]
        terms = both(second_z, cross_z)
        out[i] = out[i] - 2.5 * second_z
        for number, step in enumerate((-2, -1, 1, 2)):
            out[i] = out[i] + shift_z(terms[number], step)
    return out


def forward_image(products, field, count):
    mid = slice(2, 2 + count)
    inner = [tile[mid] for tile in field]
    slope_x = [first_x(tile, count) for tile in field]
    moved = [shift_y(inner, step, 2) for step in (-2, -1, 1, 2)]
    cross = first_y(slope_x, 2)
    out = []
    for i in range(2):
        here = inner[i]
        along = [moved[k][i] for k in range(4)]
        curve_x = second_x(field[i], count)
        curve_y = second(along[0], along[1], here, along[2], along[3])
        slope_y = first(*along)
        depth = [shift_z(here, step) for step in (-2, -1, 1, 2)]
        curve_z = second(depth[0], depth[1], here, depth[2], depth[3])
        total = (1.0 - products[0][i]) * curve_x
        total = total + (1.0 - products[1][i]) * curve_y
        total = total + (1.0 - products[2][i]) * curve_z
        cross_z = []
        for slope in (slope_x[i], slope_y):
            cross_z.append(first(*[shift_z(slope, step) for step in (-2, -1, 1, 2)]))
        mixed = products[3][i] * cross[i] + products[4][i] * cross_z[0] + products[5][i] * cross_z[1]
        out.append(total - 2.0 * mixed)
    return out


def prepare_kernel(p, q, p_old, q_old, f, c, eps, delta, tilt, azimuth, loc, low, high):
    size_x = p.shape[0]
    p_now, q_now, speed = p[...], q[...], c[...]
    p_weight = speed * (1.0 + 2.0 * eps[...])
    q_weight = speed * (1.0 + 2.0 * delta[...])
    sine = jnp.sin(tilt[...])
    wide = (
        p_weight * p_now + q_weight * q_now,
        speed * (p_now + q_now),
        sine * jnp.cos(azimuth[...]),
        sine * jnp.sin(azimuth[...]),
        jnp.cos(tilt[...]),
    )
    narrow = (
        2.0 * p_now - p_old[...],
        2.0 * q_now - q_old[...],
        p_weight,
        q_weight,
        speed,
        f[0],
        f[1],
    )
    for number, cells in enumerate(wide):
        rows = slice(number * size_x, (number + 1) * size_x)
        loc[rows] = cells
        low[rows] = cells
        high[rows] = cells
    for number, cells in enumerate(narrow):
        start = (WIDE + number) * size_x
        loc[start : start + size_x] = cells
        begin = WIDE * size_x + 2 * number
        low[begin : begin + 2] = cells[0:2]
        high[begin : begin + 2] = cells[size_x - 2 : size_x]


def tiles_of(loc, below, above, size_x, part):
    ys = slice(8 * part, 8 * part + 8)
    wide, narrow = [], []
    for number in range(WIDE):
        rows = slice(number * size_x, (number + 1) * size_x)
        wide += [below[rows, ys, :], loc[rows, ys, :], above[rows, ys, :]]
    for number in range(NARROW):
        start = (WIDE + number) * size_x
        begin = WIDE * size_x + 2 * number
        narrow += [
            below[begin : begin + 2, ys, :],
            loc[start : start + size_x, ys, :],
            above[begin : begin + 2, ys, :],
        ]
    return jnp.concatenate(wide, axis=0), jnp.concatenate(narrow, axis=0)


def pack_kernel(loc, below, above, down, up):
    size_x = loc.shape[0] // (WIDE + NARROW)
    for part, target in ((0, down), (1, up)):
        wide, narrow = tiles_of(loc, below, above, size_x, part)
        half = wide.shape[0] // 2
        quarter = narrow.shape[0] // 4
        turned = pltpu.roll(wide, 4, 1)
        mask = row_mask((half, 8, 128), 4)
        if part == 0:
            target[0:half] = jnp.where(mask, wide[:half], turned[half:])
        else:
            target[0:half] = jnp.where(mask, turned[:half], wide[half:])
        out = None
        for group in range(4):
            rows = narrow[group * quarter : (group + 1) * quarter]
            turn = (2 * group - 6 * part) % 8
            rows = pltpu.roll(rows, turn, 1) if turn else rows
            out = rows if out is None else jnp.where(row_mask(rows.shape, 2 * group), out, rows)
        target[half : half + quarter] = out


def unpack(loc, below, above, from_above, from_below):
    size_x = loc.shape[0] // (WIDE + NARROW)
    wide_rows, narrow_rows = 3 * size_x, size_x + 4
    half = WIDE * wide_rows // 2
    quarter = NARROW * narrow_rows // 4
    mask = row_mask((half, 8, 128), 4)
    high, low = from_above[0:half], from_below[0:half]
    wide_edge = jnp.concatenate(
        [jnp.where(mask, high, pltpu.roll(low, 4, 1)), jnp.where(mask, pltpu.roll(high, 4, 1), low)],
        axis=0,
    )
    high, low = from_above[half : half + quarter], from_below[half : half + quarter]
    mask = row_mask((quarter, 8, 128), 4)
    edges = []
    for group in range(4):
        first_turn, second_turn = (-2 * group) % 8, (6 - 2 * group) % 8
        upper = pltpu.roll(high, first_turn, 1) if first_turn else high
        lower = pltpu.roll(low, second_turn, 1) if second_turn else low
        edges.append(jnp.where(mask, upper, lower))
    narrow_edge = jnp.concatenate(edges, axis=0)
    wide0, narrow0 = tiles_of(loc, below, above, size_x, 0)
    wide1, narrow1 = tiles_of(loc, below, above, size_x, 1)
    wide = [
        [t[n * wide_rows : (n + 1) * wide_rows] for t in (wide0, wide1, wide_edge)] for n in range(WIDE)
    ]
    narrow = [
        [t[n * narrow_rows : (n + 1) * narrow_rows] for t in (narrow0, narrow1, narrow_edge)]
        for n in range(NARROW)
    ]
    return wide, narrow


def inject_kernel(grid_y, grid_z, size_x, size_y, recv_cells, recv_values, bound_cells, bound_force, out):
    bits_y, bits_z = grid_y.bit_length() - 1, grid_z.bit_length() - 1
    start_x = lax.axis_index("gx") * size_x
    start_y = lax.axis_index("gy") * size_y
    ring = (size_x + 4) * 24
    inner = size_x * size_y
    chunk = 512
    total = jnp.zeros((3 * (ring + inner), grid_z), jnp.float32)
    for cells_ref, values_ref, shift in ((recv_cells, recv_values, 0), (bound_cells, bound_force, bits_z)):
        for begin in range(0, cells_ref.shape[-1], chunk):
            cells = cells_ref[0:1, begin : begin + chunk]
            across = cells >> shift
            depth = cells & (grid_z - 1) if shift else jnp.zeros_like(cells)
            cell_x = (across >> bits_y) - start_x
            cell_y = (across & (grid_y - 1)) - start_y
            near = (cell_x >= -2) & (cell_x < size_x + 2) & (cell_y >= -2) & (cell_y < size_y + 2)
            wrapped = jnp.where(cell_y < 0, cell_y + 24, cell_y)
            ring_row = jnp.where(near, (cell_x + 2) * 24 + wrapped, -1)
            inside = (cell_x >= 0) & (cell_x < size_x) & (cell_y >= 0) & (cell_y < size_y)
            inner_row = jnp.where(inside, cell_x * size_y + cell_y, -1)
            ring_hit = lax.broadcasted_iota(jnp.int32, (ring, chunk), 0) == ring_row
            inner_hit = lax.broadcasted_iota(jnp.int32, (inner, chunk), 0) == inner_row
            columns = lax.broadcasted_iota(jnp.int32, (grid_z, chunk), 0) == depth
            columns = jnp.where(columns, 1.0, 0.0).astype(jnp.bfloat16)
            pieces = []
            parts = []
            for step in range(2):
                value = values_ref[step : step + 1, begin : begin + chunk]
                split = []
                for _ in range(3):
                    top = value.astype(jnp.bfloat16).astype(jnp.float32)
                    split.append(top)
                    value = value - top
                parts.append(split)
            for number in range(3):
                pieces.append(jnp.where(ring_hit, parts[0][number], 0.0).astype(jnp.bfloat16))
                pieces.append(jnp.where(inner_hit, parts[1][number], 0.0).astype(jnp.bfloat16))
            total = total + lax.dot_general(
                jnp.concatenate(pieces, axis=0),
                columns,
                (((1,), (1,)), ((), ())),
                preferred_element_type=jnp.float32,
            )
    rows = ring + inner
    out[...] = total[0:rows] + total[rows : 2 * rows] + total[2 * rows : 3 * rows]


def first_step_kernel(
    grid_y, source, loc, below, above, from_above, from_below, inject, p, q, grads, now, ahead, weights
):
    size_x, size_y = p.shape[0], p.shape[1]
    wide, narrow = unpack(loc, below, above, from_above, from_below)
    source_tiles, mix_tiles = wide[0], wide[1]
    products = [[wide[2 + a][i] * wide[2 + b][i] for i in range(3)] for a, b in PAIRS]
    p_base, q_base, p_weight, q_weight, speed, f0, f1 = narrow
    count = size_x + 4
    mid = slice(2, 2 + size_x)
    p_next = adjoint(products, source_tiles, count, 3, False)
    q_next = adjoint(products, mix_tiles, count, 3, True)
    ring = inject[0 : count * 24].reshape(count, 24, 128)
    p_next = [p_base[i] + p_next[i] + ring[:, 8 * i : 8 * i + 8] for i in range(3)]
    q_next = [q_base[i] + q_next[i] for i in range(3)]
    near = [[tile[2 : 2 + count] for tile in entry] for entry in products]
    inner = [[tile[mid] for tile in entry] for entry in near]
    bits_y = grid_y.bit_length() - 1
    source_x = (source[0] >> bits_y) - lax.axis_index("gx") * size_x
    source_y = (source[0] & (grid_y - 1)) - lax.axis_index("gy") * size_y
    images = [forward_image(inner, field, size_x) for field in (f0, f1)]
    shape = (size_x, 8, 128)
    offset_x = lax.broadcasted_iota(jnp.int32, shape, 0) - source_x
    for i in range(2):
        ys = slice(8 * i, 8 * i + 8)
        offset_y = lax.broadcasted_iota(jnp.int32, shape, 1) + (8 * i - source_y)
        squared = (offset_x * offset_x + offset_y * offset_y).astype(jnp.float32)
        taper = jnp.minimum(squared * (1.0 / float(TAPER * TAPER)), 1.0)
        scale = taper * (2.0 * speed[i][mid])
        image0, image1 = scale * images[0][i], scale * images[1][i]
        p_mid, q_mid = p_next[i][mid], q_next[i][mid]
        grads[0, :, ys, :] = p[:, ys, :] * image0 + p_mid * image1
        grads[1, :, ys, :] = q[:, ys, :] * image0 + q_mid * image1
        g0, g1 = f0[i][mid], f1[i][mid]
        grads[2, :, ys, :] = g0 * g0 + g1 * g1
        now[0, :, ys, :] = p_mid
        now[1, :, ys, :] = q_mid
    for i in range(3):
        ahead[0, i] = p_weight[i] * p_next[i] + q_weight[i] * q_next[i]
        ahead[1, i] = speed[i] * (p_next[i] + q_next[i])
        for number in range(6):
            weights[number, i] = near[number][i]


def second_step_kernel(now, ahead, weights, inject, p, q, p_out, q_out):
    size_x, size_y = p.shape[0], p.shape[1]
    products = [[weights[number, i] for i in range(3)] for number in range(6)]
    p_next = adjoint(products, [ahead[0, i] for i in range(3)], size_x, 2, False)
    q_next = adjoint(products, [ahead[1, i] for i in range(3)], size_x, 2, True)
    inner = inject[inject.shape[0] - size_x * size_y :].reshape(size_x, size_y, 128)
    for i in range(2):
        ys = slice(8 * i, 8 * i + 8)
        p_out[:, ys, :] = 2.0 * now[0, :, ys, :] - p[:, ys, :] + inner[:, ys] + p_next[i]
        q_out[:, ys, :] = 2.0 * now[1, :, ys, :] - q[:, ys, :] + q_next[i]


def both_ways(low, high, axis):
    count = lax.axis_size(axis)
    below = lax.ppermute(high, axis, [(i, i + 1) for i in range(count - 1)])
    above = lax.ppermute(low, axis, [(i + 1, i) for i in range(count - 1)])
    return below, above


def shot_sum(part):
    count = lax.axis_size("shot")
    if count != 4:
        return lax.psum(part, "shot")
    part = part + lax.ppermute(part, "shot", [(0, 1), (1, 0), (2, 3), (3, 2)])
    return part + lax.ppermute(part, "shot", [(0, 3), (3, 0), (1, 2), (2, 1)])


def body(
    p_adjoint,
    q_adjoint,
    p_previous,
    q_previous,
    forward_p,
    courant,
    epsilon,
    delta_field,
    tilt_angle,
    azimuth,
    receiver_cells,
    receiver_values,
    boundary_cells,
    boundary_force,
    source_cells,
):
    _, size_x, size_y, size_z = p_adjoint.shape
    grid_y = size_y * lax.axis_size("gy")
    p, q, p_old, q_old, f = (
        entry[0] for entry in (p_adjoint, q_adjoint, p_previous, q_previous, forward_p)
    )
    fields = WIDE + NARROW
    message = WIDE * size_x + NARROW * 2
    loc, low, high = call(
        prepare_kernel,
        [(fields * size_x, size_y, size_z)] + [(message, size_y, size_z)] * 2,
        (p, q, p_old, q_old, f, courant, epsilon, delta_field, tilt_angle, azimuth),
    )
    below, above = both_ways(low, high, "gx")
    rows = (size_x + 4) * 24 + size_x * size_y
    (inject,) = call(
        functools.partial(inject_kernel, grid_y, size_z, size_x, size_y),
        [(rows, size_z)],
        (receiver_cells, receiver_values[0], boundary_cells[None], boundary_force[0]),
        flops=800_000_000,
    )
    tiles = WIDE * 3 * size_x // 2 + NARROW * (size_x + 4) // 4
    down, up = call(pack_kernel, [(tiles, 8, size_z)] * 2, (loc, below, above))
    from_below, from_above = both_ways(down, up, "gy")
    count = size_x + 4
    grads, now, ahead, weights = call(
        functools.partial(first_step_kernel, grid_y),
        [
            (3, size_x, size_y, size_z),
            (2, size_x, size_y, size_z),
            (2, 3, count, 8, size_z),
            (6, 3, count, 8, size_z),
        ],
        (source_cells, loc, below, above, from_above, from_below, inject, p, q),
        smem=(0,),
    )
    total = shot_sum(grads)
    p_final, q_final = call(
        second_step_kernel, [(size_x, size_y, size_z)] * 2, (now, ahead, weights, inject, p, q)
    )
    scale = jnp.sqrt(total[2] + 1.0)
    return (p_final[None], q_final[None], total[0] / scale, total[1] / scale)


def solution(mesh):
    in_specs = (
        P("shot", "gx", "gy", None),
        P("shot", "gx", "gy", None),
        P("shot", "gx", "gy", None),
        P("shot", "gx", "gy", None),
        P("shot", None, "gx", "gy", None),
        P("gx", "gy", None),
        P("gx", "gy", None),
        P("gx", "gy", None),
        P("gx", "gy", None),
        P("gx", "gy", None),
        P("shot", None),
        P("shot", None, None),
        P(),
        P("shot", None, None),
        P("shot"),
    )
    out_specs = (
        P("shot", "gx", "gy", None),
        P("shot", "gx", "gy", None),
        P("gx", "gy", None),
        P("gx", "gy", None),
    )
    return jax.shard_map(body, mesh=mesh, in_specs=in_specs, out_specs=out_specs, check_vma=False)
```

```python
import functools

import jax
import jax.numpy as jnp
from jax import lax
from jax.experimental import pallas as pl
from jax.experimental.pallas import tpu as pltpu
from jax.sharding import PartitionSpec as P

TAPER = 32
WIDE = 5
NARROW = 7
FIELDS = WIDE + NARROW + 2
INPUTS = ("p", "q", "p_old", "q_old", "f", "c", "eps", "delta", "tilt", "azimuth")
PAIRS = ((0, 0), (1, 1), (2, 2), (0, 1), (0, 2), (1, 2))


def call(kernel, outs, args, scratch=(), smem=(), flops=2_000_000, space=pltpu.VMEM):
    specs = [
        pl.BlockSpec(memory_space=pltpu.SMEM if i in smem else space) for i in range(len(args))
    ]
    shapes = [jax.ShapeDtypeStruct(shape, jnp.float32) for shape in outs]
    return pl.pallas_call(
        kernel,
        out_shape=shapes,
        in_specs=specs,
        out_specs=[pl.BlockSpec(memory_space=pltpu.VMEM)] * len(outs),
        scratch_shapes=list(scratch),
        compiler_params=pltpu.CompilerParams(vmem_limit_bytes=24 * 1024 * 1024),
        cost_estimate=pl.CostEstimate(flops=flops, bytes_accessed=2_000_000, transcendentals=0),
    )(*(pltpu.with_memory_space_constraint(x, space) if space == pltpu.HBM else x for x in args))


def row_mask(shape, below):
    return lax.broadcasted_iota(jnp.int32, shape, len(shape) - 2) < below


def shift_y(tiles, step, keep=3):
    if step > 0:
        rolled = [pltpu.roll(tile, 8 - step, 1) for tile in tiles]
        mask = row_mask(tiles[0].shape, 8 - step)
        return [jnp.where(mask, rolled[i], rolled[(i + 1) % 3]) for i in range(keep)]
    rolled = [pltpu.roll(tile, -step, 1) for tile in tiles]
    mask = row_mask(tiles[0].shape, -step)
    return [jnp.where(mask, rolled[(i + 2) % 3], rolled[i]) for i in range(keep)]


def shift_z(tile, step):
    lane = lax.broadcasted_iota(jnp.int32, tile.shape, 2)
    rolled = pltpu.roll(tile, (-step) % 128, 2)
    inside = lane < 128 - step if step > 0 else lane >= -step
    return jnp.where(inside, rolled, 0.0)


def second(far_low, low, here, high, far_high):
    return (4.0 / 3.0) * (low + high) - (1.0 / 12.0) * (far_low + far_high) - 2.5 * here


def first(far_low, low, high, far_high):
    return (2.0 / 3.0) * (high - low) - (1.0 / 12.0) * (far_high - far_low)


def second_x(tile, count):
    return second(*[tile[i : i + count] for i in range(5)])


def first_x(tile, count):
    return first(*[tile[i : i + count] for i in (0, 1, 3, 4)])


def first_y(tiles, keep):
    low2, low1, high1, high2 = [shift_y(tiles, step, keep) for step in (-2, -1, 1, 2)]
    return [first(low2[i], low1[i], high1[i], high2[i]) for i in range(keep)]


def both(parts_second, parts_first):
    near_even = (4.0 / 3.0) * parts_second
    near_odd = (2.0 / 3.0) * parts_first
    far_even = (-1.0 / 12.0) * parts_second
    far_odd = (1.0 / 12.0) * parts_first
    return (far_even + far_odd, near_even - near_odd, near_even + near_odd, far_even - far_odd)


def adjoint(products, source, count, keep, plus):
    mid = slice(2, 2 + count)
    aa = []
    for axis in range(3):
        scaled = [products[axis][i] * source[i] for i in range(3)]
        aa.append(scaled if plus else [source[i] - scaled[i] for i in range(3)])
    factor = 2.0 if plus else -2.0
    doubled = [factor * tile for tile in source]
    n01 = [products[3][i] * doubled[i] for i in range(3)]
    n02 = [products[4][i] * doubled[i] for i in range(keep)]
    n12 = [products[5][i][mid] * doubled[i][mid] for i in range(3)]
    out = [second_x(aa[0][i], count) for i in range(keep)]
    second_y = [tile[mid] for tile in aa[1]]
    cross_y = [first_x(tile, count) for tile in n01]
    mixed = [both(second_y[i], cross_y[i]) for i in range(3)]
    out = [out[i] - 2.5 * second_y[i] for i in range(keep)]
    for number, step in enumerate((-2, -1, 1, 2)):
        moved = shift_y([mixed[i][number] for i in range(3)], step, keep)
        out = [out[i] + moved[i] for i in range(keep)]
    along_y = first_y(n12, keep)
    for i in range(keep):
        second_z = aa[2][i][mid]
        cross_z = first_x(n02[i], count) + along_y[i]
        terms = both(second_z, cross_z)
        out[i] = out[i] - 2.5 * second_z
        for number, step in enumerate((-2, -1, 1, 2)):
            out[i] = out[i] + shift_z(terms[number], step)
    return out


def forward_image(products, field, count):
    mid = slice(2, 2 + count)
    inner = [tile[mid] for tile in field]
    slope_x = [first_x(tile, count) for tile in field]
    moved = [shift_y(inner, step, 2) for step in (-2, -1, 1, 2)]
    cross = first_y(slope_x, 2)
    out = []
    for i in range(2):
        here = inner[i]
        along = [moved[k][i] for k in range(4)]
        curve_x = second_x(field[i], count)
        curve_y = second(along[0], along[1], here, along[2], along[3])
        slope_y = first(*along)
        depth = [shift_z(here, step) for step in (-2, -1, 1, 2)]
        curve_z = second(depth[0], depth[1], here, depth[2], depth[3])
        total = (1.0 - products[0][i]) * curve_x
        total = total + (1.0 - products[1][i]) * curve_y
        total = total + (1.0 - products[2][i]) * curve_z
        cross_z = []
        for slope in (slope_x[i], slope_y):
            cross_z.append(first(*[shift_z(slope, step) for step in (-2, -1, 1, 2)]))
        mixed = products[3][i] * cross[i] + products[4][i] * cross_z[0] + products[5][i] * cross_z[1]
        out.append(total - 2.0 * mixed)
    return out


def prepare_kernel(*refs):
    count = len(INPUTS)
    arrays, (loc, far, near), held, arrived = refs[:count], refs[count : count + 3], refs[-count - 1 : -1], refs[-1]
    copies = [pltpu.make_async_copy(arrays[i], held[i], arrived.at[i]) for i in range(count)]
    for copy in copies:
        copy.start()
    for copy in copies:
        copy.wait()
    p, q, p_old, q_old, f, c, eps, delta, tilt, azimuth = held
    size_x = p.shape[0]
    p_now, q_now, speed = p[...], q[...], c[...]
    p_weight = speed * (1.0 + 2.0 * eps[...])
    q_weight = speed * (1.0 + 2.0 * delta[...])
    sine = jnp.sin(tilt[...])
    wide = (
        p_weight * p_now + q_weight * q_now,
        speed * (p_now + q_now),
        sine * jnp.cos(azimuth[...]),
        sine * jnp.sin(azimuth[...]),
        jnp.cos(tilt[...]),
    )
    narrow = (
        2.0 * p_now - p_old[...],
        2.0 * q_now - q_old[...],
        p_weight,
        q_weight,
        speed,
        f[0],
        f[1],
    )
    for number, cells in enumerate(wide):
        rows = slice(number * size_x, (number + 1) * size_x)
        loc[rows] = cells
        near[rows] = cells
        far[rows] = cells
    for number, cells in enumerate(narrow + (p_now, q_now)):
        start = (WIDE + number) * size_x
        loc[start : start + size_x] = cells
    odd = lax.rem(lax.axis_index("gx"), 2)
    upper, lower = (1 - odd) * (size_x - 2), odd * (size_x - 2)
    for number in range(NARROW):
        start = (WIDE + number) * size_x
        begin = WIDE * size_x + 2 * number
        near[begin : begin + 2] = loc[pl.ds(start + upper, 2)]
        far[begin : begin + 2] = loc[pl.ds(start + lower, 2)]


def tiles_of(loc, near, far, size_x, part):
    ys = slice(8 * part, 8 * part + 8)
    odd = lax.rem(lax.axis_index("gx"), 2) == 1
    first, second = near[:, ys, :], far[:, ys, :]
    below, above = jnp.where(odd, first, second), jnp.where(odd, second, first)
    wide, narrow = [], []
    for number in range(WIDE):
        rows = slice(number * size_x, (number + 1) * size_x)
        wide += [below[rows], loc[rows, ys, :], above[rows]]
    for number in range(NARROW):
        start = (WIDE + number) * size_x
        begin = WIDE * size_x + 2 * number
        narrow += [
            below[begin : begin + 2],
            loc[start : start + size_x, ys, :],
            above[begin : begin + 2],
        ]
    return jnp.concatenate(wide, axis=0), jnp.concatenate(narrow, axis=0)


def pack_kernel(loc, far, near, evens, odds):
    size_x = loc.shape[0] // FIELDS
    made = []
    for part in range(2):
        wide, narrow = tiles_of(loc, near, far, size_x, part)
        half = wide.shape[0] // 2
        quarter = narrow.shape[0] // 4
        turned = pltpu.roll(wide, 4, 1)
        mask = row_mask((half, 8, 128), 4)
        if part == 0:
            top = jnp.where(mask, wide[:half], turned[half:])
        else:
            top = jnp.where(mask, turned[:half], wide[half:])
        out = None
        for group in range(4):
            rows = narrow[group * quarter : (group + 1) * quarter]
            turn = (2 * group - 6 * part) % 8
            rows = pltpu.roll(rows, turn, 1) if turn else rows
            out = rows if out is None else jnp.where(row_mask(rows.shape, 2 * group), out, rows)
        made.append((top, out))
    odd = lax.rem(lax.axis_index("gy"), 2) == 1
    down, up = made
    for rows, a, b in ((slice(0, half), down[0], up[0]), (slice(half, half + quarter), down[1], up[1])):
        evens[rows] = jnp.where(odd, a, b)
        odds[rows] = jnp.where(odd, b, a)


def unpack(loc, near, far, evens, odds):
    size_x = loc.shape[0] // FIELDS
    odd = lax.rem(lax.axis_index("gy"), 2) == 1
    from_above = jnp.where(odd, odds[...], evens[...])
    from_below = jnp.where(odd, evens[...], odds[...])
    wide_rows, narrow_rows = 3 * size_x, size_x + 4
    half = WIDE * wide_rows // 2
    quarter = NARROW * narrow_rows // 4
    mask = row_mask((half, 8, 128), 4)
    high, low = from_above[0:half], from_below[0:half]
    wide_edge = jnp.concatenate(
        [jnp.where(mask, high, pltpu.roll(low, 4, 1)), jnp.where(mask, pltpu.roll(high, 4, 1), low)],
        axis=0,
    )
    high, low = from_above[half : half + quarter], from_below[half : half + quarter]
    mask = row_mask((quarter, 8, 128), 4)
    edges = []
    for group in range(4):
        first_turn, second_turn = (-2 * group) % 8, (6 - 2 * group) % 8
        upper = pltpu.roll(high, first_turn, 1) if first_turn else high
        lower = pltpu.roll(low, second_turn, 1) if second_turn else low
        edges.append(jnp.where(mask, upper, lower))
    narrow_edge = jnp.concatenate(edges, axis=0)
    wide0, narrow0 = tiles_of(loc, near, far, size_x, 0)
    wide1, narrow1 = tiles_of(loc, near, far, size_x, 1)
    wide = [
        [t[n * wide_rows : (n + 1) * wide_rows] for t in (wide0, wide1, wide_edge)] for n in range(WIDE)
    ]
    narrow = [
        [t[n * narrow_rows : (n + 1) * narrow_rows] for t in (narrow0, narrow1, narrow_edge)]
        for n in range(NARROW)
    ]
    return wide, narrow


def inject_kernel(grid_y, grid_z, size_x, size_y, recv_cells, recv_values, bound_cells, bound_force, out):
    bits_y, bits_z = grid_y.bit_length() - 1, grid_z.bit_length() - 1
    start_x = lax.axis_index("gx") * size_x
    start_y = lax.axis_index("gy") * size_y
    ring = (size_x + 4) * 24
    inner = size_x * size_y
    chunk = 512
    total = jnp.zeros((3 * (ring + inner), grid_z), jnp.float32)
    for cells_ref, values_ref, shift in ((recv_cells, recv_values, 0), (bound_cells, bound_force, bits_z)):
        for begin in range(0, cells_ref.shape[-1], chunk):
            cells = cells_ref[0:1, begin : begin + chunk]
            across = cells >> shift
            depth = cells & (grid_z - 1) if shift else jnp.zeros_like(cells)
            cell_x = (across >> bits_y) - start_x
            cell_y = (across & (grid_y - 1)) - start_y
            near = (cell_x >= -2) & (cell_x < size_x + 2) & (cell_y >= -2) & (cell_y < size_y + 2)
            wrapped = jnp.where(cell_y < 0, cell_y + 24, cell_y)
            ring_row = jnp.where(near, (cell_x + 2) * 24 + wrapped, -1)
            inside = (cell_x >= 0) & (cell_x < size_x) & (cell_y >= 0) & (cell_y < size_y)
            inner_row = jnp.where(inside, cell_x * size_y + cell_y, -1)
            ring_hit = lax.broadcasted_iota(jnp.int32, (ring, chunk), 0) == ring_row
            inner_hit = lax.broadcasted_iota(jnp.int32, (inner, chunk), 0) == inner_row
            columns = lax.broadcasted_iota(jnp.int32, (grid_z, chunk), 0) == depth
            columns = jnp.where(columns, 1.0, 0.0).astype(jnp.bfloat16)
            pieces = []
            parts = []
            for step in range(2):
                value = values_ref[step : step + 1, begin : begin + chunk]
                split = []
                for _ in range(3):
                    top = value.astype(jnp.bfloat16).astype(jnp.float32)
                    split.append(top)
                    value = value - top
                parts.append(split)
            for number in range(3):
                pieces.append(jnp.where(ring_hit, parts[0][number], 0.0).astype(jnp.bfloat16))
                pieces.append(jnp.where(inner_hit, parts[1][number], 0.0).astype(jnp.bfloat16))
            total = total + lax.dot_general(
                jnp.concatenate(pieces, axis=0),
                columns,
                (((1,), (1,)), ((), ())),
                preferred_element_type=jnp.float32,
            )
    rows = ring + inner
    out[...] = total[0:rows] + total[rows : 2 * rows] + total[2 * rows : 3 * rows]


def first_step_kernel(
    grid_y, source, loc, far_x, near_x, evens, odds, inject, grads, now, ahead, weights
):
    size_x, size_y = loc.shape[0] // FIELDS, loc.shape[1]
    wide, narrow = unpack(loc, near_x, far_x, evens, odds)
    p = loc[(FIELDS - 2) * size_x : (FIELDS - 1) * size_x]
    q = loc[(FIELDS - 1) * size_x : FIELDS * size_x]
    source_tiles, mix_tiles = wide[0], wide[1]
    products = [[wide[2 + a][i] * wide[2 + b][i] for i in range(3)] for a, b in PAIRS]
    p_base, q_base, p_weight, q_weight, speed, f0, f1 = narrow
    count = size_x + 4
    mid = slice(2, 2 + size_x)
    p_next = adjoint(products, source_tiles, count, 3, False)
    q_next = adjoint(products, mix_tiles, count, 3, True)
    ring = inject[0 : count * 24].reshape(count, 24, 128)
    p_next = [p_base[i] + p_next[i] + ring[:, 8 * i : 8 * i + 8] for i in range(3)]
    q_next = [q_base[i] + q_next[i] for i in range(3)]
    near = [[tile[2 : 2 + count] for tile in entry] for entry in products]
    inner = [[tile[mid] for tile in entry] for entry in near]
    bits_y = grid_y.bit_length() - 1
    source_x = (source[0] >> bits_y) - lax.axis_index("gx") * size_x
    source_y = (source[0] & (grid_y - 1)) - lax.axis_index("gy") * size_y
    images = [forward_image(inner, field, size_x) for field in (f0, f1)]
    shape = (size_x, 8, 128)
    offset_x = lax.broadcasted_iota(jnp.int32, shape, 0) - source_x
    for i in range(2):
        ys = slice(8 * i, 8 * i + 8)
        offset_y = lax.broadcasted_iota(jnp.int32, shape, 1) + (8 * i - source_y)
        squared = (offset_x * offset_x + offset_y * offset_y).astype(jnp.float32)
        taper = jnp.minimum(squared * (1.0 / float(TAPER * TAPER)), 1.0)
        scale = taper * (2.0 * speed[i][mid])
        image0, image1 = scale * images[0][i], scale * images[1][i]
        p_mid, q_mid = p_next[i][mid], q_next[i][mid]
        grads[0, :, ys, :] = p[:, ys, :] * image0 + p_mid * image1
        grads[1, :, ys, :] = q[:, ys, :] * image0 + q_mid * image1
        g0, g1 = f0[i][mid], f1[i][mid]
        grads[2, :, ys, :] = g0 * g0 + g1 * g1
        now[0, :, ys, :] = p_mid
        now[1, :, ys, :] = q_mid
    for i in range(3):
        ahead[0, i] = p_weight[i] * p_next[i] + q_weight[i] * q_next[i]
        ahead[1, i] = speed[i] * (p_next[i] + q_next[i])
        for number in range(6):
            weights[number, i] = near[number][i]


def second_step_kernel(now, ahead, weights, inject, loc, p_out, q_out):
    size_x, size_y = p_out.shape[0], p_out.shape[1]
    p = loc[(FIELDS - 2) * size_x : (FIELDS - 1) * size_x]
    q = loc[(FIELDS - 1) * size_x : FIELDS * size_x]
    products = [[weights[number, i] for i in range(3)] for number in range(6)]
    p_next = adjoint(products, [ahead[0, i] for i in range(3)], size_x, 2, False)
    q_next = adjoint(products, [ahead[1, i] for i in range(3)], size_x, 2, True)
    inner = inject[inject.shape[0] - size_x * size_y :].reshape(size_x, size_y, 128)
    for i in range(2):
        ys = slice(8 * i, 8 * i + 8)
        p_out[:, ys, :] = 2.0 * now[0, :, ys, :] - p[:, ys, :] + inner[:, ys] + p_next[i]
        q_out[:, ys, :] = 2.0 * now[1, :, ys, :] - q[:, ys, :] + q_next[i]


def swap(part, axis, start):
    lows = range(start, lax.axis_size(axis) - 1, 2)
    return lax.ppermute(part, axis, [(i, i + 1) for i in lows] + [(i + 1, i) for i in lows])


def shot_sum(part):
    count = lax.axis_size("shot")
    if count != 4:
        return lax.psum(part, "shot")
    part = part + lax.ppermute(part, "shot", [(0, 1), (1, 0), (2, 3), (3, 2)])
    return part + lax.ppermute(part, "shot", [(0, 3), (3, 0), (1, 2), (2, 1)])


def body(
    p_adjoint,
    q_adjoint,
    p_previous,
    q_previous,
    forward_p,
    courant,
    epsilon,
    delta_field,
    tilt_angle,
    azimuth,
    receiver_cells,
    receiver_values,
    boundary_cells,
    boundary_force,
    source_cells,
):
    _, size_x, size_y, size_z = p_adjoint.shape
    grid_y = size_y * lax.axis_size("gy")
    p, q, p_old, q_old, f = (
        entry[0] for entry in (p_adjoint, q_adjoint, p_previous, q_previous, forward_p)
    )
    message = WIDE * size_x + NARROW * 2
    inputs = (p, q, p_old, q_old, f, courant, epsilon, delta_field, tilt_angle, azimuth)
    loc, far, near = call(
        prepare_kernel,
        [(FIELDS * size_x, size_y, size_z)] + [(message, size_y, size_z)] * 2,
        inputs,
        scratch=[pltpu.VMEM(entry.shape, entry.dtype) for entry in inputs]
        + [pltpu.SemaphoreType.DMA((len(inputs),))],
        space=pltpu.HBM,
    )
    far = swap(far, "gx", 1)
    near = swap(near, "gx", 0)
    rows = (size_x + 4) * 24 + size_x * size_y
    (inject,) = call(
        functools.partial(inject_kernel, grid_y, size_z, size_x, size_y),
        [(rows, size_z)],
        (receiver_cells, receiver_values[0], boundary_cells[None], boundary_force[0]),
        flops=800_000_000,
    )
    tiles = WIDE * 3 * size_x // 2 + NARROW * (size_x + 4) // 4
    evens, odds = call(pack_kernel, [(tiles, 8, size_z)] * 2, (loc, far, near))
    evens = swap(evens, "gy", 0)
    odds = swap(odds, "gy", 1)
    count = size_x + 4
    grads, now, ahead, weights = call(
        functools.partial(first_step_kernel, grid_y),
        [
            (3, size_x, size_y, size_z),
            (2, size_x, size_y, size_z),
            (2, 3, count, 8, size_z),
            (6, 3, count, 8, size_z),
        ],
        (source_cells, loc, far, near, evens, odds, inject),
        smem=(0,),
    )
    total = shot_sum(grads)
    p_final, q_final = call(
        second_step_kernel, [(size_x, size_y, size_z)] * 2, (now, ahead, weights, inject, loc)
    )
    scale = jnp.sqrt(total[2] + 1.0)
    return (p_final[None], q_final[None], total[0] / scale, total[1] / scale)


def solution(mesh):
    in_specs = (
        P("shot", "gx", "gy", None),
        P("shot", "gx", "gy", None),
        P("shot", "gx", "gy", None),
        P("shot", "gx", "gy", None),
        P("shot", None, "gx", "gy", None),
        P("gx", "gy", None),
        P("gx", "gy", None),
        P("gx", "gy", None),
        P("gx", "gy", None),
        P("gx", "gy", None),
        P("shot", None),
        P("shot", None, None),
        P(),
        P("shot", None, None),
        P("shot"),
    )
    out_specs = (
        P("shot", "gx", "gy", None),
        P("shot", "gx", "gy", None),
        P("gx", "gy", None),
        P("gx", "gy", None),
    )
    return jax.shard_map(body, mesh=mesh, in_specs=in_specs, out_specs=out_specs, check_vma=False)
```

```python
import functools

import jax
import jax.numpy as jnp
from jax import lax
from jax.experimental import pallas as pl
from jax.experimental.pallas import tpu as pltpu
from jax.sharding import PartitionSpec as P

TAPER = 32
WIDE = 5
NARROW = 7
FIELDS = WIDE + NARROW + 2
INPUTS = ("p", "q", "p_old", "q_old", "f", "c", "eps", "delta", "tilt", "azimuth")
PAIRS = ((0, 0), (1, 1), (2, 2), (0, 1), (0, 2), (1, 2))


def call(kernel, outs, args, scratch=(), smem=(), flops=2_000_000, space=pltpu.VMEM):
    specs = [
        pl.BlockSpec(memory_space=pltpu.SMEM if i in smem else space) for i in range(len(args))
    ]
    shapes = [jax.ShapeDtypeStruct(shape, jnp.float32) for shape in outs]
    return pl.pallas_call(
        kernel,
        out_shape=shapes,
        in_specs=specs,
        out_specs=[pl.BlockSpec(memory_space=pltpu.VMEM)] * len(outs),
        scratch_shapes=list(scratch),
        compiler_params=pltpu.CompilerParams(vmem_limit_bytes=24 * 1024 * 1024),
        cost_estimate=pl.CostEstimate(flops=flops, bytes_accessed=2_000_000, transcendentals=0),
    )(*(pltpu.with_memory_space_constraint(x, space) if space == pltpu.HBM else x for x in args))


def row_mask(shape, below):
    return lax.broadcasted_iota(jnp.int32, shape, len(shape) - 2) < below


def shift_y(tiles, step, keep=3):
    if step > 0:
        rolled = [pltpu.roll(tile, 8 - step, 1) for tile in tiles]
        mask = row_mask(tiles[0].shape, 8 - step)
        return [jnp.where(mask, rolled[i], rolled[(i + 1) % 3]) for i in range(keep)]
    rolled = [pltpu.roll(tile, -step, 1) for tile in tiles]
    mask = row_mask(tiles[0].shape, -step)
    return [jnp.where(mask, rolled[(i + 2) % 3], rolled[i]) for i in range(keep)]


def shift_z(tile, step):
    lane = lax.broadcasted_iota(jnp.int32, tile.shape, 2)
    rolled = pltpu.roll(tile, (-step) % 128, 2)
    inside = lane < 128 - step if step > 0 else lane >= -step
    return jnp.where(inside, rolled, 0.0)


def second(far_low, low, here, high, far_high):
    return (4.0 / 3.0) * (low + high) - (1.0 / 12.0) * (far_low + far_high) - 2.5 * here


def first(far_low, low, high, far_high):
    return (2.0 / 3.0) * (high - low) - (1.0 / 12.0) * (far_high - far_low)


def second_x(tile, count):
    return second(*[tile[i : i + count] for i in range(5)])


def first_x(tile, count):
    return first(*[tile[i : i + count] for i in (0, 1, 3, 4)])


def first_y(tiles, keep):
    low2, low1, high1, high2 = [shift_y(tiles, step, keep) for step in (-2, -1, 1, 2)]
    return [first(low2[i], low1[i], high1[i], high2[i]) for i in range(keep)]


def both(parts_second, parts_first):
    near_even = (4.0 / 3.0) * parts_second
    near_odd = (2.0 / 3.0) * parts_first
    far_even = (-1.0 / 12.0) * parts_second
    far_odd = (1.0 / 12.0) * parts_first
    return (far_even + far_odd, near_even - near_odd, near_even + near_odd, far_even - far_odd)


def adjoint(products, source, count, keep, plus):
    mid = slice(2, 2 + count)
    aa = []
    for axis in range(3):
        scaled = [products[axis][i] * source[i] for i in range(3)]
        aa.append(scaled if plus else [source[i] - scaled[i] for i in range(3)])
    factor = 2.0 if plus else -2.0
    doubled = [factor * tile for tile in source]
    n01 = [products[3][i] * doubled[i] for i in range(3)]
    n02 = [products[4][i] * doubled[i] for i in range(keep)]
    n12 = [products[5][i][mid] * doubled[i][mid] for i in range(3)]
    out = [second_x(aa[0][i], count) for i in range(keep)]
    second_y = [tile[mid] for tile in aa[1]]
    cross_y = [first_x(tile, count) for tile in n01]
    mixed = [both(second_y[i], cross_y[i]) for i in range(3)]
    out = [out[i] - 2.5 * second_y[i] for i in range(keep)]
    for number, step in enumerate((-2, -1, 1, 2)):
        moved = shift_y([mixed[i][number] for i in range(3)], step, keep)
        out = [out[i] + moved[i] for i in range(keep)]
    along_y = first_y(n12, keep)
    for i in range(keep):
        second_z = aa[2][i][mid]
        cross_z = first_x(n02[i], count) + along_y[i]
        terms = both(second_z, cross_z)
        out[i] = out[i] - 2.5 * second_z
        for number, step in enumerate((-2, -1, 1, 2)):
            out[i] = out[i] + shift_z(terms[number], step)
    return out


def forward_image(products, field, count):
    mid = slice(2, 2 + count)
    inner = [tile[mid] for tile in field]
    slope_x = [first_x(tile, count) for tile in field]
    moved = [shift_y(inner, step, 2) for step in (-2, -1, 1, 2)]
    cross = first_y(slope_x, 2)
    out = []
    for i in range(2):
        here = inner[i]
        along = [moved[k][i] for k in range(4)]
        curve_x = second_x(field[i], count)
        curve_y = second(along[0], along[1], here, along[2], along[3])
        slope_y = first(*along)
        depth = [shift_z(here, step) for step in (-2, -1, 1, 2)]
        curve_z = second(depth[0], depth[1], here, depth[2], depth[3])
        total = (1.0 - products[0][i]) * curve_x
        total = total + (1.0 - products[1][i]) * curve_y
        total = total + (1.0 - products[2][i]) * curve_z
        cross_z = []
        for slope in (slope_x[i], slope_y):
            cross_z.append(first(*[shift_z(slope, step) for step in (-2, -1, 1, 2)]))
        mixed = products[3][i] * cross[i] + products[4][i] * cross_z[0] + products[5][i] * cross_z[1]
        out.append(total - 2.0 * mixed)
    return out


def prepare_kernel(*refs):
    count = len(INPUTS)
    arrays, (loc, far, near), held, arrived = refs[:count], refs[count : count + 3], refs[-count - 1 : -1], refs[-1]
    copies = [pltpu.make_async_copy(arrays[i], held[i], arrived.at[i]) for i in range(count)]
    for copy in copies:
        copy.start()
    for copy in copies:
        copy.wait()
    p, q, p_old, q_old, f, c, eps, delta, tilt, azimuth = held
    size_x = p.shape[0]
    p_now, q_now, speed = p[...], q[...], c[...]
    p_weight = speed * (1.0 + 2.0 * eps[...])
    q_weight = speed * (1.0 + 2.0 * delta[...])
    sine = jnp.sin(tilt[...])
    wide = (
        p_weight * p_now + q_weight * q_now,
        speed * (p_now + q_now),
        sine * jnp.cos(azimuth[...]),
        sine * jnp.sin(azimuth[...]),
        jnp.cos(tilt[...]),
    )
    narrow = (
        2.0 * p_now - p_old[...],
        2.0 * q_now - q_old[...],
        p_weight,
        q_weight,
        speed,
        f[0],
        f[1],
    )
    for number, cells in enumerate(wide):
        rows = slice(number * size_x, (number + 1) * size_x)
        loc[rows] = cells
        near[rows] = cells
        far[rows] = cells
    for number, cells in enumerate(narrow + (p_now, q_now)):
        start = (WIDE + number) * size_x
        loc[start : start + size_x] = cells
    odd = lax.rem(lax.axis_index("gx"), 2)
    upper, lower = (1 - odd) * (size_x - 2), odd * (size_x - 2)
    for number in range(NARROW):
        start = (WIDE + number) * size_x
        begin = WIDE * size_x + 2 * number
        near[begin : begin + 2] = loc[pl.ds(start + upper, 2)]
        far[begin : begin + 2] = loc[pl.ds(start + lower, 2)]


def tiles_of(loc, near, far, size_x, part):
    ys = slice(8 * part, 8 * part + 8)
    odd = lax.rem(lax.axis_index("gx"), 2) == 1
    first, second = near[:, ys, :], far[:, ys, :]
    below, above = jnp.where(odd, first, second), jnp.where(odd, second, first)
    wide, narrow = [], []
    for number in range(WIDE):
        rows = slice(number * size_x, (number + 1) * size_x)
        wide += [below[rows], loc[rows, ys, :], above[rows]]
    for number in range(NARROW):
        start = (WIDE + number) * size_x
        begin = WIDE * size_x + 2 * number
        narrow += [
            below[begin : begin + 2],
            loc[start : start + size_x, ys, :],
            above[begin : begin + 2],
        ]
    return jnp.concatenate(wide, axis=0), jnp.concatenate(narrow, axis=0)


def pack_kernel(loc, far, near, odds, evens):
    size_x = loc.shape[0] // FIELDS
    made = []
    for part in range(2):
        wide, narrow = tiles_of(loc, near, far, size_x, part)
        half = wide.shape[0] // 2
        quarter = narrow.shape[0] // 4
        turned = pltpu.roll(wide, 4, 1)
        mask = row_mask((half, 8, 128), 4)
        if part == 0:
            top = jnp.where(mask, wide[:half], turned[half:])
        else:
            top = jnp.where(mask, turned[:half], wide[half:])
        out = None
        for group in range(4):
            rows = narrow[group * quarter : (group + 1) * quarter]
            turn = (2 * group - 6 * part) % 8
            rows = pltpu.roll(rows, turn, 1) if turn else rows
            out = rows if out is None else jnp.where(row_mask(rows.shape, 2 * group), out, rows)
        made.append((top, out))
    odd = lax.rem(lax.axis_index("gy"), 2) == 1
    down, up = made
    for rows, a, b in ((slice(0, half), down[0], up[0]), (slice(half, half + quarter), down[1], up[1])):
        evens[rows] = jnp.where(odd, a, b)
        odds[rows] = jnp.where(odd, b, a)


def unpack(loc, near, far, evens, odds):
    size_x = loc.shape[0] // FIELDS
    odd = lax.rem(lax.axis_index("gy"), 2) == 1
    from_above = jnp.where(odd, odds[...], evens[...])
    from_below = jnp.where(odd, evens[...], odds[...])
    wide_rows, narrow_rows = 3 * size_x, size_x + 4
    half = WIDE * wide_rows // 2
    quarter = NARROW * narrow_rows // 4
    mask = row_mask((half, 8, 128), 4)
    high, low = from_above[0:half], from_below[0:half]
    wide_edge = jnp.concatenate(
        [jnp.where(mask, high, pltpu.roll(low, 4, 1)), jnp.where(mask, pltpu.roll(high, 4, 1), low)],
        axis=0,
    )
    high, low = from_above[half : half + quarter], from_below[half : half + quarter]
    mask = row_mask((quarter, 8, 128), 4)
    edges = []
    for group in range(4):
        first_turn, second_turn = (-2 * group) % 8, (6 - 2 * group) % 8
        upper = pltpu.roll(high, first_turn, 1) if first_turn else high
        lower = pltpu.roll(low, second_turn, 1) if second_turn else low
        edges.append(jnp.where(mask, upper, lower))
    narrow_edge = jnp.concatenate(edges, axis=0)
    wide0, narrow0 = tiles_of(loc, near, far, size_x, 0)
    wide1, narrow1 = tiles_of(loc, near, far, size_x, 1)
    wide = [
        [t[n * wide_rows : (n + 1) * wide_rows] for t in (wide0, wide1, wide_edge)] for n in range(WIDE)
    ]
    narrow = [
        [t[n * narrow_rows : (n + 1) * narrow_rows] for t in (narrow0, narrow1, narrow_edge)]
        for n in range(NARROW)
    ]
    return wide, narrow


def inject_kernel(grid_y, grid_z, size_x, size_y, recv_cells, recv_values, bound_cells, bound_force, out):
    bits_y, bits_z = grid_y.bit_length() - 1, grid_z.bit_length() - 1
    start_x = lax.axis_index("gx") * size_x
    start_y = lax.axis_index("gy") * size_y
    ring = (size_x + 4) * 24
    inner = size_x * size_y
    chunk = 512
    total = jnp.zeros((3 * (ring + inner), grid_z), jnp.float32)
    for cells_ref, values_ref, shift in ((recv_cells, recv_values, 0), (bound_cells, bound_force, bits_z)):
        for begin in range(0, cells_ref.shape[-1], chunk):
            cells = cells_ref[0:1, begin : begin + chunk]
            across = cells >> shift
            depth = cells & (grid_z - 1) if shift else jnp.zeros_like(cells)
            cell_x = (across >> bits_y) - start_x
            cell_y = (across & (grid_y - 1)) - start_y
            near = (cell_x >= -2) & (cell_x < size_x + 2) & (cell_y >= -2) & (cell_y < size_y + 2)
            wrapped = jnp.where(cell_y < 0, cell_y + 24, cell_y)
            ring_row = jnp.where(near, (cell_x + 2) * 24 + wrapped, -1)
            inside = (cell_x >= 0) & (cell_x < size_x) & (cell_y >= 0) & (cell_y < size_y)
            inner_row = jnp.where(inside, cell_x * size_y + cell_y, -1)
            ring_hit = lax.broadcasted_iota(jnp.int32, (ring, chunk), 0) == ring_row
            inner_hit = lax.broadcasted_iota(jnp.int32, (inner, chunk), 0) == inner_row
            columns = lax.broadcasted_iota(jnp.int32, (grid_z, chunk), 0) == depth
            columns = jnp.where(columns, 1.0, 0.0).astype(jnp.bfloat16)
            pieces = []
            parts = []
            for step in range(2):
                value = values_ref[step : step + 1, begin : begin + chunk]
                split = []
                for _ in range(3):
                    top = value.astype(jnp.bfloat16).astype(jnp.float32)
                    split.append(top)
                    value = value - top
                parts.append(split)
            for number in range(3):
                pieces.append(jnp.where(ring_hit, parts[0][number], 0.0).astype(jnp.bfloat16))
                pieces.append(jnp.where(inner_hit, parts[1][number], 0.0).astype(jnp.bfloat16))
            total = total + lax.dot_general(
                jnp.concatenate(pieces, axis=0),
                columns,
                (((1,), (1,)), ((), ())),
                preferred_element_type=jnp.float32,
            )
    rows = ring + inner
    out[...] = total[0:rows] + total[rows : 2 * rows] + total[2 * rows : 3 * rows]


def first_step_kernel(
    grid_y, source, loc, far_x, near_x, odds, evens, inject, grads, now, ahead, weights
):
    size_x, size_y = loc.shape[0] // FIELDS, loc.shape[1]
    wide, narrow = unpack(loc, near_x, far_x, evens, odds)
    p = loc[(FIELDS - 2) * size_x : (FIELDS - 1) * size_x]
    q = loc[(FIELDS - 1) * size_x : FIELDS * size_x]
    source_tiles, mix_tiles = wide[0], wide[1]
    products = [[wide[2 + a][i] * wide[2 + b][i] for i in range(3)] for a, b in PAIRS]
    p_base, q_base, p_weight, q_weight, speed, f0, f1 = narrow
    count = size_x + 4
    mid = slice(2, 2 + size_x)
    p_next = adjoint(products, source_tiles, count, 3, False)
    q_next = adjoint(products, mix_tiles, count, 3, True)
    ring = inject[0 : count * 24].reshape(count, 24, 128)
    p_next = [p_base[i] + p_next[i] + ring[:, 8 * i : 8 * i + 8] for i in range(3)]
    q_next = [q_base[i] + q_next[i] for i in range(3)]
    near = [[tile[2 : 2 + count] for tile in entry] for entry in products]
    inner = [[tile[mid] for tile in entry] for entry in near]
    bits_y = grid_y.bit_length() - 1
    source_x = (source[0] >> bits_y) - lax.axis_index("gx") * size_x
    source_y = (source[0] & (grid_y - 1)) - lax.axis_index("gy") * size_y
    images = [forward_image(inner, field, size_x) for field in (f0, f1)]
    shape = (size_x, 8, 128)
    offset_x = lax.broadcasted_iota(jnp.int32, shape, 0) - source_x
    for i in range(2):
        ys = slice(8 * i, 8 * i + 8)
        offset_y = lax.broadcasted_iota(jnp.int32, shape, 1) + (8 * i - source_y)
        squared = (offset_x * offset_x + offset_y * offset_y).astype(jnp.float32)
        taper = jnp.minimum(squared * (1.0 / float(TAPER * TAPER)), 1.0)
        scale = taper * (2.0 * speed[i][mid])
        image0, image1 = scale * images[0][i], scale * images[1][i]
        p_mid, q_mid = p_next[i][mid], q_next[i][mid]
        grads[0, :, ys, :] = p[:, ys, :] * image0 + p_mid * image1
        grads[1, :, ys, :] = q[:, ys, :] * image0 + q_mid * image1
        g0, g1 = f0[i][mid], f1[i][mid]
        grads[2, :, ys, :] = g0 * g0 + g1 * g1
        now[0, :, ys, :] = p_mid
        now[1, :, ys, :] = q_mid
    for i in range(3):
        ahead[0, i] = p_weight[i] * p_next[i] + q_weight[i] * q_next[i]
        ahead[1, i] = speed[i] * (p_next[i] + q_next[i])
        for number in range(6):
            weights[number, i] = near[number][i]


def second_step_kernel(now, ahead, weights, inject, loc, p_out, q_out):
    size_x, size_y = p_out.shape[0], p_out.shape[1]
    p = loc[(FIELDS - 2) * size_x : (FIELDS - 1) * size_x]
    q = loc[(FIELDS - 1) * size_x : FIELDS * size_x]
    products = [[weights[number, i] for i in range(3)] for number in range(6)]
    p_next = adjoint(products, [ahead[0, i] for i in range(3)], size_x, 2, False)
    q_next = adjoint(products, [ahead[1, i] for i in range(3)], size_x, 2, True)
    inner = inject[inject.shape[0] - size_x * size_y :].reshape(size_x, size_y, 128)
    for i in range(2):
        ys = slice(8 * i, 8 * i + 8)
        p_out[:, ys, :] = 2.0 * now[0, :, ys, :] - p[:, ys, :] + inner[:, ys] + p_next[i]
        q_out[:, ys, :] = 2.0 * now[1, :, ys, :] - q[:, ys, :] + q_next[i]


def swap(part, axis, start):
    lows = range(start, lax.axis_size(axis) - 1, 2)
    return lax.ppermute(part, axis, [(i, i + 1) for i in lows] + [(i + 1, i) for i in lows])


def finish_kernel(own, across, beside, around, grad_e, grad_d):
    total = [(own[i] + beside[i]) + (around[i] + across[i]) for i in range(3)]
    scale = 1.0 / jnp.sqrt(total[2] + 1.0)
    grad_e[...] = total[0] * scale
    grad_d[...] = total[1] * scale


def body(
    p_adjoint,
    q_adjoint,
    p_previous,
    q_previous,
    forward_p,
    courant,
    epsilon,
    delta_field,
    tilt_angle,
    azimuth,
    receiver_cells,
    receiver_values,
    boundary_cells,
    boundary_force,
    source_cells,
):
    _, size_x, size_y, size_z = p_adjoint.shape
    grid_y = size_y * lax.axis_size("gy")
    p, q, p_old, q_old, f = (
        entry[0] for entry in (p_adjoint, q_adjoint, p_previous, q_previous, forward_p)
    )
    message = WIDE * size_x + NARROW * 2
    inputs = (p, q, p_old, q_old, f, courant, epsilon, delta_field, tilt_angle, azimuth)
    loc, far, near = call(
        prepare_kernel,
        [(FIELDS * size_x, size_y, size_z)] + [(message, size_y, size_z)] * 2,
        inputs,
        scratch=[pltpu.VMEM(entry.shape, entry.dtype) for entry in inputs]
        + [pltpu.SemaphoreType.DMA((len(inputs),))],
        space=pltpu.HBM,
    )
    far = swap(far, "gx", 1)
    near = swap(near, "gx", 0)
    rows = (size_x + 4) * 24 + size_x * size_y
    (inject,) = call(
        functools.partial(inject_kernel, grid_y, size_z, size_x, size_y),
        [(rows, size_z)],
        (receiver_cells, receiver_values[0], boundary_cells[None], boundary_force[0]),
        flops=800_000_000,
    )
    tiles = WIDE * 3 * size_x // 2 + NARROW * (size_x + 4) // 4
    odds, evens = call(pack_kernel, [(tiles, 8, size_z)] * 2, (loc, far, near))
    odds = swap(odds, "gy", 1)
    evens = swap(evens, "gy", 0)
    count = size_x + 4
    grads, now, ahead, weights = call(
        functools.partial(first_step_kernel, grid_y),
        [
            (3, size_x, size_y, size_z),
            (2, size_x, size_y, size_z),
            (2, 3, count, 8, size_z),
            (6, 3, count, 8, size_z),
        ],
        (source_cells, loc, far, near, odds, evens, inject),
        smem=(0,),
    )
    shots = range(lax.axis_size("shot"))
    parts = [
        lax.ppermute(grads, "shot", [(i, i ^ turn) for i in shots]) for turn in (2, 1, 3)
    ]
    p_final, q_final = call(
        second_step_kernel, [(size_x, size_y, size_z)] * 2, (now, ahead, weights, inject, loc)
    )
    grad_e, grad_d = call(finish_kernel, [(size_x, size_y, size_z)] * 2, (grads, *parts))
    return (p_final[None], q_final[None], grad_e, grad_d)


def solution(mesh):
    in_specs = (
        P("shot", "gx", "gy", None),
        P("shot", "gx", "gy", None),
        P("shot", "gx", "gy", None),
        P("shot", "gx", "gy", None),
        P("shot", None, "gx", "gy", None),
        P("gx", "gy", None),
        P("gx", "gy", None),
        P("gx", "gy", None),
        P("gx", "gy", None),
        P("gx", "gy", None),
        P("shot", None),
        P("shot", None, None),
        P(),
        P("shot", None, None),
        P("shot"),
    )
    out_specs = (
        P("shot", "gx", "gy", None),
        P("shot", "gx", "gy", None),
        P("gx", "gy", None),
        P("gx", "gy", None),
    )
    return jax.shard_map(body, mesh=mesh, in_specs=in_specs, out_specs=out_specs, check_vma=False)
```

```python
import functools

import jax
import jax.numpy as jnp
from jax import lax
from jax.experimental import pallas as pl
from jax.experimental.pallas import tpu as pltpu
from jax.sharding import PartitionSpec as P

TAPER = 32
WIDE = 5
NARROW = 7
FIELDS = WIDE + NARROW + 2
INPUTS = ("p", "q", "p_old", "q_old", "f", "c", "eps", "delta", "tilt", "azimuth")
PAIRS = ((0, 0), (1, 1), (2, 2), (0, 1), (0, 2), (1, 2))


def call(kernel, outs, args, scratch=(), smem=(), flops=2_000_000, space=pltpu.VMEM):
    specs = [
        pl.BlockSpec(memory_space=pltpu.SMEM if i in smem else space) for i in range(len(args))
    ]
    shapes = [jax.ShapeDtypeStruct(shape, jnp.float32) for shape in outs]
    return pl.pallas_call(
        kernel,
        out_shape=shapes,
        in_specs=specs,
        out_specs=[pl.BlockSpec(memory_space=pltpu.VMEM)] * len(outs),
        scratch_shapes=list(scratch),
        compiler_params=pltpu.CompilerParams(vmem_limit_bytes=24 * 1024 * 1024),
        cost_estimate=pl.CostEstimate(flops=flops, bytes_accessed=2_000_000, transcendentals=0),
    )(*(pltpu.with_memory_space_constraint(x, space) if space == pltpu.HBM else x for x in args))


def row_mask(shape, below):
    return lax.broadcasted_iota(jnp.int32, shape, len(shape) - 2) < below


def shift_y(tiles, step, keep=3):
    if step > 0:
        rolled = [pltpu.roll(tile, 8 - step, 1) for tile in tiles]
        mask = row_mask(tiles[0].shape, 8 - step)
        return [jnp.where(mask, rolled[i], rolled[(i + 1) % 3]) for i in range(keep)]
    rolled = [pltpu.roll(tile, -step, 1) for tile in tiles]
    mask = row_mask(tiles[0].shape, -step)
    return [jnp.where(mask, rolled[(i + 2) % 3], rolled[i]) for i in range(keep)]


def shift_z(tile, step):
    lane = lax.broadcasted_iota(jnp.int32, tile.shape, 2)
    rolled = pltpu.roll(tile, (-step) % 128, 2)
    inside = lane < 128 - step if step > 0 else lane >= -step
    return jnp.where(inside, rolled, 0.0)


def second(far_low, low, here, high, far_high):
    return (4.0 / 3.0) * (low + high) - (1.0 / 12.0) * (far_low + far_high) - 2.5 * here


def first(far_low, low, high, far_high):
    return (2.0 / 3.0) * (high - low) - (1.0 / 12.0) * (far_high - far_low)


def second_x(tile, count):
    return second(*[tile[i : i + count] for i in range(5)])


def first_x(tile, count):
    return first(*[tile[i : i + count] for i in (0, 1, 3, 4)])


def first_y(tiles, keep):
    low2, low1, high1, high2 = [shift_y(tiles, step, keep) for step in (-2, -1, 1, 2)]
    return [first(low2[i], low1[i], high1[i], high2[i]) for i in range(keep)]


def both(parts_second, parts_first):
    near_even = (4.0 / 3.0) * parts_second
    near_odd = (2.0 / 3.0) * parts_first
    far_even = (-1.0 / 12.0) * parts_second
    far_odd = (1.0 / 12.0) * parts_first
    return (far_even + far_odd, near_even - near_odd, near_even + near_odd, far_even - far_odd)


def adjoint(products, source, count, keep, plus):
    mid = slice(2, 2 + count)
    aa = []
    for axis in range(3):
        scaled = [products[axis][i] * source[i] for i in range(3)]
        aa.append(scaled if plus else [source[i] - scaled[i] for i in range(3)])
    factor = 2.0 if plus else -2.0
    doubled = [factor * tile for tile in source]
    n01 = [products[3][i] * doubled[i] for i in range(3)]
    n02 = [products[4][i] * doubled[i] for i in range(keep)]
    n12 = [products[5][i][mid] * doubled[i][mid] for i in range(3)]
    out = [second_x(aa[0][i], count) for i in range(keep)]
    second_y = [tile[mid] for tile in aa[1]]
    cross_y = [first_x(tile, count) for tile in n01]
    mixed = [both(second_y[i], cross_y[i]) for i in range(3)]
    out = [out[i] - 2.5 * second_y[i] for i in range(keep)]
    for number, step in enumerate((-2, -1, 1, 2)):
        moved = shift_y([mixed[i][number] for i in range(3)], step, keep)
        out = [out[i] + moved[i] for i in range(keep)]
    along_y = first_y(n12, keep)
    for i in range(keep):
        second_z = aa[2][i][mid]
        cross_z = first_x(n02[i], count) + along_y[i]
        terms = both(second_z, cross_z)
        out[i] = out[i] - 2.5 * second_z
        for number, step in enumerate((-2, -1, 1, 2)):
            out[i] = out[i] + shift_z(terms[number], step)
    return out


def forward_image(products, field, count):
    mid = slice(2, 2 + count)
    inner = [tile[mid] for tile in field]
    slope_x = [first_x(tile, count) for tile in field]
    moved = [shift_y(inner, step, 2) for step in (-2, -1, 1, 2)]
    cross = first_y(slope_x, 2)
    out = []
    for i in range(2):
        here = inner[i]
        along = [moved[k][i] for k in range(4)]
        curve_x = second_x(field[i], count)
        curve_y = second(along[0], along[1], here, along[2], along[3])
        slope_y = first(*along)
        depth = [shift_z(here, step) for step in (-2, -1, 1, 2)]
        curve_z = second(depth[0], depth[1], here, depth[2], depth[3])
        total = (1.0 - products[0][i]) * curve_x
        total = total + (1.0 - products[1][i]) * curve_y
        total = total + (1.0 - products[2][i]) * curve_z
        cross_z = []
        for slope in (slope_x[i], slope_y):
            cross_z.append(first(*[shift_z(slope, step) for step in (-2, -1, 1, 2)]))
        mixed = products[3][i] * cross[i] + products[4][i] * cross_z[0] + products[5][i] * cross_z[1]
        out.append(total - 2.0 * mixed)
    return out


def prepare_kernel(*refs):
    count = len(INPUTS)
    arrays, (loc, far, near), held, arrived = refs[:count], refs[count : count + 3], refs[-count - 1 : -1], refs[-1]
    copies = [pltpu.make_async_copy(arrays[i], held[i], arrived.at[i]) for i in range(count)]
    for copy in copies:
        copy.start()
    for copy in copies:
        copy.wait()
    p, q, p_old, q_old, f, c, eps, delta, tilt, azimuth = held
    size_x = p.shape[0]
    p_now, q_now, speed = p[...], q[...], c[...]
    p_weight = speed * (1.0 + 2.0 * eps[...])
    q_weight = speed * (1.0 + 2.0 * delta[...])
    sine = jnp.sin(tilt[...])
    wide = (
        p_weight * p_now + q_weight * q_now,
        speed * (p_now + q_now),
        sine * jnp.cos(azimuth[...]),
        sine * jnp.sin(azimuth[...]),
        jnp.cos(tilt[...]),
    )
    narrow = (
        2.0 * p_now - p_old[...],
        2.0 * q_now - q_old[...],
        p_weight,
        q_weight,
        speed,
        f[0],
        f[1],
    )
    for number, cells in enumerate(wide):
        rows = slice(number * size_x, (number + 1) * size_x)
        loc[rows] = cells
        near[rows] = cells
        far[rows] = cells
    for number, cells in enumerate(narrow + (p_now, q_now)):
        start = (WIDE + number) * size_x
        loc[start : start + size_x] = cells
    odd = lax.rem(lax.axis_index("gx"), 2)
    upper, lower = (1 - odd) * (size_x - 2), odd * (size_x - 2)
    for number in range(NARROW):
        start = (WIDE + number) * size_x
        begin = WIDE * size_x + 2 * number
        near[begin : begin + 2] = loc[pl.ds(start + upper, 2)]
        far[begin : begin + 2] = loc[pl.ds(start + lower, 2)]


def tiles_of(loc, near, far, size_x, part):
    ys = slice(8 * part, 8 * part + 8)
    odd = lax.rem(lax.axis_index("gx"), 2) == 1
    first, second = near[:, ys, :], far[:, ys, :]
    below, above = jnp.where(odd, first, second), jnp.where(odd, second, first)
    wide, narrow = [], []
    for number in range(WIDE):
        rows = slice(number * size_x, (number + 1) * size_x)
        wide += [below[rows], loc[rows, ys, :], above[rows]]
    for number in range(NARROW):
        start = (WIDE + number) * size_x
        begin = WIDE * size_x + 2 * number
        narrow += [
            below[begin : begin + 2],
            loc[start : start + size_x, ys, :],
            above[begin : begin + 2],
        ]
    return jnp.concatenate(wide, axis=0), jnp.concatenate(narrow, axis=0)


def pack_kernel(loc, far, near, odds, evens):
    size_x = loc.shape[0] // FIELDS
    made = []
    for part in range(2):
        wide, narrow = tiles_of(loc, near, far, size_x, part)
        half = wide.shape[0] // 2
        quarter = narrow.shape[0] // 4
        turned = pltpu.roll(wide, 4, 1)
        mask = row_mask((half, 8, 128), 4)
        if part == 0:
            top = jnp.where(mask, wide[:half], turned[half:])
        else:
            top = jnp.where(mask, turned[:half], wide[half:])
        out = None
        for group in range(4):
            rows = narrow[group * quarter : (group + 1) * quarter]
            turn = (2 * group - 6 * part) % 8
            rows = pltpu.roll(rows, turn, 1) if turn else rows
            out = rows if out is None else jnp.where(row_mask(rows.shape, 2 * group), out, rows)
        made.append((top, out))
    odd = lax.rem(lax.axis_index("gy"), 2) == 1
    down, up = made
    for rows, a, b in ((slice(0, half), down[0], up[0]), (slice(half, half + quarter), down[1], up[1])):
        evens[rows] = jnp.where(odd, a, b)
        odds[rows] = jnp.where(odd, b, a)


def unpack(loc, near, far, evens, odds):
    size_x = loc.shape[0] // FIELDS
    odd = lax.rem(lax.axis_index("gy"), 2) == 1
    from_above = jnp.where(odd, odds[...], evens[...])
    from_below = jnp.where(odd, evens[...], odds[...])
    wide_rows, narrow_rows = 3 * size_x, size_x + 4
    half = WIDE * wide_rows // 2
    quarter = NARROW * narrow_rows // 4
    mask = row_mask((half, 8, 128), 4)
    high, low = from_above[0:half], from_below[0:half]
    wide_edge = jnp.concatenate(
        [jnp.where(mask, high, pltpu.roll(low, 4, 1)), jnp.where(mask, pltpu.roll(high, 4, 1), low)],
        axis=0,
    )
    high, low = from_above[half : half + quarter], from_below[half : half + quarter]
    mask = row_mask((quarter, 8, 128), 4)
    edges = []
    for group in range(4):
        first_turn, second_turn = (-2 * group) % 8, (6 - 2 * group) % 8
        upper = pltpu.roll(high, first_turn, 1) if first_turn else high
        lower = pltpu.roll(low, second_turn, 1) if second_turn else low
        edges.append(jnp.where(mask, upper, lower))
    narrow_edge = jnp.concatenate(edges, axis=0)
    wide0, narrow0 = tiles_of(loc, near, far, size_x, 0)
    wide1, narrow1 = tiles_of(loc, near, far, size_x, 1)
    wide = [
        [t[n * wide_rows : (n + 1) * wide_rows] for t in (wide0, wide1, wide_edge)] for n in range(WIDE)
    ]
    narrow = [
        [t[n * narrow_rows : (n + 1) * narrow_rows] for t in (narrow0, narrow1, narrow_edge)]
        for n in range(NARROW)
    ]
    return wide, narrow


def inject_kernel(grid_y, grid_z, size_x, size_y, recv_cells, recv_values, bound_cells, bound_force, out):
    bits_y, bits_z = grid_y.bit_length() - 1, grid_z.bit_length() - 1
    start_x = lax.axis_index("gx") * size_x
    start_y = lax.axis_index("gy") * size_y
    ring = (size_x + 4) * 24
    inner = size_x * size_y
    chunk = 512
    total = jnp.zeros((3 * (ring + inner), grid_z), jnp.float32)
    for cells_ref, values_ref, shift in ((recv_cells, recv_values, 0), (bound_cells, bound_force, bits_z)):
        for begin in range(0, cells_ref.shape[-1], chunk):
            cells = cells_ref[0:1, begin : begin + chunk]
            across = cells >> shift
            depth = cells & (grid_z - 1) if shift else jnp.zeros_like(cells)
            cell_x = (across >> bits_y) - start_x
            cell_y = (across & (grid_y - 1)) - start_y
            near = (cell_x >= -2) & (cell_x < size_x + 2) & (cell_y >= -2) & (cell_y < size_y + 2)
            wrapped = jnp.where(cell_y < 0, cell_y + 24, cell_y)
            ring_row = jnp.where(near, (cell_x + 2) * 24 + wrapped, -1)
            inside = (cell_x >= 0) & (cell_x < size_x) & (cell_y >= 0) & (cell_y < size_y)
            inner_row = jnp.where(inside, cell_x * size_y + cell_y, -1)
            ring_hit = lax.broadcasted_iota(jnp.int32, (ring, chunk), 0) == ring_row
            inner_hit = lax.broadcasted_iota(jnp.int32, (inner, chunk), 0) == inner_row
            columns = lax.broadcasted_iota(jnp.int32, (grid_z, chunk), 0) == depth
            columns = jnp.where(columns, 1.0, 0.0).astype(jnp.bfloat16)
            pieces = []
            parts = []
            for step in range(2):
                value = values_ref[step : step + 1, begin : begin + chunk]
                split = []
                for _ in range(3):
                    top = value.astype(jnp.bfloat16).astype(jnp.float32)
                    split.append(top)
                    value = value - top
                parts.append(split)
            for number in range(3):
                pieces.append(jnp.where(ring_hit, parts[0][number], 0.0).astype(jnp.bfloat16))
                pieces.append(jnp.where(inner_hit, parts[1][number], 0.0).astype(jnp.bfloat16))
            total = total + lax.dot_general(
                jnp.concatenate(pieces, axis=0),
                columns,
                (((1,), (1,)), ((), ())),
                preferred_element_type=jnp.float32,
            )
    rows = ring + inner
    out[...] = total[0:rows] + total[rows : 2 * rows] + total[2 * rows : 3 * rows]


def first_step_kernel(
    grid_y, source, loc, far_x, near_x, odds, evens, inject, grads, now, ahead, weights
):
    size_x, size_y = loc.shape[0] // FIELDS, loc.shape[1]
    wide, narrow = unpack(loc, near_x, far_x, evens, odds)
    p = loc[(FIELDS - 2) * size_x : (FIELDS - 1) * size_x]
    q = loc[(FIELDS - 1) * size_x : FIELDS * size_x]
    source_tiles, mix_tiles = wide[0], wide[1]
    products = [[wide[2 + a][i] * wide[2 + b][i] for i in range(3)] for a, b in PAIRS]
    p_base, q_base, p_weight, q_weight, speed, f0, f1 = narrow
    count = size_x + 4
    mid = slice(2, 2 + size_x)
    p_next = adjoint(products, source_tiles, count, 3, False)
    q_next = adjoint(products, mix_tiles, count, 3, True)
    ring = inject[0 : count * 24].reshape(count, 24, 128)
    p_next = [p_base[i] + p_next[i] + ring[:, 8 * i : 8 * i + 8] for i in range(3)]
    q_next = [q_base[i] + q_next[i] for i in range(3)]
    near = [[tile[2 : 2 + count] for tile in entry] for entry in products]
    inner = [[tile[mid] for tile in entry] for entry in near]
    bits_y = grid_y.bit_length() - 1
    source_x = (source[0] >> bits_y) - lax.axis_index("gx") * size_x
    source_y = (source[0] & (grid_y - 1)) - lax.axis_index("gy") * size_y
    images = [forward_image(inner, field, size_x) for field in (f0, f1)]
    shape = (size_x, 8, 128)
    offset_x = lax.broadcasted_iota(jnp.int32, shape, 0) - source_x
    for i in range(2):
        ys = slice(8 * i, 8 * i + 8)
        offset_y = lax.broadcasted_iota(jnp.int32, shape, 1) + (8 * i - source_y)
        squared = (offset_x * offset_x + offset_y * offset_y).astype(jnp.float32)
        taper = jnp.minimum(squared * (1.0 / float(TAPER * TAPER)), 1.0)
        scale = taper * (2.0 * speed[i][mid])
        image0, image1 = scale * images[0][i], scale * images[1][i]
        p_mid, q_mid = p_next[i][mid], q_next[i][mid]
        g0, g1 = f0[i][mid], f1[i][mid]
        sums = (
            p[:, ys, :] * image0 + p_mid * image1,
            q[:, ys, :] * image0 + q_mid * image1,
            g0 * g0 + g1 * g1,
        )
        for shot in range(grads.shape[0]):
            for number in range(3):
                grads[shot, number, :, ys, :] = sums[number]
        now[0, :, ys, :] = p_mid
        now[1, :, ys, :] = q_mid
    for i in range(3):
        ahead[0, i] = p_weight[i] * p_next[i] + q_weight[i] * q_next[i]
        ahead[1, i] = speed[i] * (p_next[i] + q_next[i])
        for number in range(6):
            weights[number, i] = near[number][i]


def second_step_kernel(now, ahead, weights, inject, loc, p_out, q_out):
    size_x, size_y = p_out.shape[0], p_out.shape[1]
    p = loc[(FIELDS - 2) * size_x : (FIELDS - 1) * size_x]
    q = loc[(FIELDS - 1) * size_x : FIELDS * size_x]
    products = [[weights[number, i] for i in range(3)] for number in range(6)]
    p_next = adjoint(products, [ahead[0, i] for i in range(3)], size_x, 2, False)
    q_next = adjoint(products, [ahead[1, i] for i in range(3)], size_x, 2, True)
    inner = inject[inject.shape[0] - size_x * size_y :].reshape(size_x, size_y, 128)
    for i in range(2):
        ys = slice(8 * i, 8 * i + 8)
        p_out[:, ys, :] = 2.0 * now[0, :, ys, :] - p[:, ys, :] + inner[:, ys] + p_next[i]
        q_out[:, ys, :] = 2.0 * now[1, :, ys, :] - q[:, ys, :] + q_next[i]


def swap(part, axis, start):
    lows = range(start, lax.axis_size(axis) - 1, 2)
    return lax.ppermute(part, axis, [(i, i + 1) for i in lows] + [(i + 1, i) for i in lows])


def finish_kernel(parts, grad_e, grad_d):
    total = [sum(parts[shot, i] for shot in range(parts.shape[0])) for i in range(3)]
    scale = 1.0 / jnp.sqrt(total[2] + 1.0)
    grad_e[...] = total[0] * scale
    grad_d[...] = total[1] * scale


def body(
    p_adjoint,
    q_adjoint,
    p_previous,
    q_previous,
    forward_p,
    courant,
    epsilon,
    delta_field,
    tilt_angle,
    azimuth,
    receiver_cells,
    receiver_values,
    boundary_cells,
    boundary_force,
    source_cells,
):
    _, size_x, size_y, size_z = p_adjoint.shape
    grid_y = size_y * lax.axis_size("gy")
    p, q, p_old, q_old, f = (
        entry[0] for entry in (p_adjoint, q_adjoint, p_previous, q_previous, forward_p)
    )
    message = WIDE * size_x + NARROW * 2
    inputs = (p, q, p_old, q_old, f, courant, epsilon, delta_field, tilt_angle, azimuth)
    loc, far, near = call(
        prepare_kernel,
        [(FIELDS * size_x, size_y, size_z)] + [(message, size_y, size_z)] * 2,
        inputs,
        scratch=[pltpu.VMEM(entry.shape, entry.dtype) for entry in inputs]
        + [pltpu.SemaphoreType.DMA((len(inputs),))],
        space=pltpu.HBM,
    )
    far = swap(far, "gx", 1)
    near = swap(near, "gx", 0)
    rows = (size_x + 4) * 24 + size_x * size_y
    (inject,) = call(
        functools.partial(inject_kernel, grid_y, size_z, size_x, size_y),
        [(rows, size_z)],
        (receiver_cells, receiver_values[0], boundary_cells[None], boundary_force[0]),
        flops=800_000_000,
    )
    tiles = WIDE * 3 * size_x // 2 + NARROW * (size_x + 4) // 4
    odds, evens = call(pack_kernel, [(tiles, 8, size_z)] * 2, (loc, far, near))
    odds = swap(odds, "gy", 1)
    evens = swap(evens, "gy", 0)
    count = size_x + 4
    grads, now, ahead, weights = call(
        functools.partial(first_step_kernel, grid_y),
        [
            (lax.axis_size("shot"), 3, size_x, size_y, size_z),
            (2, size_x, size_y, size_z),
            (2, 3, count, 8, size_z),
            (6, 3, count, 8, size_z),
        ],
        (source_cells, loc, far, near, odds, evens, inject),
        smem=(0,),
    )
    parts = lax.all_to_all(grads, "shot", 0, 0)
    p_final, q_final = call(
        second_step_kernel, [(size_x, size_y, size_z)] * 2, (now, ahead, weights, inject, loc)
    )
    grad_e, grad_d = call(finish_kernel, [(size_x, size_y, size_z)] * 2, (parts,))
    return (p_final[None], q_final[None], grad_e, grad_d)


def solution(mesh):
    in_specs = (
        P("shot", "gx", "gy", None),
        P("shot", "gx", "gy", None),
        P("shot", "gx", "gy", None),
        P("shot", "gx", "gy", None),
        P("shot", None, "gx", "gy", None),
        P("gx", "gy", None),
        P("gx", "gy", None),
        P("gx", "gy", None),
        P("gx", "gy", None),
        P("gx", "gy", None),
        P("shot", None),
        P("shot", None, None),
        P(),
        P("shot", None, None),
        P("shot"),
    )
    out_specs = (
        P("shot", "gx", "gy", None),
        P("shot", "gx", "gy", None),
        P("gx", "gy", None),
        P("gx", "gy", None),
    )
    return jax.shard_map(body, mesh=mesh, in_specs=in_specs, out_specs=out_specs, check_vma=False)
```

```python
import functools

import jax
import jax.numpy as jnp
from jax import lax
from jax.experimental import pallas as pl
from jax.experimental.pallas import tpu as pltpu
from jax.sharding import PartitionSpec as P

TAPER = 32
WIDE = 5
NARROW = 7
FIELDS = WIDE + NARROW + 2
INPUTS = ("p", "q", "p_old", "q_old", "f", "c", "eps", "delta", "tilt", "azimuth")
PAIRS = ((0, 0), (1, 1), (2, 2), (0, 1), (0, 2), (1, 2))


def call(kernel, outs, args, scratch=(), smem=(), flops=2_000_000, space=pltpu.VMEM):
    specs = [
        pl.BlockSpec(memory_space=pltpu.SMEM if i in smem else space) for i in range(len(args))
    ]
    shapes = [jax.ShapeDtypeStruct(shape, jnp.float32) for shape in outs]
    return pl.pallas_call(
        kernel,
        out_shape=shapes,
        in_specs=specs,
        out_specs=[pl.BlockSpec(memory_space=pltpu.VMEM)] * len(outs),
        scratch_shapes=list(scratch),
        compiler_params=pltpu.CompilerParams(vmem_limit_bytes=24 * 1024 * 1024),
        cost_estimate=pl.CostEstimate(flops=flops, bytes_accessed=2_000_000, transcendentals=0),
    )(*(pltpu.with_memory_space_constraint(x, space) if space == pltpu.HBM else x for x in args))


def row_mask(shape, below):
    return lax.broadcasted_iota(jnp.int32, shape, len(shape) - 2) < below


def shift_y(tiles, step, keep=3):
    if step > 0:
        rolled = [pltpu.roll(tile, 8 - step, 1) for tile in tiles]
        mask = row_mask(tiles[0].shape, 8 - step)
        return [jnp.where(mask, rolled[i], rolled[(i + 1) % 3]) for i in range(keep)]
    rolled = [pltpu.roll(tile, -step, 1) for tile in tiles]
    mask = row_mask(tiles[0].shape, -step)
    return [jnp.where(mask, rolled[(i + 2) % 3], rolled[i]) for i in range(keep)]


def shift_z(tile, step):
    lane = lax.broadcasted_iota(jnp.int32, tile.shape, 2)
    rolled = pltpu.roll(tile, (-step) % 128, 2)
    inside = lane < 128 - step if step > 0 else lane >= -step
    return jnp.where(inside, rolled, 0.0)


def second(far_low, low, here, high, far_high):
    return (4.0 / 3.0) * (low + high) - (1.0 / 12.0) * (far_low + far_high) - 2.5 * here


def first(far_low, low, high, far_high):
    return (2.0 / 3.0) * (high - low) - (1.0 / 12.0) * (far_high - far_low)


def second_x(tile, count):
    return second(*[tile[i : i + count] for i in range(5)])


def first_x(tile, count):
    return first(*[tile[i : i + count] for i in (0, 1, 3, 4)])


def first_y(tiles, keep):
    low2, low1, high1, high2 = [shift_y(tiles, step, keep) for step in (-2, -1, 1, 2)]
    return [first(low2[i], low1[i], high1[i], high2[i]) for i in range(keep)]


def both(parts_second, parts_first):
    near_even = (4.0 / 3.0) * parts_second
    near_odd = (2.0 / 3.0) * parts_first
    far_even = (-1.0 / 12.0) * parts_second
    far_odd = (1.0 / 12.0) * parts_first
    return (far_even + far_odd, near_even - near_odd, near_even + near_odd, far_even - far_odd)


def adjoint(products, source, count, keep, plus):
    mid = slice(2, 2 + count)
    aa = []
    for axis in range(3):
        scaled = [products[axis][i] * source[i] for i in range(3)]
        aa.append(scaled if plus else [source[i] - scaled[i] for i in range(3)])
    factor = 2.0 if plus else -2.0
    doubled = [factor * tile for tile in source]
    n01 = [products[3][i] * doubled[i] for i in range(3)]
    n02 = [products[4][i] * doubled[i] for i in range(keep)]
    n12 = [products[5][i][mid] * doubled[i][mid] for i in range(3)]
    out = [second_x(aa[0][i], count) for i in range(keep)]
    second_y = [tile[mid] for tile in aa[1]]
    cross_y = [first_x(tile, count) for tile in n01]
    mixed = [both(second_y[i], cross_y[i]) for i in range(3)]
    out = [out[i] - 2.5 * second_y[i] for i in range(keep)]
    for number, step in enumerate((-2, -1, 1, 2)):
        moved = shift_y([mixed[i][number] for i in range(3)], step, keep)
        out = [out[i] + moved[i] for i in range(keep)]
    along_y = first_y(n12, keep)
    for i in range(keep):
        second_z = aa[2][i][mid]
        cross_z = first_x(n02[i], count) + along_y[i]
        terms = both(second_z, cross_z)
        out[i] = out[i] - 2.5 * second_z
        for number, step in enumerate((-2, -1, 1, 2)):
            out[i] = out[i] + shift_z(terms[number], step)
    return out


def forward_image(products, field, count):
    mid = slice(2, 2 + count)
    inner = [tile[mid] for tile in field]
    slope_x = [first_x(tile, count) for tile in field]
    moved = [shift_y(inner, step, 2) for step in (-2, -1, 1, 2)]
    cross = first_y(slope_x, 2)
    out = []
    for i in range(2):
        here = inner[i]
        along = [moved[k][i] for k in range(4)]
        curve_x = second_x(field[i], count)
        curve_y = second(along[0], along[1], here, along[2], along[3])
        slope_y = first(*along)
        depth = [shift_z(here, step) for step in (-2, -1, 1, 2)]
        curve_z = second(depth[0], depth[1], here, depth[2], depth[3])
        total = (1.0 - products[0][i]) * curve_x
        total = total + (1.0 - products[1][i]) * curve_y
        total = total + (1.0 - products[2][i]) * curve_z
        cross_z = []
        for slope in (slope_x[i], slope_y):
            cross_z.append(first(*[shift_z(slope, step) for step in (-2, -1, 1, 2)]))
        mixed = products[3][i] * cross[i] + products[4][i] * cross_z[0] + products[5][i] * cross_z[1]
        out.append(total - 2.0 * mixed)
    return out


def prepare_kernel(*refs):
    count = len(INPUTS)
    arrays, (loc, far, near), held, arrived = refs[:count], refs[count : count + 3], refs[-count - 1 : -1], refs[-1]
    copies = [pltpu.make_async_copy(arrays[i], held[i], arrived.at[i]) for i in range(count)]
    for copy in copies:
        copy.start()
    for copy in copies:
        copy.wait()
    p, q, p_old, q_old, f, c, eps, delta, tilt, azimuth = held
    size_x = p.shape[0]
    p_now, q_now, speed = p[...], q[...], c[...]
    p_weight = speed * (1.0 + 2.0 * eps[...])
    q_weight = speed * (1.0 + 2.0 * delta[...])
    sine = jnp.sin(tilt[...])
    wide = (
        p_weight * p_now + q_weight * q_now,
        speed * (p_now + q_now),
        sine * jnp.cos(azimuth[...]),
        sine * jnp.sin(azimuth[...]),
        jnp.cos(tilt[...]),
    )
    narrow = (
        2.0 * p_now - p_old[...],
        2.0 * q_now - q_old[...],
        p_weight,
        q_weight,
        speed,
        f[0],
        f[1],
    )
    for number, cells in enumerate(wide):
        rows = slice(number * size_x, (number + 1) * size_x)
        loc[rows] = cells
        near[rows] = cells
        far[rows] = cells
    for number, cells in enumerate(narrow + (p_now, q_now)):
        start = (WIDE + number) * size_x
        loc[start : start + size_x] = cells
    odd = lax.rem(lax.axis_index("gx"), 2)
    upper, lower = (1 - odd) * (size_x - 2), odd * (size_x - 2)
    for number in range(NARROW):
        start = (WIDE + number) * size_x
        begin = WIDE * size_x + 2 * number
        near[begin : begin + 2] = loc[pl.ds(start + upper, 2)]
        far[begin : begin + 2] = loc[pl.ds(start + lower, 2)]


def tiles_of(loc, near, far, size_x, part):
    ys = slice(8 * part, 8 * part + 8)
    odd = lax.rem(lax.axis_index("gx"), 2) == 1
    first, second = near[:, ys, :], far[:, ys, :]
    below, above = jnp.where(odd, first, second), jnp.where(odd, second, first)
    wide, narrow = [], []
    for number in range(WIDE):
        rows = slice(number * size_x, (number + 1) * size_x)
        wide.append(jnp.concatenate([below[rows], loc[rows, ys, :], above[rows]], axis=0))
    for number in range(NARROW):
        start = (WIDE + number) * size_x
        begin = WIDE * size_x + 2 * number
        rows = slice(begin, begin + 2)
        here = loc[start : start + size_x, ys, :]
        narrow.append(jnp.concatenate([below[rows], here, above[rows]], axis=0))
    return wide, narrow


def turn(rows, by):
    by = by % 8
    return pltpu.roll(rows, by, 1) if by else rows


def pack(rows, part, groups):
    height, count = 8 // groups, rows.shape[0] // groups
    out = None
    for group in range(groups):
        piece = turn(rows[group * count : (group + 1) * count], height * (group - part * (groups - 1)))
        mask = row_mask(piece.shape, height * group)
        out = piece if out is None else jnp.where(mask, out, piece)
    return out


def unpack(high, low, groups):
    height = 8 // groups
    edges = []
    for group in range(groups):
        upper = turn(high, -height * group)
        lower = turn(low, height * (groups - 1 - group))
        edges.append(jnp.where(row_mask(high.shape, 4), upper, lower))
    return jnp.concatenate(edges, axis=0)


def early_rows(wide, narrow):
    return [tile[2 : tile.shape[0] - 2] for tile in wide] + narrow[5:]


def send_both(parts, evens, odds, start):
    odd = lax.rem(lax.axis_index("gy"), 2) == 1
    rows = slice(start, start + parts[0].shape[0])
    evens[rows] = jnp.where(odd, parts[0], parts[1])
    odds[rows] = jnp.where(odd, parts[1], parts[0])


def from_both(evens, odds):
    odd = lax.rem(lax.axis_index("gy"), 2) == 1
    return jnp.where(odd, odds[...], evens[...]), jnp.where(odd, evens[...], odds[...])


def early_kernel(loc, far, near, odds, evens):
    size_x = loc.shape[0] // FIELDS
    parts = []
    for part in range(2):
        wide, narrow = tiles_of(loc, near, far, size_x, part)
        parts.append(pack(jnp.concatenate(early_rows(wide, narrow), axis=0), part, 4))
    send_both(parts, evens, odds, 0)


def late_kernel(loc, far, near, odds, evens):
    size_x = loc.shape[0] // FIELDS
    wides, narrows = [], []
    for part in range(2):
        wide, narrow = tiles_of(loc, near, far, size_x, part)
        wides.append(pack(jnp.concatenate(wide, axis=0), part, 2))
        narrows.append(pack(jnp.concatenate(narrow[:5], axis=0), part, 4))
    send_both(wides, evens, odds, 0)
    send_both(narrows, evens, odds, wides[0].shape[0])


def cut(rows, count):
    return [rows[i : i + count] for i in range(0, rows.shape[0], count)]


def inject_kernel(grid_y, grid_z, size_x, size_y, recv_cells, recv_values, bound_cells, bound_force, out):
    bits_y, bits_z = grid_y.bit_length() - 1, grid_z.bit_length() - 1
    start_x = lax.axis_index("gx") * size_x
    start_y = lax.axis_index("gy") * size_y
    ring = (size_x + 4) * 24
    inner = size_x * size_y
    chunk = 512
    total = jnp.zeros((3 * (ring + inner), grid_z), jnp.float32)
    for cells_ref, values_ref, shift in ((recv_cells, recv_values, 0), (bound_cells, bound_force, bits_z)):
        for begin in range(0, cells_ref.shape[-1], chunk):
            cells = cells_ref[0:1, begin : begin + chunk]
            across = cells >> shift
            depth = cells & (grid_z - 1) if shift else jnp.zeros_like(cells)
            cell_x = (across >> bits_y) - start_x
            cell_y = (across & (grid_y - 1)) - start_y
            near = (cell_x >= -2) & (cell_x < size_x + 2) & (cell_y >= -2) & (cell_y < size_y + 2)
            wrapped = jnp.where(cell_y < 0, cell_y + 24, cell_y)
            ring_row = jnp.where(near, (cell_x + 2) * 24 + wrapped, -1)
            inside = (cell_x >= 0) & (cell_x < size_x) & (cell_y >= 0) & (cell_y < size_y)
            inner_row = jnp.where(inside, cell_x * size_y + cell_y, -1)
            ring_hit = lax.broadcasted_iota(jnp.int32, (ring, chunk), 0) == ring_row
            inner_hit = lax.broadcasted_iota(jnp.int32, (inner, chunk), 0) == inner_row
            columns = lax.broadcasted_iota(jnp.int32, (grid_z, chunk), 0) == depth
            columns = jnp.where(columns, 1.0, 0.0).astype(jnp.bfloat16)
            pieces = []
            parts = []
            for step in range(2):
                value = values_ref[step : step + 1, begin : begin + chunk]
                split = []
                for _ in range(3):
                    top = value.astype(jnp.bfloat16).astype(jnp.float32)
                    split.append(top)
                    value = value - top
                parts.append(split)
            for number in range(3):
                pieces.append(jnp.where(ring_hit, parts[0][number], 0.0).astype(jnp.bfloat16))
                pieces.append(jnp.where(inner_hit, parts[1][number], 0.0).astype(jnp.bfloat16))
            total = total + lax.dot_general(
                jnp.concatenate(pieces, axis=0),
                columns,
                (((1,), (1,)), ((), ())),
                preferred_element_type=jnp.float32,
            )
    rows = ring + inner
    out[...] = total[0:rows] + total[rows : 2 * rows] + total[2 * rows : 3 * rows]


def first_step_kernel(grid_y, source, loc, far_x, near_x, odds, evens, inject, grads):
    size_x, size_y = loc.shape[0] // FIELDS, loc.shape[1]
    count = size_x + 4
    high, low = from_both(evens, odds)
    edge = cut(unpack(high, low, 4), count)
    middle = [early_rows(*tiles_of(loc, near_x, far_x, size_x, part)) for part in range(2)]
    fields = [[middle[0][n], middle[1][n], edge[n]] for n in range(len(edge))]
    products = [[fields[2 + a][i] * fields[2 + b][i] for i in range(3)] for a, b in PAIRS]
    mid = slice(2, 2 + size_x)
    p_next = adjoint(products, fields[0], size_x, 2, False)
    q_next = adjoint(products, fields[1], size_x, 2, True)
    inner = [[tile[mid] for tile in entry] for entry in products]
    images = [forward_image(inner, field, size_x) for field in fields[5:7]]
    ring = inject[0 : count * 24].reshape(count, 24, 128)
    bits_y = grid_y.bit_length() - 1
    source_x = (source[0] >> bits_y) - lax.axis_index("gx") * size_x
    source_y = (source[0] & (grid_y - 1)) - lax.axis_index("gy") * size_y
    shape = (size_x, 8, 128)
    offset_x = lax.broadcasted_iota(jnp.int32, shape, 0) - source_x

    def block(field, ys):
        return loc[field * size_x : (field + 1) * size_x, ys, :]

    for i in range(2):
        ys = slice(8 * i, 8 * i + 8)
        offset_y = lax.broadcasted_iota(jnp.int32, shape, 1) + (8 * i - source_y)
        squared = (offset_x * offset_x + offset_y * offset_y).astype(jnp.float32)
        taper = jnp.minimum(squared * (1.0 / float(TAPER * TAPER)), 1.0)
        scale = taper * (2.0 * block(WIDE + 4, ys))
        image0, image1 = scale * images[0][i], scale * images[1][i]
        p_mid = block(WIDE, ys) + p_next[i] + ring[mid, ys, :]
        q_mid = block(WIDE + 1, ys) + q_next[i]
        grads[0, :, ys, :] = block(FIELDS - 2, ys) * image0 + p_mid * image1
        grads[1, :, ys, :] = block(FIELDS - 1, ys) * image0 + q_mid * image1
        f0, f1 = block(WIDE + 5, ys), block(WIDE + 6, ys)
        grads[2, :, ys, :] = f0 * f0 + f1 * f1


def second_step_kernel(loc, far_x, near_x, odds, evens, inject, p_out, q_out):
    size_x, size_y = p_out.shape[0], p_out.shape[1]
    count = size_x + 4
    high, low = from_both(evens, odds)
    half = WIDE * (size_x + 8) // 2
    wide_edge = cut(unpack(high[:half], low[:half], 2), size_x + 8)
    narrow_edge = cut(unpack(high[half:], low[half:], 4), count)
    parts = [tiles_of(loc, near_x, far_x, size_x, part) for part in range(2)]
    wide = [[parts[0][0][n], parts[1][0][n], wide_edge[n]] for n in range(WIDE)]
    narrow = [[parts[0][1][n], parts[1][1][n], narrow_edge[n]] for n in range(5)]
    products = [[wide[2 + a][i] * wide[2 + b][i] for i in range(3)] for a, b in PAIRS]
    p_base, q_base, p_weight, q_weight, speed = narrow
    mid = slice(2, 2 + size_x)
    p_next = adjoint(products, wide[0], count, 3, False)
    q_next = adjoint(products, wide[1], count, 3, True)
    ring = inject[0 : count * 24].reshape(count, 24, 128)
    p_next = [p_base[i] + p_next[i] + ring[:, 8 * i : 8 * i + 8] for i in range(3)]
    q_next = [q_base[i] + q_next[i] for i in range(3)]
    source = [p_weight[i] * p_next[i] + q_weight[i] * q_next[i] for i in range(3)]
    mix = [speed[i] * (p_next[i] + q_next[i]) for i in range(3)]
    products = [[tile[2 : 2 + count] for tile in entry] for entry in products]
    p_last = adjoint(products, source, size_x, 2, False)
    q_last = adjoint(products, mix, size_x, 2, True)
    inner = inject[count * 24 :].reshape(size_x, size_y, 128)
    p = loc[(FIELDS - 2) * size_x : (FIELDS - 1) * size_x]
    q = loc[(FIELDS - 1) * size_x : FIELDS * size_x]
    for i in range(2):
        ys = slice(8 * i, 8 * i + 8)
        p_out[:, ys, :] = 2.0 * p_next[i][mid] - p[:, ys] + inner[:, ys] + p_last[i]
        q_out[:, ys, :] = 2.0 * q_next[i][mid] - q[:, ys] + q_last[i]


def finish_kernel(own, other, grad_e, grad_d):
    total = [own[i] + other[i] for i in range(3)]
    scale = 1.0 / jnp.sqrt(total[2] + 1.0)
    grad_e[...] = total[0] * scale
    grad_d[...] = total[1] * scale


def swap(part, axis, start):
    lows = range(start, lax.axis_size(axis) - 1, 2)
    return lax.ppermute(part, axis, [(i, i + 1) for i in lows] + [(i + 1, i) for i in lows])


def body(
    p_adjoint,
    q_adjoint,
    p_previous,
    q_previous,
    forward_p,
    courant,
    epsilon,
    delta_field,
    tilt_angle,
    azimuth,
    receiver_cells,
    receiver_values,
    boundary_cells,
    boundary_force,
    source_cells,
):
    _, size_x, size_y, size_z = p_adjoint.shape
    grid_y = size_y * lax.axis_size("gy")
    p, q, p_old, q_old, f = (
        entry[0] for entry in (p_adjoint, q_adjoint, p_previous, q_previous, forward_p)
    )
    message = WIDE * size_x + NARROW * 2
    inputs = (p, q, p_old, q_old, f, courant, epsilon, delta_field, tilt_angle, azimuth)
    loc, far, near = call(
        prepare_kernel,
        [(FIELDS * size_x, size_y, size_z)] + [(message, size_y, size_z)] * 2,
        inputs,
        scratch=[pltpu.VMEM(entry.shape, entry.dtype) for entry in inputs]
        + [pltpu.SemaphoreType.DMA((len(inputs),))],
        space=pltpu.HBM,
    )
    far = swap(far, "gx", 1)
    near = swap(near, "gx", 0)
    rows = (size_x + 4) * 24 + size_x * size_y
    (inject,) = call(
        functools.partial(inject_kernel, grid_y, size_z, size_x, size_y),
        [(rows, size_z)],
        (receiver_cells, receiver_values[0], boundary_cells[None], boundary_force[0]),
        flops=800_000_000,
    )
    edges = (loc, far, near)
    early = (WIDE + 2) * (size_x + 4) // 4
    late = WIDE * (size_x + 8) // 2 + 5 * (size_x + 4) // 4
    odds, evens = call(early_kernel, [(early, 8, size_z)] * 2, edges)
    odds, evens = swap(odds, "gy", 1), swap(evens, "gy", 0)
    late_odds, late_evens = call(late_kernel, [(late, 8, size_z)] * 2, edges)
    (grads,) = call(
        functools.partial(first_step_kernel, grid_y),
        [(3, size_x, size_y, size_z)],
        (source_cells, *edges, odds, evens, inject),
        smem=(0,),
    )
    grads, late_odds, late_evens = lax.optimization_barrier((grads, late_odds, late_evens))
    shots = range(lax.axis_size("shot"))
    grads = grads + lax.ppermute(grads, "shot", [(i, i ^ 1) for i in shots])
    late_odds, late_evens = swap(late_odds, "gy", 1), swap(late_evens, "gy", 0)
    other = lax.ppermute(grads, "shot", [(i, i ^ 3) for i in shots])
    p_final, q_final = call(
        second_step_kernel,
        [(size_x, size_y, size_z)] * 2,
        (*edges, late_odds, late_evens, inject),
        flops=20_000_000,
    )
    grad_e, grad_d = call(finish_kernel, [(size_x, size_y, size_z)] * 2, (grads, other))
    return (p_final[None], q_final[None], grad_e, grad_d)


def solution(mesh):
    in_specs = (
        P("shot", "gx", "gy", None),
        P("shot", "gx", "gy", None),
        P("shot", "gx", "gy", None),
        P("shot", "gx", "gy", None),
        P("shot", None, "gx", "gy", None),
        P("gx", "gy", None),
        P("gx", "gy", None),
        P("gx", "gy", None),
        P("gx", "gy", None),
        P("gx", "gy", None),
        P("shot", None),
        P("shot", None, None),
        P(),
        P("shot", None, None),
        P("shot"),
    )
    out_specs = (
        P("shot", "gx", "gy", None),
        P("shot", "gx", "gy", None),
        P("gx", "gy", None),
        P("gx", "gy", None),
    )
    return jax.shard_map(body, mesh=mesh, in_specs=in_specs, out_specs=out_specs, check_vma=False)
```

```python
import functools

import jax
import jax.numpy as jnp
from jax import lax
from jax.experimental import pallas as pl
from jax.experimental.pallas import tpu as pltpu
from jax.sharding import PartitionSpec as P

TAPER = 32
EDGE = 5
BOTH = 7
ALONG = 12
FIELDS = 14
INPUTS = ("p", "q", "p_old", "q_old", "f", "c", "eps", "delta", "tilt", "azimuth")
PAIRS = ((0, 0), (1, 1), (2, 2), (0, 1), (0, 2), (1, 2))


def call(kernel, outs, args, scratch=(), smem=(), flops=2_000_000, space=pltpu.VMEM):
    specs = [
        pl.BlockSpec(memory_space=pltpu.SMEM if i in smem else space) for i in range(len(args))
    ]
    shapes = [jax.ShapeDtypeStruct(shape, jnp.float32) for shape in outs]
    return pl.pallas_call(
        kernel,
        out_shape=shapes,
        in_specs=specs,
        out_specs=[pl.BlockSpec(memory_space=pltpu.VMEM)] * len(outs),
        scratch_shapes=list(scratch),
        compiler_params=pltpu.CompilerParams(vmem_limit_bytes=24 * 1024 * 1024),
        cost_estimate=pl.CostEstimate(flops=flops, bytes_accessed=2_000_000, transcendentals=0),
    )(*(pltpu.with_memory_space_constraint(x, space) if space == pltpu.HBM else x for x in args))


def row_mask(shape, below):
    return lax.broadcasted_iota(jnp.int32, shape, len(shape) - 2) < below


def shift_y(tiles, step, keep=3):
    if step > 0:
        rolled = [pltpu.roll(tile, 8 - step, 1) for tile in tiles]
        mask = row_mask(tiles[0].shape, 8 - step)
        return [jnp.where(mask, rolled[i], rolled[(i + 1) % 3]) for i in range(keep)]
    rolled = [pltpu.roll(tile, -step, 1) for tile in tiles]
    mask = row_mask(tiles[0].shape, -step)
    return [jnp.where(mask, rolled[(i + 2) % 3], rolled[i]) for i in range(keep)]


def shift_z(tile, step):
    lane = lax.broadcasted_iota(jnp.int32, tile.shape, 2)
    rolled = pltpu.roll(tile, (-step) % 128, 2)
    inside = lane < 128 - step if step > 0 else lane >= -step
    return jnp.where(inside, rolled, 0.0)


def second(far_low, low, here, high, far_high):
    return (4.0 / 3.0) * (low + high) - (1.0 / 12.0) * (far_low + far_high) - 2.5 * here


def first(far_low, low, high, far_high):
    return (2.0 / 3.0) * (high - low) - (1.0 / 12.0) * (far_high - far_low)


def second_x(tile, count):
    return second(*[tile[i : i + count] for i in range(5)])


def first_x(tile, count):
    return first(*[tile[i : i + count] for i in (0, 1, 3, 4)])


def first_y(tiles, keep):
    low2, low1, high1, high2 = [shift_y(tiles, step, keep) for step in (-2, -1, 1, 2)]
    return [first(low2[i], low1[i], high1[i], high2[i]) for i in range(keep)]


def both(parts_second, parts_first):
    near_even = (4.0 / 3.0) * parts_second
    near_odd = (2.0 / 3.0) * parts_first
    far_even = (-1.0 / 12.0) * parts_second
    far_odd = (1.0 / 12.0) * parts_first
    return (far_even + far_odd, near_even - near_odd, near_even + near_odd, far_even - far_odd)


def adjoint(products, source, count, keep, plus):
    mid = slice(2, 2 + count)
    aa = []
    for axis in range(3):
        scaled = [products[axis][i] * source[i] for i in range(3)]
        aa.append(scaled if plus else [source[i] - scaled[i] for i in range(3)])
    factor = 2.0 if plus else -2.0
    doubled = [factor * tile for tile in source]
    n01 = [products[3][i] * doubled[i] for i in range(3)]
    n02 = [products[4][i] * doubled[i] for i in range(keep)]
    n12 = [products[5][i][mid] * doubled[i][mid] for i in range(3)]
    out = [second_x(aa[0][i], count) for i in range(keep)]
    second_y = [tile[mid] for tile in aa[1]]
    cross_y = [first_x(tile, count) for tile in n01]
    mixed = [both(second_y[i], cross_y[i]) for i in range(3)]
    out = [out[i] - 2.5 * second_y[i] for i in range(keep)]
    for number, step in enumerate((-2, -1, 1, 2)):
        moved = shift_y([mixed[i][number] for i in range(3)], step, keep)
        out = [out[i] + moved[i] for i in range(keep)]
    along_y = first_y(n12, keep)
    for i in range(keep):
        second_z = aa[2][i][mid]
        cross_z = first_x(n02[i], count) + along_y[i]
        terms = both(second_z, cross_z)
        out[i] = out[i] - 2.5 * second_z
        for number, step in enumerate((-2, -1, 1, 2)):
            out[i] = out[i] + shift_z(terms[number], step)
    return out


def forward_image(products, field, count):
    mid = slice(2, 2 + count)
    inner = [tile[mid] for tile in field]
    slope_x = [first_x(tile, count) for tile in field]
    moved = [shift_y(inner, step, 2) for step in (-2, -1, 1, 2)]
    cross = first_y(slope_x, 2)
    out = []
    for i in range(2):
        here = inner[i]
        along = [moved[k][i] for k in range(4)]
        curve_x = second_x(field[i], count)
        curve_y = second(along[0], along[1], here, along[2], along[3])
        slope_y = first(*along)
        depth = [shift_z(here, step) for step in (-2, -1, 1, 2)]
        curve_z = second(depth[0], depth[1], here, depth[2], depth[3])
        total = (1.0 - products[0][i]) * curve_x
        total = total + (1.0 - products[1][i]) * curve_y
        total = total + (1.0 - products[2][i]) * curve_z
        cross_z = []
        for slope in (slope_x[i], slope_y):
            cross_z.append(first(*[shift_z(slope, step) for step in (-2, -1, 1, 2)]))
        mixed = products[3][i] * cross[i] + products[4][i] * cross_z[0] + products[5][i] * cross_z[1]
        out.append(total - 2.0 * mixed)
    return out


def prepare_kernel(*refs):
    count = len(INPUTS)
    arrays, (loc, far, near), held, arrived = refs[:count], refs[count : count + 3], refs[-count - 1 : -1], refs[-1]
    copies = [pltpu.make_async_copy(arrays[i], held[i], arrived.at[i]) for i in range(count)]
    for copy in copies:
        copy.start()
    for copy in copies:
        copy.wait()
    p, q, p_old, q_old, f, c, eps, delta, tilt, azimuth = held
    size_x = p.shape[0]
    p_now, q_now, speed = p[...], q[...], c[...]
    p_weight = speed * (1.0 + 2.0 * eps[...])
    q_weight = speed * (1.0 + 2.0 * delta[...])
    sine = jnp.sin(tilt[...])
    fields = (
        p_weight * p_now + q_weight * q_now,
        speed * (p_now + q_now),
        sine * jnp.cos(azimuth[...]),
        sine * jnp.sin(azimuth[...]),
        jnp.cos(tilt[...]),
        f[0],
        f[1],
        2.0 * p_now - p_old[...],
        2.0 * q_now - q_old[...],
        p_weight,
        q_weight,
        speed,
        p_now,
        q_now,
    )
    for number, cells in enumerate(fields):
        loc[number * size_x : (number + 1) * size_x] = cells
    send_x(loc, near, far, BOTH, size_x)


def send_x(loc, near, far, count, size_x):
    odd = lax.rem(lax.axis_index("gx"), 2)
    upper, lower = (1 - odd) * (size_x - 2), odd * (size_x - 2)
    for number in range(count):
        rows = slice(2 * number, 2 * number + 2)
        near[rows] = loc[pl.ds(number * size_x + upper, 2)]
        far[rows] = loc[pl.ds(number * size_x + lower, 2)]


def with_rows(loc, near, far, count, size_x, part):
    ys = slice(8 * part, 8 * part + 8)
    odd = lax.rem(lax.axis_index("gx"), 2) == 1
    first, second = near[:, ys, :], far[:, ys, :]
    below, above = jnp.where(odd, first, second), jnp.where(odd, second, first)
    out = []
    for number in range(count):
        rows = slice(2 * number, 2 * number + 2)
        here = loc[number * size_x : (number + 1) * size_x, ys, :]
        out.append(jnp.concatenate([below[rows], here, above[rows]], axis=0))
    return out


def turn(rows, by):
    by = by % 8
    return pltpu.roll(rows, by, 1) if by else rows


def pack(rows, part, groups):
    height, count = 8 // groups, rows.shape[0] // groups
    out = None
    for group in range(groups):
        piece = turn(rows[group * count : (group + 1) * count], height * (group - part * (groups - 1)))
        mask = row_mask(piece.shape, height * group)
        out = piece if out is None else jnp.where(mask, out, piece)
    return out


def unpack(high, low, groups):
    height = 8 // groups
    edges = []
    for group in range(groups):
        upper = turn(high, -height * group)
        lower = turn(low, height * (groups - 1 - group))
        edges.append(jnp.where(row_mask(high.shape, 4), upper, lower))
    return jnp.concatenate(edges, axis=0)


def send_both(parts, evens, odds, start):
    odd = lax.rem(lax.axis_index("gy"), 2) == 1
    rows = slice(start, start + parts[0].shape[0])
    evens[rows] = jnp.where(odd, parts[0], parts[1])
    odds[rows] = jnp.where(odd, parts[1], parts[0])


def from_both(evens, odds):
    odd = lax.rem(lax.axis_index("gy"), 2) == 1
    return jnp.where(odd, odds[...], evens[...]), jnp.where(odd, evens[...], odds[...])


def pack_kernel(loc, far, near, odds, evens):
    size_x = loc.shape[0] // FIELDS
    groups = ([], [], [])
    for part in range(2):
        ys = slice(8 * part, 8 * part + 8)
        tiles = with_rows(loc, near, far, BOTH, size_x, part)
        groups[0].append(pack(jnp.concatenate(tiles[:EDGE], axis=0), part, 2))
        groups[1].append(pack(jnp.concatenate(tiles[EDGE:], axis=0), part, 4))
        groups[2].append(pack(loc[BOTH * size_x : ALONG * size_x, ys, :], part, 4))
    start = 0
    for parts in groups:
        send_both(parts, evens, odds, start)
        start += parts[0].shape[0]


def fields_of(loc, far, near, odds, evens, every):
    size_x = loc.shape[0] // FIELDS
    count = size_x + 4
    high, low = from_both(evens, odds)
    ends = (EDGE * count // 2, EDGE * count // 2 + (BOTH - EDGE) * count // 4)
    edge = cut(unpack(high[: ends[0]], low[: ends[0]], 2), count)
    tiles = [with_rows(loc, near, far, BOTH if every else EDGE, size_x, part) for part in range(2)]
    if every:
        edge += cut(unpack(high[ends[0] : ends[1]], low[ends[0] : ends[1]], 4), count)
    fields = [[tiles[0][n], tiles[1][n], edge[n]] for n in range(len(edge))]
    along = []
    if every:
        edge = cut(unpack(high[ends[1] :], low[ends[1] :], 4), size_x)
        for number in range(ALONG - BOTH):
            rows = loc[(BOTH + number) * size_x : (BOTH + number + 1) * size_x]
            along.append([rows[:, 0:8], rows[:, 8:16], edge[number]])
    products = [[fields[2 + a][i] * fields[2 + b][i] for i in range(3)] for a, b in PAIRS]
    return fields, along, products


def cut(rows, count):
    return [rows[i : i + count] for i in range(0, rows.shape[0], count)]


def inject_kernel(grid_y, grid_z, size_x, size_y, recv_cells, recv_values, bound_cells, bound_force, out):
    bits_y, bits_z = grid_y.bit_length() - 1, grid_z.bit_length() - 1
    start_x = lax.axis_index("gx") * size_x
    start_y = lax.axis_index("gy") * size_y
    ring = size_x * 24
    inner = size_x * size_y
    chunk = 512
    total = jnp.zeros((3 * (ring + inner), grid_z), jnp.float32)
    for cells_ref, values_ref, shift in ((recv_cells, recv_values, 0), (bound_cells, bound_force, bits_z)):
        for begin in range(0, cells_ref.shape[-1], chunk):
            cells = cells_ref[0:1, begin : begin + chunk]
            across = cells >> shift
            depth = cells & (grid_z - 1) if shift else jnp.zeros_like(cells)
            cell_x = (across >> bits_y) - start_x
            cell_y = (across & (grid_y - 1)) - start_y
            near = (cell_x >= 0) & (cell_x < size_x) & (cell_y >= -2) & (cell_y < size_y + 2)
            wrapped = jnp.where(cell_y < 0, cell_y + 24, cell_y)
            ring_row = jnp.where(near, cell_x * 24 + wrapped, -1)
            inside = (cell_x >= 0) & (cell_x < size_x) & (cell_y >= 0) & (cell_y < size_y)
            inner_row = jnp.where(inside, cell_x * size_y + cell_y, -1)
            ring_hit = lax.broadcasted_iota(jnp.int32, (ring, chunk), 0) == ring_row
            inner_hit = lax.broadcasted_iota(jnp.int32, (inner, chunk), 0) == inner_row
            columns = lax.broadcasted_iota(jnp.int32, (grid_z, chunk), 0) == depth
            columns = jnp.where(columns, 1.0, 0.0).astype(jnp.bfloat16)
            pieces = []
            parts = []
            for step in range(2):
                value = values_ref[step : step + 1, begin : begin + chunk]
                split = []
                for _ in range(3):
                    top = value.astype(jnp.bfloat16).astype(jnp.float32)
                    split.append(top)
                    value = value - top
                parts.append(split)
            for number in range(3):
                pieces.append(jnp.where(ring_hit, parts[0][number], 0.0).astype(jnp.bfloat16))
                pieces.append(jnp.where(inner_hit, parts[1][number], 0.0).astype(jnp.bfloat16))
            total = total + lax.dot_general(
                jnp.concatenate(pieces, axis=0),
                columns,
                (((1,), (1,)), ((), ())),
                preferred_element_type=jnp.float32,
            )
    rows = ring + inner
    out[...] = total[0:rows] + total[rows : 2 * rows] + total[2 * rows : 3 * rows]


def first_step_kernel(grid_y, source, loc, far, near, odds, evens, inject, grads, now, ahead, near_next, far_next):
    size_x = loc.shape[0] // FIELDS
    fields, along, products = fields_of(loc, far, near, odds, evens, True)
    p_base, q_base, p_weight, q_weight, speed = along
    mid = slice(2, 2 + size_x)
    p_next = adjoint(products, fields[0], size_x, 3, False)
    q_next = adjoint(products, fields[1], size_x, 3, True)
    inner = [[tile[mid] for tile in entry] for entry in products]
    images = [forward_image(inner, field, size_x) for field in fields[EDGE:BOTH]]
    ring = inject[0 : size_x * 24].reshape(size_x, 24, 128)
    p_next = [p_base[i] + p_next[i] + ring[:, 8 * i : 8 * i + 8] for i in range(3)]
    q_next = [q_base[i] + q_next[i] for i in range(3)]
    for i in range(3):
        ys = slice(8 * i, 8 * i + 8)
        ahead[0:size_x, ys, :] = p_weight[i] * p_next[i] + q_weight[i] * q_next[i]
        ahead[size_x : 2 * size_x, ys, :] = speed[i] * (p_next[i] + q_next[i])
    send_x(ahead, near_next, far_next, 2, size_x)
    bits_y = grid_y.bit_length() - 1
    source_x = (source[0] >> bits_y) - lax.axis_index("gx") * size_x
    source_y = (source[0] & (grid_y - 1)) - lax.axis_index("gy") * loc.shape[1]
    shape = (size_x, 8, 128)
    offset_x = lax.broadcasted_iota(jnp.int32, shape, 0) - source_x
    for i in range(2):
        ys = slice(8 * i, 8 * i + 8)
        offset_y = lax.broadcasted_iota(jnp.int32, shape, 1) + (8 * i - source_y)
        squared = (offset_x * offset_x + offset_y * offset_y).astype(jnp.float32)
        taper = jnp.minimum(squared * (1.0 / float(TAPER * TAPER)), 1.0)
        scale = taper * (2.0 * speed[i])
        image0, image1 = scale * images[0][i], scale * images[1][i]
        p, q = [loc[n * size_x : (n + 1) * size_x, ys, :] for n in (FIELDS - 2, FIELDS - 1)]
        f0, f1 = fields[EDGE][i][mid], fields[EDGE + 1][i][mid]
        grads[0, :, ys, :] = p * image0 + p_next[i] * image1
        grads[1, :, ys, :] = q * image0 + q_next[i] * image1
        grads[2, :, ys, :] = f0 * f0 + f1 * f1
        now[0, :, ys, :] = p_next[i]
        now[1, :, ys, :] = q_next[i]


def second_step_kernel(loc, far, near, odds, evens, now, ahead, far_next, near_next, inject, p_out, q_out):
    size_x, size_y = p_out.shape[0], p_out.shape[1]
    _, _, products = fields_of(loc, far, near, odds, evens, False)
    tiles = [with_rows(ahead, near_next, far_next, 2, size_x, part) for part in range(3)]
    p_last = adjoint(products, [tile[0] for tile in tiles], size_x, 2, False)
    q_last = adjoint(products, [tile[1] for tile in tiles], size_x, 2, True)
    inner = inject[size_x * 24 :].reshape(size_x, size_y, 128)
    p = loc[(FIELDS - 2) * size_x : (FIELDS - 1) * size_x]
    q = loc[(FIELDS - 1) * size_x : FIELDS * size_x]
    for i in range(2):
        ys = slice(8 * i, 8 * i + 8)
        p_out[:, ys, :] = 2.0 * now[0, :, ys, :] - p[:, ys] + inner[:, ys] + p_last[i]
        q_out[:, ys, :] = 2.0 * now[1, :, ys, :] - q[:, ys] + q_last[i]


def finish_kernel(own, other, grad_e, grad_d):
    total = [own[i] + other[i] for i in range(3)]
    scale = 1.0 / jnp.sqrt(total[2] + 1.0)
    grad_e[...] = total[0] * scale
    grad_d[...] = total[1] * scale


def swap(part, axis, start):
    lows = range(start, lax.axis_size(axis) - 1, 2)
    return lax.ppermute(part, axis, [(i, i + 1) for i in lows] + [(i + 1, i) for i in lows])


def body(
    p_adjoint,
    q_adjoint,
    p_previous,
    q_previous,
    forward_p,
    courant,
    epsilon,
    delta_field,
    tilt_angle,
    azimuth,
    receiver_cells,
    receiver_values,
    boundary_cells,
    boundary_force,
    source_cells,
):
    _, size_x, size_y, size_z = p_adjoint.shape
    grid_y = size_y * lax.axis_size("gy")
    p, q, p_old, q_old, f = (
        entry[0] for entry in (p_adjoint, q_adjoint, p_previous, q_previous, forward_p)
    )
    message = 2 * BOTH
    inputs = (p, q, p_old, q_old, f, courant, epsilon, delta_field, tilt_angle, azimuth)
    loc, far, near = call(
        prepare_kernel,
        [(FIELDS * size_x, size_y, size_z)] + [(message, size_y, size_z)] * 2,
        inputs,
        scratch=[pltpu.VMEM(entry.shape, entry.dtype) for entry in inputs]
        + [pltpu.SemaphoreType.DMA((len(inputs),))],
        space=pltpu.HBM,
    )
    far = swap(far, "gx", 1)
    near = swap(near, "gx", 0)
    rows = size_x * 24 + size_x * size_y
    (inject,) = call(
        functools.partial(inject_kernel, grid_y, size_z, size_x, size_y),
        [(rows, size_z)],
        (receiver_cells, receiver_values[0], boundary_cells[None], boundary_force[0]),
        flops=800_000_000,
    )
    count = EDGE * (size_x + 4) // 2 + (BOTH - EDGE) * (size_x + 4) // 4 + (ALONG - BOTH) * size_x // 4
    odds, evens = call(pack_kernel, [(count, 8, size_z)] * 2, (loc, far, near))
    odds, evens = swap(odds, "gy", 1), swap(evens, "gy", 0)
    edges = (loc, far, near, odds, evens)
    grads, now, ahead, near_next, far_next = call(
        functools.partial(first_step_kernel, grid_y),
        [
            (3, size_x, size_y, size_z),
            (2, size_x, size_y, size_z),
            (2 * size_x, 24, size_z),
            (4, 24, size_z),
            (4, 24, size_z),
        ],
        (source_cells, *edges, inject),
        smem=(0,),
    )
    shots = range(lax.axis_size("shot"))
    grads = grads + lax.ppermute(grads, "shot", [(i, i ^ 1) for i in shots])
    far_next, near_next = swap(far_next, "gx", 1), swap(near_next, "gx", 0)
    grads, far_next, near_next = lax.optimization_barrier((grads, far_next, near_next))
    other = lax.ppermute(grads, "shot", [(i, i ^ 3) for i in shots])
    p_final, q_final = call(
        second_step_kernel,
        [(size_x, size_y, size_z)] * 2,
        (*edges, now, ahead, far_next, near_next, inject),
        flops=20_000_000,
    )
    grad_e, grad_d = call(finish_kernel, [(size_x, size_y, size_z)] * 2, (grads, other))
    return (p_final[None], q_final[None], grad_e, grad_d)


def solution(mesh):
    in_specs = (
        P("shot", "gx", "gy", None),
        P("shot", "gx", "gy", None),
        P("shot", "gx", "gy", None),
        P("shot", "gx", "gy", None),
        P("shot", None, "gx", "gy", None),
        P("gx", "gy", None),
        P("gx", "gy", None),
        P("gx", "gy", None),
        P("gx", "gy", None),
        P("gx", "gy", None),
        P("shot", None),
        P("shot", None, None),
        P(),
        P("shot", None, None),
        P("shot"),
    )
    out_specs = (
        P("shot", "gx", "gy", None),
        P("shot", "gx", "gy", None),
        P("gx", "gy", None),
        P("gx", "gy", None),
    )
    return jax.shard_map(body, mesh=mesh, in_specs=in_specs, out_specs=out_specs, check_vma=False)
```

```python
import functools

import jax
import jax.numpy as jnp
from jax import lax
from jax.experimental import pallas as pl
from jax.experimental.pallas import tpu as pltpu
from jax.sharding import PartitionSpec as P

TAPER = 32
WIDE = 5
NARROW = 7
FIELDS = WIDE + NARROW + 2
INPUTS = ("p", "q", "p_old", "q_old", "f", "c", "eps", "delta", "tilt", "azimuth")
PAIRS = ((0, 0), (1, 1), (2, 2), (0, 1), (0, 2), (1, 2))


def call(kernel, outs, args, scratch=(), smem=(), flops=2_000_000, space=pltpu.VMEM):
    specs = [
        pl.BlockSpec(memory_space=pltpu.SMEM if i in smem else space) for i in range(len(args))
    ]
    shapes = [jax.ShapeDtypeStruct(shape, jnp.float32) for shape in outs]
    return pl.pallas_call(
        kernel,
        out_shape=shapes,
        in_specs=specs,
        out_specs=[pl.BlockSpec(memory_space=pltpu.VMEM)] * len(outs),
        scratch_shapes=list(scratch),
        compiler_params=pltpu.CompilerParams(vmem_limit_bytes=24 * 1024 * 1024),
        cost_estimate=pl.CostEstimate(flops=flops, bytes_accessed=2_000_000, transcendentals=0),
    )(*(pltpu.with_memory_space_constraint(x, space) if space == pltpu.HBM else x for x in args))


def row_mask(shape, below):
    return lax.broadcasted_iota(jnp.int32, shape, len(shape) - 2) < below


def shift_y(tiles, step, keep=3):
    if step > 0:
        rolled = [pltpu.roll(tile, 8 - step, 1) for tile in tiles]
        mask = row_mask(tiles[0].shape, 8 - step)
        return [jnp.where(mask, rolled[i], rolled[(i + 1) % 3]) for i in range(keep)]
    rolled = [pltpu.roll(tile, -step, 1) for tile in tiles]
    mask = row_mask(tiles[0].shape, -step)
    return [jnp.where(mask, rolled[(i + 2) % 3], rolled[i]) for i in range(keep)]


def shift_z(tile, step):
    lane = lax.broadcasted_iota(jnp.int32, tile.shape, 2)
    rolled = pltpu.roll(tile, (-step) % 128, 2)
    inside = lane < 128 - step if step > 0 else lane >= -step
    return jnp.where(inside, rolled, 0.0)


def second(far_low, low, here, high, far_high):
    return (4.0 / 3.0) * (low + high) - (1.0 / 12.0) * (far_low + far_high) - 2.5 * here


def first(far_low, low, high, far_high):
    return (2.0 / 3.0) * (high - low) - (1.0 / 12.0) * (far_high - far_low)


def second_x(tile, count):
    return second(*[tile[i : i + count] for i in range(5)])


def first_x(tile, count):
    return first(*[tile[i : i + count] for i in (0, 1, 3, 4)])


def first_y(tiles, keep):
    low2, low1, high1, high2 = [shift_y(tiles, step, keep) for step in (-2, -1, 1, 2)]
    return [first(low2[i], low1[i], high1[i], high2[i]) for i in range(keep)]


def both(parts_second, parts_first):
    near_even = (4.0 / 3.0) * parts_second
    near_odd = (2.0 / 3.0) * parts_first
    far_even = (-1.0 / 12.0) * parts_second
    far_odd = (1.0 / 12.0) * parts_first
    return (far_even + far_odd, near_even - near_odd, near_even + near_odd, far_even - far_odd)


def adjoint(products, source, count, keep, plus):
    mid = slice(2, 2 + count)
    aa = []
    for axis in range(3):
        scaled = [products[axis][i] * source[i] for i in range(3)]
        aa.append(scaled if plus else [source[i] - scaled[i] for i in range(3)])
    factor = 2.0 if plus else -2.0
    doubled = [factor * tile for tile in source]
    n01 = [products[3][i] * doubled[i] for i in range(3)]
    n02 = [products[4][i] * doubled[i] for i in range(keep)]
    n12 = [products[5][i][mid] * doubled[i][mid] for i in range(3)]
    out = [second_x(aa[0][i], count) for i in range(keep)]
    second_y = [tile[mid] for tile in aa[1]]
    cross_y = [first_x(tile, count) for tile in n01]
    mixed = [both(second_y[i], cross_y[i]) for i in range(3)]
    out = [out[i] - 2.5 * second_y[i] for i in range(keep)]
    for number, step in enumerate((-2, -1, 1, 2)):
        moved = shift_y([mixed[i][number] for i in range(3)], step, keep)
        out = [out[i] + moved[i] for i in range(keep)]
    along_y = first_y(n12, keep)
    for i in range(keep):
        second_z = aa[2][i][mid]
        cross_z = first_x(n02[i], count) + along_y[i]
        terms = both(second_z, cross_z)
        out[i] = out[i] - 2.5 * second_z
        for number, step in enumerate((-2, -1, 1, 2)):
            out[i] = out[i] + shift_z(terms[number], step)
    return out


def forward_image(products, field, count):
    mid = slice(2, 2 + count)
    inner = [tile[mid] for tile in field]
    slope_x = [first_x(tile, count) for tile in field]
    moved = [shift_y(inner, step, 2) for step in (-2, -1, 1, 2)]
    cross = first_y(slope_x, 2)
    out = []
    for i in range(2):
        here = inner[i]
        along = [moved[k][i] for k in range(4)]
        curve_x = second_x(field[i], count)
        curve_y = second(along[0], along[1], here, along[2], along[3])
        slope_y = first(*along)
        depth = [shift_z(here, step) for step in (-2, -1, 1, 2)]
        curve_z = second(depth[0], depth[1], here, depth[2], depth[3])
        total = (1.0 - products[0][i]) * curve_x
        total = total + (1.0 - products[1][i]) * curve_y
        total = total + (1.0 - products[2][i]) * curve_z
        cross_z = []
        for slope in (slope_x[i], slope_y):
            cross_z.append(first(*[shift_z(slope, step) for step in (-2, -1, 1, 2)]))
        mixed = products[3][i] * cross[i] + products[4][i] * cross_z[0] + products[5][i] * cross_z[1]
        out.append(total - 2.0 * mixed)
    return out


def prepare_kernel(*refs):
    count = len(INPUTS)
    arrays, (loc, far, near), held, arrived = refs[:count], refs[count : count + 3], refs[-count - 1 : -1], refs[-1]
    copies = [pltpu.make_async_copy(arrays[i], held[i], arrived.at[i]) for i in range(count)]
    for copy in copies:
        copy.start()
    for copy in copies:
        copy.wait()
    p, q, p_old, q_old, f, c, eps, delta, tilt, azimuth = held
    size_x = p.shape[0]
    p_now, q_now, speed = p[...], q[...], c[...]
    p_weight = speed * (1.0 + 2.0 * eps[...])
    q_weight = speed * (1.0 + 2.0 * delta[...])
    sine = jnp.sin(tilt[...])
    wide = (
        p_weight * p_now + q_weight * q_now,
        speed * (p_now + q_now),
        sine * jnp.cos(azimuth[...]),
        sine * jnp.sin(azimuth[...]),
        jnp.cos(tilt[...]),
    )
    narrow = (
        2.0 * p_now - p_old[...],
        2.0 * q_now - q_old[...],
        p_weight,
        q_weight,
        speed,
        f[0],
        f[1],
    )
    for number, cells in enumerate(wide):
        rows = slice(number * size_x, (number + 1) * size_x)
        loc[rows] = cells
        near[rows] = cells
        far[rows] = cells
    for number, cells in enumerate(narrow + (p_now, q_now)):
        start = (WIDE + number) * size_x
        loc[start : start + size_x] = cells
    odd = lax.rem(lax.axis_index("gx"), 2)
    upper, lower = (1 - odd) * (size_x - 2), odd * (size_x - 2)
    for number in range(NARROW):
        start = (WIDE + number) * size_x
        begin = WIDE * size_x + 2 * number
        near[begin : begin + 2] = loc[pl.ds(start + upper, 2)]
        far[begin : begin + 2] = loc[pl.ds(start + lower, 2)]


def tiles_of(loc, near, far, size_x, part):
    ys = slice(8 * part, 8 * part + 8)
    odd = lax.rem(lax.axis_index("gx"), 2) == 1
    first, second = near[:, ys, :], far[:, ys, :]
    below, above = jnp.where(odd, first, second), jnp.where(odd, second, first)
    wide, narrow = [], []
    for number in range(WIDE):
        rows = slice(number * size_x, (number + 1) * size_x)
        wide.append(jnp.concatenate([below[rows], loc[rows, ys, :], above[rows]], axis=0))
    for number in range(NARROW):
        start = (WIDE + number) * size_x
        begin = WIDE * size_x + 2 * number
        rows = slice(begin, begin + 2)
        here = loc[start : start + size_x, ys, :]
        narrow.append(jnp.concatenate([below[rows], here, above[rows]], axis=0))
    return wide, narrow


def turn(rows, by):
    by = by % 8
    return pltpu.roll(rows, by, 1) if by else rows


def pack(rows, part, groups):
    height, count = 8 // groups, rows.shape[0] // groups
    out = None
    for group in range(groups):
        piece = turn(rows[group * count : (group + 1) * count], height * (group - part * (groups - 1)))
        mask = row_mask(piece.shape, height * group)
        out = piece if out is None else jnp.where(mask, out, piece)
    return out


def unpack(high, low, groups):
    height = 8 // groups
    edges = []
    for group in range(groups):
        upper = turn(high, -height * group)
        lower = turn(low, height * (groups - 1 - group))
        edges.append(jnp.where(row_mask(high.shape, 4), upper, lower))
    return jnp.concatenate(edges, axis=0)


def early_rows(wide, narrow):
    return [tile[2 : tile.shape[0] - 2] for tile in wide] + narrow[5:]


def send_both(parts, evens, odds, start):
    odd = lax.rem(lax.axis_index("gy"), 2) == 1
    rows = slice(start, start + parts[0].shape[0])
    evens[rows] = jnp.where(odd, parts[0], parts[1])
    odds[rows] = jnp.where(odd, parts[1], parts[0])


def from_both(evens, odds):
    odd = lax.rem(lax.axis_index("gy"), 2) == 1
    return jnp.where(odd, odds[...], evens[...]), jnp.where(odd, evens[...], odds[...])


def early_kernel(loc, far, near, odds, evens):
    size_x = loc.shape[0] // FIELDS
    parts = []
    for part in range(2):
        wide, narrow = tiles_of(loc, near, far, size_x, part)
        parts.append(pack(jnp.concatenate(early_rows(wide, narrow), axis=0), part, 4))
    send_both(parts, evens, odds, 0)


def late_kernel(loc, far, near, odds, evens):
    size_x = loc.shape[0] // FIELDS
    wides, narrows = [], []
    for part in range(2):
        wide, narrow = tiles_of(loc, near, far, size_x, part)
        wides.append(pack(jnp.concatenate(wide, axis=0), part, 2))
        narrows.append(pack(jnp.concatenate(narrow[:5], axis=0), part, 4))
    send_both(wides, evens, odds, 0)
    send_both(narrows, evens, odds, wides[0].shape[0])


def cut(rows, count):
    return [rows[i : i + count] for i in range(0, rows.shape[0], count)]


def inject_kernel(grid_y, grid_z, size_x, size_y, recv_cells, recv_values, bound_cells, bound_force, out):
    bits_y, bits_z = grid_y.bit_length() - 1, grid_z.bit_length() - 1
    start_x = lax.axis_index("gx") * size_x
    start_y = lax.axis_index("gy") * size_y
    ring = (size_x + 4) * 24
    inner = size_x * size_y
    chunk = 512
    total = jnp.zeros((3 * (ring + inner), grid_z), jnp.float32)
    for cells_ref, values_ref, shift in ((recv_cells, recv_values, 0), (bound_cells, bound_force, bits_z)):
        for begin in range(0, cells_ref.shape[-1], chunk):
            cells = cells_ref[0:1, begin : begin + chunk]
            across = cells >> shift
            depth = cells & (grid_z - 1) if shift else jnp.zeros_like(cells)
            cell_x = (across >> bits_y) - start_x
            cell_y = (across & (grid_y - 1)) - start_y
            near = (cell_x >= -2) & (cell_x < size_x + 2) & (cell_y >= -2) & (cell_y < size_y + 2)
            wrapped = jnp.where(cell_y < 0, cell_y + 24, cell_y)
            ring_row = jnp.where(near, (cell_x + 2) * 24 + wrapped, -1)
            inside = (cell_x >= 0) & (cell_x < size_x) & (cell_y >= 0) & (cell_y < size_y)
            inner_row = jnp.where(inside, cell_x * size_y + cell_y, -1)
            ring_hit = lax.broadcasted_iota(jnp.int32, (ring, chunk), 0) == ring_row
            inner_hit = lax.broadcasted_iota(jnp.int32, (inner, chunk), 0) == inner_row
            columns = lax.broadcasted_iota(jnp.int32, (grid_z, chunk), 0) == depth
            columns = jnp.where(columns, 1.0, 0.0).astype(jnp.bfloat16)
            pieces = []
            parts = []
            for step in range(2):
                value = values_ref[step : step + 1, begin : begin + chunk]
                split = []
                for _ in range(3):
                    top = value.astype(jnp.bfloat16).astype(jnp.float32)
                    split.append(top)
                    value = value - top
                parts.append(split)
            for number in range(3):
                pieces.append(jnp.where(ring_hit, parts[0][number], 0.0).astype(jnp.bfloat16))
                pieces.append(jnp.where(inner_hit, parts[1][number], 0.0).astype(jnp.bfloat16))
            total = total + lax.dot_general(
                jnp.concatenate(pieces, axis=0),
                columns,
                (((1,), (1,)), ((), ())),
                preferred_element_type=jnp.float32,
            )
    rows = ring + inner
    out[...] = total[0:rows] + total[rows : 2 * rows] + total[2 * rows : 3 * rows]


def first_step_kernel(grid_y, source, loc, far_x, near_x, evens, odds, inject, grads):
    size_x, size_y = loc.shape[0] // FIELDS, loc.shape[1]
    count = size_x + 4
    high, low = from_both(evens, odds)
    edge = cut(unpack(high, low, 4), count)
    middle = [early_rows(*tiles_of(loc, near_x, far_x, size_x, part)) for part in range(2)]
    fields = [[middle[0][n], middle[1][n], edge[n]] for n in range(len(edge))]
    products = [[fields[2 + a][i] * fields[2 + b][i] for i in range(3)] for a, b in PAIRS]
    mid = slice(2, 2 + size_x)
    p_next = adjoint(products, fields[0], size_x, 2, False)
    q_next = adjoint(products, fields[1], size_x, 2, True)
    inner = [[tile[mid] for tile in entry] for entry in products]
    images = [forward_image(inner, field, size_x) for field in fields[5:7]]
    ring = inject[0 : count * 24].reshape(count, 24, 128)
    bits_y = grid_y.bit_length() - 1
    source_x = (source[0] >> bits_y) - lax.axis_index("gx") * size_x
    source_y = (source[0] & (grid_y - 1)) - lax.axis_index("gy") * size_y
    shape = (size_x, 8, 128)
    offset_x = lax.broadcasted_iota(jnp.int32, shape, 0) - source_x

    def block(field, ys):
        return loc[field * size_x : (field + 1) * size_x, ys, :]

    for i in range(2):
        ys = slice(8 * i, 8 * i + 8)
        offset_y = lax.broadcasted_iota(jnp.int32, shape, 1) + (8 * i - source_y)
        squared = (offset_x * offset_x + offset_y * offset_y).astype(jnp.float32)
        taper = jnp.minimum(squared * (1.0 / float(TAPER * TAPER)), 1.0)
        scale = taper * (2.0 * block(WIDE + 4, ys))
        image0, image1 = scale * images[0][i], scale * images[1][i]
        p_mid = block(WIDE, ys) + p_next[i] + ring[mid, ys, :]
        q_mid = block(WIDE + 1, ys) + q_next[i]
        grads[0, :, ys, :] = block(FIELDS - 2, ys) * image0 + p_mid * image1
        grads[1, :, ys, :] = block(FIELDS - 1, ys) * image0 + q_mid * image1
        f0, f1 = block(WIDE + 5, ys), block(WIDE + 6, ys)
        grads[2, :, ys, :] = f0 * f0 + f1 * f1


def second_step_kernel(loc, far_x, near_x, evens, odds, inject, p_out, q_out):
    size_x, size_y = p_out.shape[0], p_out.shape[1]
    count = size_x + 4
    high, low = from_both(evens, odds)
    half = WIDE * (size_x + 8) // 2
    wide_edge = cut(unpack(high[:half], low[:half], 2), size_x + 8)
    narrow_edge = cut(unpack(high[half:], low[half:], 4), count)
    parts = [tiles_of(loc, near_x, far_x, size_x, part) for part in range(2)]
    wide = [[parts[0][0][n], parts[1][0][n], wide_edge[n]] for n in range(WIDE)]
    narrow = [[parts[0][1][n], parts[1][1][n], narrow_edge[n]] for n in range(5)]
    products = [[wide[2 + a][i] * wide[2 + b][i] for i in range(3)] for a, b in PAIRS]
    p_base, q_base, p_weight, q_weight, speed = narrow
    mid = slice(2, 2 + size_x)
    p_next = adjoint(products, wide[0], count, 3, False)
    q_next = adjoint(products, wide[1], count, 3, True)
    ring = inject[0 : count * 24].reshape(count, 24, 128)
    p_next = [p_base[i] + p_next[i] + ring[:, 8 * i : 8 * i + 8] for i in range(3)]
    q_next = [q_base[i] + q_next[i] for i in range(3)]
    source = [p_weight[i] * p_next[i] + q_weight[i] * q_next[i] for i in range(3)]
    mix = [speed[i] * (p_next[i] + q_next[i]) for i in range(3)]
    products = [[tile[2 : 2 + count] for tile in entry] for entry in products]
    p_last = adjoint(products, source, size_x, 2, False)
    q_last = adjoint(products, mix, size_x, 2, True)
    inner = inject[count * 24 :].reshape(size_x, size_y, 128)
    p = loc[(FIELDS - 2) * size_x : (FIELDS - 1) * size_x]
    q = loc[(FIELDS - 1) * size_x : FIELDS * size_x]
    for i in range(2):
        ys = slice(8 * i, 8 * i + 8)
        p_out[:, ys, :] = 2.0 * p_next[i][mid] - p[:, ys] + inner[:, ys] + p_last[i]
        q_out[:, ys, :] = 2.0 * q_next[i][mid] - q[:, ys] + q_last[i]


def finish_kernel(own, other, grad_e, grad_d):
    total = [own[i] + other[i] for i in range(3)]
    scale = 1.0 / jnp.sqrt(total[2] + 1.0)
    grad_e[...] = total[0] * scale
    grad_d[...] = total[1] * scale


def swap(part, axis, start):
    lows = range(start, lax.axis_size(axis) - 1, 2)
    return lax.ppermute(part, axis, [(i, i + 1) for i in lows] + [(i + 1, i) for i in lows])


def body(
    p_adjoint,
    q_adjoint,
    p_previous,
    q_previous,
    forward_p,
    courant,
    epsilon,
    delta_field,
    tilt_angle,
    azimuth,
    receiver_cells,
    receiver_values,
    boundary_cells,
    boundary_force,
    source_cells,
):
    _, size_x, size_y, size_z = p_adjoint.shape
    grid_y = size_y * lax.axis_size("gy")
    p, q, p_old, q_old, f = (
        entry[0] for entry in (p_adjoint, q_adjoint, p_previous, q_previous, forward_p)
    )
    message = WIDE * size_x + NARROW * 2
    inputs = (p, q, p_old, q_old, f, courant, epsilon, delta_field, tilt_angle, azimuth)
    loc, far, near = call(
        prepare_kernel,
        [(FIELDS * size_x, size_y, size_z)] + [(message, size_y, size_z)] * 2,
        inputs,
        scratch=[pltpu.VMEM(entry.shape, entry.dtype) for entry in inputs]
        + [pltpu.SemaphoreType.DMA((len(inputs),))],
        space=pltpu.HBM,
    )
    far = swap(far, "gx", 1)
    near = swap(near, "gx", 0)
    rows = (size_x + 4) * 24 + size_x * size_y
    (inject,) = call(
        functools.partial(inject_kernel, grid_y, size_z, size_x, size_y),
        [(rows, size_z)],
        (receiver_cells, receiver_values[0], boundary_cells[None], boundary_force[0]),
        flops=800_000_000,
    )
    edges = (loc, far, near)
    early = (WIDE + 2) * (size_x + 4) // 4
    late = WIDE * (size_x + 8) // 2 + 5 * (size_x + 4) // 4
    odds, evens = call(early_kernel, [(early, 8, size_z)] * 2, edges)
    odds, evens = swap(odds, "gy", 1), swap(evens, "gy", 0)
    late_odds, late_evens = call(late_kernel, [(late, 8, size_z)] * 2, edges)
    (grads,) = call(
        functools.partial(first_step_kernel, grid_y),
        [(3, size_x, size_y, size_z)],
        (source_cells, *edges, evens, odds, inject),
        smem=(0,),
    )
    grads, late_odds, late_evens = lax.optimization_barrier((grads, late_odds, late_evens))
    shots = range(lax.axis_size("shot"))
    grads = grads + lax.ppermute(grads, "shot", [(i, i ^ 1) for i in shots])
    late_odds, late_evens = swap(late_odds, "gy", 1), swap(late_evens, "gy", 0)
    other = lax.ppermute(grads, "shot", [(i, i ^ 3) for i in shots])
    p_final, q_final = call(
        second_step_kernel,
        [(size_x, size_y, size_z)] * 2,
        (*edges, late_evens, late_odds, inject),
        flops=20_000_000,
    )
    grad_e, grad_d = call(finish_kernel, [(size_x, size_y, size_z)] * 2, (grads, other))
    return (p_final[None], q_final[None], grad_e, grad_d)


def solution(mesh):
    in_specs = (
        P("shot", "gx", "gy", None),
        P("shot", "gx", "gy", None),
        P("shot", "gx", "gy", None),
        P("shot", "gx", "gy", None),
        P("shot", None, "gx", "gy", None),
        P("gx", "gy", None),
        P("gx", "gy", None),
        P("gx", "gy", None),
        P("gx", "gy", None),
        P("gx", "gy", None),
        P("shot", None),
        P("shot", None, None),
        P(),
        P("shot", None, None),
        P("shot"),
    )
    out_specs = (
        P("shot", "gx", "gy", None),
        P("shot", "gx", "gy", None),
        P("gx", "gy", None),
        P("gx", "gy", None),
    )
    return jax.shard_map(body, mesh=mesh, in_specs=in_specs, out_specs=out_specs, check_vma=False)
```

```python
import functools

import jax
import jax.numpy as jnp
from jax import lax
from jax.experimental import pallas as pl
from jax.experimental.pallas import tpu as pltpu
from jax.sharding import PartitionSpec as P

TAPER = 32
WIDE = 5
NARROW = 7
FIELDS = WIDE + NARROW + 2
INPUTS = ("p", "q", "p_old", "q_old", "f", "c", "eps", "delta", "tilt", "azimuth")
PAIRS = ((0, 0), (1, 1), (2, 2), (0, 1), (0, 2), (1, 2))


def call(kernel, outs, args, scratch=(), smem=(), flops=2_000_000, space=pltpu.VMEM):
    specs = [
        pl.BlockSpec(memory_space=pltpu.SMEM if i in smem else space) for i in range(len(args))
    ]
    shapes = [jax.ShapeDtypeStruct(shape, jnp.float32) for shape in outs]
    return pl.pallas_call(
        kernel,
        out_shape=shapes,
        in_specs=specs,
        out_specs=[pl.BlockSpec(memory_space=pltpu.VMEM)] * len(outs),
        scratch_shapes=list(scratch),
        compiler_params=pltpu.CompilerParams(vmem_limit_bytes=24 * 1024 * 1024),
        cost_estimate=pl.CostEstimate(flops=flops, bytes_accessed=2_000_000, transcendentals=0),
    )(*(pltpu.with_memory_space_constraint(x, space) if space == pltpu.HBM else x for x in args))


def row_mask(shape, below):
    return lax.broadcasted_iota(jnp.int32, shape, len(shape) - 2) < below


def shift_y(tiles, step, keep=3):
    if step > 0:
        rolled = [pltpu.roll(tile, 8 - step, 1) for tile in tiles]
        mask = row_mask(tiles[0].shape, 8 - step)
        return [jnp.where(mask, rolled[i], rolled[(i + 1) % 3]) for i in range(keep)]
    rolled = [pltpu.roll(tile, -step, 1) for tile in tiles]
    mask = row_mask(tiles[0].shape, -step)
    return [jnp.where(mask, rolled[(i + 2) % 3], rolled[i]) for i in range(keep)]


def shift_z(tile, step):
    lane = lax.broadcasted_iota(jnp.int32, tile.shape, 2)
    rolled = pltpu.roll(tile, (-step) % 128, 2)
    inside = lane < 128 - step if step > 0 else lane >= -step
    return jnp.where(inside, rolled, 0.0)


def second(far_low, low, here, high, far_high):
    return (4.0 / 3.0) * (low + high) - (1.0 / 12.0) * (far_low + far_high) - 2.5 * here


def first(far_low, low, high, far_high):
    return (2.0 / 3.0) * (high - low) - (1.0 / 12.0) * (far_high - far_low)


def second_x(tile, count):
    return second(*[tile[i : i + count] for i in range(5)])


def first_x(tile, count):
    return first(*[tile[i : i + count] for i in (0, 1, 3, 4)])


def first_y(tiles, keep):
    low2, low1, high1, high2 = [shift_y(tiles, step, keep) for step in (-2, -1, 1, 2)]
    return [first(low2[i], low1[i], high1[i], high2[i]) for i in range(keep)]


def both(parts_second, parts_first):
    near_even = (4.0 / 3.0) * parts_second
    near_odd = (2.0 / 3.0) * parts_first
    far_even = (-1.0 / 12.0) * parts_second
    far_odd = (1.0 / 12.0) * parts_first
    return (far_even + far_odd, near_even - near_odd, near_even + near_odd, far_even - far_odd)


def adjoint(products, source, count, keep, plus):
    mid = slice(2, 2 + count)
    aa = []
    for axis in range(3):
        scaled = [products[axis][i] * source[i] for i in range(3)]
        aa.append(scaled if plus else [source[i] - scaled[i] for i in range(3)])
    factor = 2.0 if plus else -2.0
    doubled = [factor * tile for tile in source]
    n01 = [products[3][i] * doubled[i] for i in range(3)]
    n02 = [products[4][i] * doubled[i] for i in range(keep)]
    n12 = [products[5][i][mid] * doubled[i][mid] for i in range(3)]
    out = [second_x(aa[0][i], count) for i in range(keep)]
    second_y = [tile[mid] for tile in aa[1]]
    cross_y = [first_x(tile, count) for tile in n01]
    mixed = [both(second_y[i], cross_y[i]) for i in range(3)]
    out = [out[i] - 2.5 * second_y[i] for i in range(keep)]
    for number, step in enumerate((-2, -1, 1, 2)):
        moved = shift_y([mixed[i][number] for i in range(3)], step, keep)
        out = [out[i] + moved[i] for i in range(keep)]
    along_y = first_y(n12, keep)
    for i in range(keep):
        second_z = aa[2][i][mid]
        cross_z = first_x(n02[i], count) + along_y[i]
        terms = both(second_z, cross_z)
        out[i] = out[i] - 2.5 * second_z
        for number, step in enumerate((-2, -1, 1, 2)):
            out[i] = out[i] + shift_z(terms[number], step)
    return out


def forward_image(products, field, count):
    mid = slice(2, 2 + count)
    inner = [tile[mid] for tile in field]
    slope_x = [first_x(tile, count) for tile in field]
    moved = [shift_y(inner, step, 2) for step in (-2, -1, 1, 2)]
    cross = first_y(slope_x, 2)
    out = []
    for i in range(2):
        here = inner[i]
        along = [moved[k][i] for k in range(4)]
        curve_x = second_x(field[i], count)
        curve_y = second(along[0], along[1], here, along[2], along[3])
        slope_y = first(*along)
        depth = [shift_z(here, step) for step in (-2, -1, 1, 2)]
        curve_z = second(depth[0], depth[1], here, depth[2], depth[3])
        total = (1.0 - products[0][i]) * curve_x
        total = total + (1.0 - products[1][i]) * curve_y
        total = total + (1.0 - products[2][i]) * curve_z
        cross_z = []
        for slope in (slope_x[i], slope_y):
            cross_z.append(first(*[shift_z(slope, step) for step in (-2, -1, 1, 2)]))
        mixed = products[3][i] * cross[i] + products[4][i] * cross_z[0] + products[5][i] * cross_z[1]
        out.append(total - 2.0 * mixed)
    return out


def prepare_kernel(*refs):
    count = len(INPUTS)
    arrays, (loc, far, near), held, arrived = refs[:count], refs[count : count + 3], refs[-count - 1 : -1], refs[-1]
    copies = [pltpu.make_async_copy(arrays[i], held[i], arrived.at[i]) for i in range(count)]
    for copy in copies:
        copy.start()
    for copy in copies:
        copy.wait()
    p, q, p_old, q_old, f, c, eps, delta, tilt, azimuth = held
    size_x = p.shape[0]
    p_now, q_now, speed = p[...], q[...], c[...]
    p_weight = speed * (1.0 + 2.0 * eps[...])
    q_weight = speed * (1.0 + 2.0 * delta[...])
    sine = jnp.sin(tilt[...])
    wide = (
        p_weight * p_now + q_weight * q_now,
        speed * (p_now + q_now),
        sine * jnp.cos(azimuth[...]),
        sine * jnp.sin(azimuth[...]),
        jnp.cos(tilt[...]),
    )
    narrow = (
        2.0 * p_now - p_old[...],
        2.0 * q_now - q_old[...],
        p_weight,
        q_weight,
        speed,
        f[0],
        f[1],
    )
    for number, cells in enumerate(wide):
        rows = slice(number * size_x, (number + 1) * size_x)
        loc[rows] = cells
        near[rows] = cells
        far[rows] = cells
    for number, cells in enumerate(narrow + (p_now, q_now)):
        start = (WIDE + number) * size_x
        loc[start : start + size_x] = cells
    odd = lax.rem(lax.axis_index("gx"), 2)
    upper, lower = (1 - odd) * (size_x - 2), odd * (size_x - 2)
    for number in range(NARROW):
        start = (WIDE + number) * size_x
        begin = WIDE * size_x + 2 * number
        near[begin : begin + 2] = loc[pl.ds(start + upper, 2)]
        far[begin : begin + 2] = loc[pl.ds(start + lower, 2)]


def tiles_of(loc, near, far, size_x, part):
    ys = slice(8 * part, 8 * part + 8)
    odd = lax.rem(lax.axis_index("gx"), 2) == 1
    first, second = near[:, ys, :], far[:, ys, :]
    below, above = jnp.where(odd, first, second), jnp.where(odd, second, first)
    wide, narrow = [], []
    for number in range(WIDE):
        rows = slice(number * size_x, (number + 1) * size_x)
        wide += [below[rows], loc[rows, ys, :], above[rows]]
    for number in range(NARROW):
        start = (WIDE + number) * size_x
        begin = WIDE * size_x + 2 * number
        narrow += [
            below[begin : begin + 2],
            loc[start : start + size_x, ys, :],
            above[begin : begin + 2],
        ]
    return jnp.concatenate(wide, axis=0), jnp.concatenate(narrow, axis=0)


def pack_kernel(loc, far, near, odds, evens):
    size_x = loc.shape[0] // FIELDS
    made = []
    for part in range(2):
        wide, narrow = tiles_of(loc, near, far, size_x, part)
        half = wide.shape[0] // 2
        quarter = narrow.shape[0] // 4
        turned = pltpu.roll(wide, 4, 1)
        mask = row_mask((half, 8, 128), 4)
        if part == 0:
            top = jnp.where(mask, wide[:half], turned[half:])
        else:
            top = jnp.where(mask, turned[:half], wide[half:])
        out = None
        for group in range(4):
            rows = narrow[group * quarter : (group + 1) * quarter]
            turn = (2 * group - 6 * part) % 8
            rows = pltpu.roll(rows, turn, 1) if turn else rows
            out = rows if out is None else jnp.where(row_mask(rows.shape, 2 * group), out, rows)
        made.append((top, out))
    odd = lax.rem(lax.axis_index("gy"), 2) == 1
    down, up = made
    for rows, a, b in ((slice(0, half), down[0], up[0]), (slice(half, half + quarter), down[1], up[1])):
        evens[rows] = jnp.where(odd, a, b)
        odds[rows] = jnp.where(odd, b, a)


def unpack(loc, near, far, evens, odds):
    size_x = loc.shape[0] // FIELDS
    odd = lax.rem(lax.axis_index("gy"), 2) == 1
    from_above = jnp.where(odd, odds[...], evens[...])
    from_below = jnp.where(odd, evens[...], odds[...])
    wide_rows, narrow_rows = 3 * size_x, size_x + 4
    half = WIDE * wide_rows // 2
    quarter = NARROW * narrow_rows // 4
    mask = row_mask((half, 8, 128), 4)
    high, low = from_above[0:half], from_below[0:half]
    wide_edge = jnp.concatenate(
        [jnp.where(mask, high, pltpu.roll(low, 4, 1)), jnp.where(mask, pltpu.roll(high, 4, 1), low)],
        axis=0,
    )
    high, low = from_above[half : half + quarter], from_below[half : half + quarter]
    mask = row_mask((quarter, 8, 128), 4)
    edges = []
    for group in range(4):
        first_turn, second_turn = (-2 * group) % 8, (6 - 2 * group) % 8
        upper = pltpu.roll(high, first_turn, 1) if first_turn else high
        lower = pltpu.roll(low, second_turn, 1) if second_turn else low
        edges.append(jnp.where(mask, upper, lower))
    narrow_edge = jnp.concatenate(edges, axis=0)
    wide0, narrow0 = tiles_of(loc, near, far, size_x, 0)
    wide1, narrow1 = tiles_of(loc, near, far, size_x, 1)
    wide = [
        [t[n * wide_rows : (n + 1) * wide_rows] for t in (wide0, wide1, wide_edge)] for n in range(WIDE)
    ]
    narrow = [
        [t[n * narrow_rows : (n + 1) * narrow_rows] for t in (narrow0, narrow1, narrow_edge)]
        for n in range(NARROW)
    ]
    return wide, narrow


def inject_kernel(grid_y, grid_z, size_x, size_y, recv_cells, recv_values, bound_cells, bound_force, out):
    bits_y, bits_z = grid_y.bit_length() - 1, grid_z.bit_length() - 1
    start_x = lax.axis_index("gx") * size_x
    start_y = lax.axis_index("gy") * size_y
    ring = (size_x + 4) * 24
    inner = size_x * size_y
    chunk = 512
    total = jnp.zeros((3 * (ring + inner), grid_z), jnp.float32)
    for cells_ref, values_ref, shift in ((recv_cells, recv_values, 0), (bound_cells, bound_force, bits_z)):
        for begin in range(0, cells_ref.shape[-1], chunk):
            cells = cells_ref[0:1, begin : begin + chunk]
            across = cells >> shift
            depth = cells & (grid_z - 1) if shift else jnp.zeros_like(cells)
            cell_x = (across >> bits_y) - start_x
            cell_y = (across & (grid_y - 1)) - start_y
            near = (cell_x >= -2) & (cell_x < size_x + 2) & (cell_y >= -2) & (cell_y < size_y + 2)
            wrapped = jnp.where(cell_y < 0, cell_y + 24, cell_y)
            ring_row = jnp.where(near, (cell_x + 2) * 24 + wrapped, -1)
            inside = (cell_x >= 0) & (cell_x < size_x) & (cell_y >= 0) & (cell_y < size_y)
            inner_row = jnp.where(inside, cell_x * size_y + cell_y, -1)
            ring_hit = lax.broadcasted_iota(jnp.int32, (ring, chunk), 0) == ring_row
            inner_hit = lax.broadcasted_iota(jnp.int32, (inner, chunk), 0) == inner_row
            columns = lax.broadcasted_iota(jnp.int32, (grid_z, chunk), 0) == depth
            columns = jnp.where(columns, 1.0, 0.0).astype(jnp.bfloat16)
            pieces = []
            parts = []
            for step in range(2):
                value = values_ref[step : step + 1, begin : begin + chunk]
                split = []
                for _ in range(3):
                    top = value.astype(jnp.bfloat16).astype(jnp.float32)
                    split.append(top)
                    value = value - top
                parts.append(split)
            for number in range(3):
                pieces.append(jnp.where(ring_hit, parts[0][number], 0.0).astype(jnp.bfloat16))
                pieces.append(jnp.where(inner_hit, parts[1][number], 0.0).astype(jnp.bfloat16))
            total = total + lax.dot_general(
                jnp.concatenate(pieces, axis=0),
                columns,
                (((1,), (1,)), ((), ())),
                preferred_element_type=jnp.float32,
            )
    rows = ring + inner
    out[...] = total[0:rows] + total[rows : 2 * rows] + total[2 * rows : 3 * rows]


def first_step_kernel(
    grid_y, source, loc, far_x, near_x, odds, evens, inject, grads, now, ahead, weights
):
    size_x, size_y = loc.shape[0] // FIELDS, loc.shape[1]
    wide, narrow = unpack(loc, near_x, far_x, evens, odds)
    p = loc[(FIELDS - 2) * size_x : (FIELDS - 1) * size_x]
    q = loc[(FIELDS - 1) * size_x : FIELDS * size_x]
    source_tiles, mix_tiles = wide[0], wide[1]
    products = [[wide[2 + a][i] * wide[2 + b][i] for i in range(3)] for a, b in PAIRS]
    p_base, q_base, p_weight, q_weight, speed, f0, f1 = narrow
    count = size_x + 4
    mid = slice(2, 2 + size_x)
    p_next = adjoint(products, source_tiles, count, 3, False)
    q_next = adjoint(products, mix_tiles, count, 3, True)
    ring = inject[0 : count * 24].reshape(count, 24, 128)
    p_next = [p_base[i] + p_next[i] + ring[:, 8 * i : 8 * i + 8] for i in range(3)]
    q_next = [q_base[i] + q_next[i] for i in range(3)]
    near = [[tile[2 : 2 + count] for tile in entry] for entry in products]
    inner = [[tile[mid] for tile in entry] for entry in near]
    bits_y = grid_y.bit_length() - 1
    source_x = (source[0] >> bits_y) - lax.axis_index("gx") * size_x
    source_y = (source[0] & (grid_y - 1)) - lax.axis_index("gy") * size_y
    images = [forward_image(inner, field, size_x) for field in (f0, f1)]
    shape = (size_x, 8, 128)
    offset_x = lax.broadcasted_iota(jnp.int32, shape, 0) - source_x
    for i in range(2):
        ys = slice(8 * i, 8 * i + 8)
        offset_y = lax.broadcasted_iota(jnp.int32, shape, 1) + (8 * i - source_y)
        squared = (offset_x * offset_x + offset_y * offset_y).astype(jnp.float32)
        taper = jnp.minimum(squared * (1.0 / float(TAPER * TAPER)), 1.0)
        scale = taper * (2.0 * speed[i][mid])
        image0, image1 = scale * images[0][i], scale * images[1][i]
        p_mid, q_mid = p_next[i][mid], q_next[i][mid]
        grads[0, :, ys, :] = p[:, ys, :] * image0 + p_mid * image1
        grads[1, :, ys, :] = q[:, ys, :] * image0 + q_mid * image1
        g0, g1 = f0[i][mid], f1[i][mid]
        grads[2, :, ys, :] = g0 * g0 + g1 * g1
        now[0, :, ys, :] = p_mid
        now[1, :, ys, :] = q_mid
    for i in range(3):
        ahead[0, i] = p_weight[i] * p_next[i] + q_weight[i] * q_next[i]
        ahead[1, i] = speed[i] * (p_next[i] + q_next[i])
        for number in range(6):
            weights[number, i] = near[number][i]


def second_step_kernel(now, ahead, weights, inject, loc, p_out, q_out):
    size_x, size_y = p_out.shape[0], p_out.shape[1]
    p = loc[(FIELDS - 2) * size_x : (FIELDS - 1) * size_x]
    q = loc[(FIELDS - 1) * size_x : FIELDS * size_x]
    products = [[weights[number, i] for i in range(3)] for number in range(6)]
    p_next = adjoint(products, [ahead[0, i] for i in range(3)], size_x, 2, False)
    q_next = adjoint(products, [ahead[1, i] for i in range(3)], size_x, 2, True)
    inner = inject[inject.shape[0] - size_x * size_y :].reshape(size_x, size_y, 128)
    for i in range(2):
        ys = slice(8 * i, 8 * i + 8)
        p_out[:, ys, :] = 2.0 * now[0, :, ys, :] - p[:, ys, :] + inner[:, ys] + p_next[i]
        q_out[:, ys, :] = 2.0 * now[1, :, ys, :] - q[:, ys, :] + q_next[i]


def swap(part, axis, start):
    lows = range(start, lax.axis_size(axis) - 1, 2)
    return lax.ppermute(part, axis, [(i, i + 1) for i in lows] + [(i + 1, i) for i in lows])


def finish_kernel(own, other, grad_e, grad_d):
    total = [own[i] + other[i] for i in range(3)]
    scale = 1.0 / jnp.sqrt(total[2] + 1.0)
    grad_e[...] = total[0] * scale
    grad_d[...] = total[1] * scale


def body(
    p_adjoint,
    q_adjoint,
    p_previous,
    q_previous,
    forward_p,
    courant,
    epsilon,
    delta_field,
    tilt_angle,
    azimuth,
    receiver_cells,
    receiver_values,
    boundary_cells,
    boundary_force,
    source_cells,
):
    _, size_x, size_y, size_z = p_adjoint.shape
    grid_y = size_y * lax.axis_size("gy")
    p, q, p_old, q_old, f = (
        entry[0] for entry in (p_adjoint, q_adjoint, p_previous, q_previous, forward_p)
    )
    message = WIDE * size_x + NARROW * 2
    inputs = (p, q, p_old, q_old, f, courant, epsilon, delta_field, tilt_angle, azimuth)
    loc, far, near = call(
        prepare_kernel,
        [(FIELDS * size_x, size_y, size_z)] + [(message, size_y, size_z)] * 2,
        inputs,
        scratch=[pltpu.VMEM(entry.shape, entry.dtype) for entry in inputs]
        + [pltpu.SemaphoreType.DMA((len(inputs),))],
        space=pltpu.HBM,
    )
    far = swap(far, "gx", 1)
    near = swap(near, "gx", 0)
    rows = (size_x + 4) * 24 + size_x * size_y
    (inject,) = call(
        functools.partial(inject_kernel, grid_y, size_z, size_x, size_y),
        [(rows, size_z)],
        (receiver_cells, receiver_values[0], boundary_cells[None], boundary_force[0]),
        flops=800_000_000,
    )
    tiles = WIDE * 3 * size_x // 2 + NARROW * (size_x + 4) // 4
    odds, evens = call(pack_kernel, [(tiles, 8, size_z)] * 2, (loc, far, near))
    odds = swap(odds, "gy", 1)
    evens = swap(evens, "gy", 0)
    count = size_x + 4
    grads, now, ahead, weights = call(
        functools.partial(first_step_kernel, grid_y),
        [
            (3, size_x, size_y, size_z),
            (2, size_x, size_y, size_z),
            (2, 3, count, 8, size_z),
            (6, 3, count, 8, size_z),
        ],
        (source_cells, loc, far, near, odds, evens, inject),
        smem=(0,),
    )
    shots = range(lax.axis_size("shot"))
    grads = grads + lax.ppermute(grads, "shot", [(i, i ^ 1) for i in shots])
    other = lax.ppermute(grads, "shot", [(i, i ^ 3) for i in shots])
    p_final, q_final = call(
        second_step_kernel, [(size_x, size_y, size_z)] * 2, (now, ahead, weights, inject, loc)
    )
    grad_e, grad_d = call(finish_kernel, [(size_x, size_y, size_z)] * 2, (grads, other))
    return (p_final[None], q_final[None], grad_e, grad_d)


def solution(mesh):
    in_specs = (
        P("shot", "gx", "gy", None),
        P("shot", "gx", "gy", None),
        P("shot", "gx", "gy", None),
        P("shot", "gx", "gy", None),
        P("shot", None, "gx", "gy", None),
        P("gx", "gy", None),
        P("gx", "gy", None),
        P("gx", "gy", None),
        P("gx", "gy", None),
        P("gx", "gy", None),
        P("shot", None),
        P("shot", None, None),
        P(),
        P("shot", None, None),
        P("shot"),
    )
    out_specs = (
        P("shot", "gx", "gy", None),
        P("shot", "gx", "gy", None),
        P("gx", "gy", None),
        P("gx", "gy", None),
    )
    return jax.shard_map(body, mesh=mesh, in_specs=in_specs, out_specs=out_specs, check_vma=False)
```

```python
import functools

import jax
import jax.numpy as jnp
from jax import lax
from jax.experimental import pallas as pl
from jax.experimental.pallas import tpu as pltpu
from jax.sharding import PartitionSpec as P

TAPER = 32
WIDE = 4
NARROW = 7
FIELDS = WIDE + NARROW + 2
INPUTS = ("p", "q", "p_old", "q_old", "f", "c", "eps", "delta", "tilt", "azimuth")
PAIRS = ((0, 0), (1, 1), (2, 2), (0, 1), (0, 2), (1, 2))


def call(kernel, outs, args, scratch=(), smem=(), flops=2_000_000, space=pltpu.VMEM):
    specs = [
        pl.BlockSpec(memory_space=pltpu.SMEM if i in smem else space) for i in range(len(args))
    ]
    shapes = [jax.ShapeDtypeStruct(shape, jnp.float32) for shape in outs]
    return pl.pallas_call(
        kernel,
        out_shape=shapes,
        in_specs=specs,
        out_specs=[pl.BlockSpec(memory_space=pltpu.VMEM)] * len(outs),
        scratch_shapes=list(scratch),
        compiler_params=pltpu.CompilerParams(vmem_limit_bytes=24 * 1024 * 1024),
        cost_estimate=pl.CostEstimate(flops=flops, bytes_accessed=2_000_000, transcendentals=0),
    )(*(pltpu.with_memory_space_constraint(x, space) if space == pltpu.HBM else x for x in args))


def row_mask(shape, below):
    return lax.broadcasted_iota(jnp.int32, shape, len(shape) - 2) < below


def shift_y(tiles, step, keep=3):
    if step > 0:
        rolled = [pltpu.roll(tile, 8 - step, 1) for tile in tiles]
        mask = row_mask(tiles[0].shape, 8 - step)
        return [jnp.where(mask, rolled[i], rolled[(i + 1) % 3]) for i in range(keep)]
    rolled = [pltpu.roll(tile, -step, 1) for tile in tiles]
    mask = row_mask(tiles[0].shape, -step)
    return [jnp.where(mask, rolled[(i + 2) % 3], rolled[i]) for i in range(keep)]


def shift_z(tile, step):
    lane = lax.broadcasted_iota(jnp.int32, tile.shape, 2)
    rolled = pltpu.roll(tile, (-step) % 128, 2)
    inside = lane < 128 - step if step > 0 else lane >= -step
    return jnp.where(inside, rolled, 0.0)


def second(far_low, low, here, high, far_high):
    return (4.0 / 3.0) * (low + high) - (1.0 / 12.0) * (far_low + far_high) - 2.5 * here


def first(far_low, low, high, far_high):
    return (2.0 / 3.0) * (high - low) - (1.0 / 12.0) * (far_high - far_low)


def second_x(tile, count):
    return second(*[tile[i : i + count] for i in range(5)])


def first_x(tile, count):
    return first(*[tile[i : i + count] for i in (0, 1, 3, 4)])


def first_y(tiles, keep):
    low2, low1, high1, high2 = [shift_y(tiles, step, keep) for step in (-2, -1, 1, 2)]
    return [first(low2[i], low1[i], high1[i], high2[i]) for i in range(keep)]


def both(parts_second, parts_first):
    near_even = (4.0 / 3.0) * parts_second
    near_odd = (2.0 / 3.0) * parts_first
    far_even = (-1.0 / 12.0) * parts_second
    far_odd = (1.0 / 12.0) * parts_first
    return (far_even + far_odd, near_even - near_odd, near_even + near_odd, far_even - far_odd)


def adjoint(products, source, count, keep, plus):
    mid = slice(2, 2 + count)
    aa = []
    for axis in range(3):
        scaled = [products[axis][i] * source[i] for i in range(3)]
        aa.append(scaled if plus else [source[i] - scaled[i] for i in range(3)])
    factor = 2.0 if plus else -2.0
    doubled = [factor * tile for tile in source]
    n01 = [products[3][i] * doubled[i] for i in range(3)]
    n02 = [products[4][i] * doubled[i] for i in range(keep)]
    n12 = [products[5][i][mid] * doubled[i][mid] for i in range(3)]
    out = [second_x(aa[0][i], count) for i in range(keep)]
    second_y = [tile[mid] for tile in aa[1]]
    cross_y = [first_x(tile, count) for tile in n01]
    mixed = [both(second_y[i], cross_y[i]) for i in range(3)]
    out = [out[i] - 2.5 * second_y[i] for i in range(keep)]
    for number, step in enumerate((-2, -1, 1, 2)):
        moved = shift_y([mixed[i][number] for i in range(3)], step, keep)
        out = [out[i] + moved[i] for i in range(keep)]
    along_y = first_y(n12, keep)
    for i in range(keep):
        second_z = aa[2][i][mid]
        cross_z = first_x(n02[i], count) + along_y[i]
        terms = both(second_z, cross_z)
        out[i] = out[i] - 2.5 * second_z
        for number, step in enumerate((-2, -1, 1, 2)):
            out[i] = out[i] + shift_z(terms[number], step)
    return out


def forward_image(products, field, count):
    mid = slice(2, 2 + count)
    inner = [tile[mid] for tile in field]
    slope_x = [first_x(tile, count) for tile in field]
    moved = [shift_y(inner, step, 2) for step in (-2, -1, 1, 2)]
    cross = first_y(slope_x, 2)
    out = []
    for i in range(2):
        here = inner[i]
        along = [moved[k][i] for k in range(4)]
        curve_x = second_x(field[i], count)
        curve_y = second(along[0], along[1], here, along[2], along[3])
        slope_y = first(*along)
        depth = [shift_z(here, step) for step in (-2, -1, 1, 2)]
        curve_z = second(depth[0], depth[1], here, depth[2], depth[3])
        total = (1.0 - products[0][i]) * curve_x
        total = total + (1.0 - products[1][i]) * curve_y
        total = total + (1.0 - products[2][i]) * curve_z
        cross_z = []
        for slope in (slope_x[i], slope_y):
            cross_z.append(first(*[shift_z(slope, step) for step in (-2, -1, 1, 2)]))
        mixed = products[3][i] * cross[i] + products[4][i] * cross_z[0] + products[5][i] * cross_z[1]
        out.append(total - 2.0 * mixed)
    return out


def prepare_kernel(*refs):
    count = len(INPUTS)
    arrays, (loc, far, near), held, arrived = refs[:count], refs[count : count + 3], refs[-count - 1 : -1], refs[-1]
    copies = [pltpu.make_async_copy(arrays[i], held[i], arrived.at[i]) for i in range(count)]
    for copy in copies:
        copy.start()
    for copy in copies:
        copy.wait()
    p, q, p_old, q_old, f, c, eps, delta, tilt, azimuth = held
    size_x = p.shape[0]
    p_now, q_now, speed = p[...], q[...], c[...]
    p_weight = speed * (1.0 + 2.0 * eps[...])
    q_weight = speed * (1.0 + 2.0 * delta[...])
    wide = (
        p_weight * p_now + q_weight * q_now,
        speed * (p_now + q_now),
        tilt[...],
        azimuth[...],
    )
    narrow = (
        2.0 * p_now - p_old[...],
        2.0 * q_now - q_old[...],
        p_weight,
        q_weight,
        speed,
        f[0],
        f[1],
    )
    for number, cells in enumerate(wide):
        rows = slice(number * size_x, (number + 1) * size_x)
        loc[rows] = cells
        near[rows] = cells
        far[rows] = cells
    for number, cells in enumerate(narrow + (p_now, q_now)):
        start = (WIDE + number) * size_x
        loc[start : start + size_x] = cells
    odd = lax.rem(lax.axis_index("gx"), 2)
    upper, lower = (1 - odd) * (size_x - 2), odd * (size_x - 2)
    for number in range(NARROW):
        start = (WIDE + number) * size_x
        begin = WIDE * size_x + 2 * number
        near[begin : begin + 2] = loc[pl.ds(start + upper, 2)]
        far[begin : begin + 2] = loc[pl.ds(start + lower, 2)]


def tiles_of(loc, near, far, size_x, part):
    ys = slice(8 * part, 8 * part + 8)
    odd = lax.rem(lax.axis_index("gx"), 2) == 1
    first, second = near[:, ys, :], far[:, ys, :]
    below, above = jnp.where(odd, first, second), jnp.where(odd, second, first)
    wide, narrow = [], []
    for number in range(WIDE):
        rows = slice(number * size_x, (number + 1) * size_x)
        wide.append(jnp.concatenate([below[rows], loc[rows, ys, :], above[rows]], axis=0))
    for number in range(NARROW):
        start = (WIDE + number) * size_x
        begin = WIDE * size_x + 2 * number
        rows = slice(begin, begin + 2)
        here = loc[start : start + size_x, ys, :]
        narrow.append(jnp.concatenate([below[rows], here, above[rows]], axis=0))
    return wide, narrow


def turn(rows, by):
    by = by % 8
    return pltpu.roll(rows, by, 1) if by else rows


def pack(rows, part, groups):
    height, count = 8 // groups, rows.shape[0] // groups
    out = None
    for group in range(groups):
        piece = turn(rows[group * count : (group + 1) * count], height * (group - part * (groups - 1)))
        mask = row_mask(piece.shape, height * group)
        out = piece if out is None else jnp.where(mask, out, piece)
    return out


def unpack(high, low, groups):
    height = 8 // groups
    edges = []
    for group in range(groups):
        upper = turn(high, -height * group)
        lower = turn(low, height * (groups - 1 - group))
        edges.append(jnp.where(row_mask(high.shape, 4), upper, lower))
    return jnp.concatenate(edges, axis=0)


def send_both(parts, evens, odds, start):
    odd = lax.rem(lax.axis_index("gy"), 2) == 1
    rows = slice(start, start + parts[0].shape[0])
    evens[rows] = jnp.where(odd, parts[0], parts[1])
    odds[rows] = jnp.where(odd, parts[1], parts[0])


def from_both(evens, odds):
    odd = lax.rem(lax.axis_index("gy"), 2) == 1
    return jnp.where(odd, odds[...], evens[...]), jnp.where(odd, evens[...], odds[...])


def pack_kernel(loc, far, near, odds, evens):
    size_x = loc.shape[0] // FIELDS
    wides, narrows = [], []
    for part in range(2):
        wide, narrow = tiles_of(loc, near, far, size_x, part)
        wides.append(pack(jnp.concatenate(wide, axis=0), part, 2))
        narrows.append(pack(jnp.concatenate(narrow, axis=0), part, 4))
    send_both(wides, evens, odds, 0)
    send_both(narrows, evens, odds, wides[0].shape[0])


def normal_of(tilt, azimuth):
    sine = jnp.sin(tilt)
    return sine * jnp.cos(azimuth), sine * jnp.sin(azimuth), jnp.cos(tilt)


def normal_kernel(loc, far, near, out):
    size_x = loc.shape[0] // FIELDS
    for part in range(2):
        wide, _ = tiles_of(loc, near, far, size_x, part)
        for axis, cells in enumerate(normal_of(wide[2], wide[3])):
            out[axis, part] = cells


def cut(rows, count):
    return [rows[i : i + count] for i in range(0, rows.shape[0], count)]


def inject_kernel(grid_y, grid_z, size_x, size_y, recv_cells, recv_values, bound_cells, bound_force, out):
    bits_y, bits_z = grid_y.bit_length() - 1, grid_z.bit_length() - 1
    start_x = lax.axis_index("gx") * size_x
    start_y = lax.axis_index("gy") * size_y
    ring = (size_x + 4) * 24
    inner = size_x * size_y
    chunk = 512
    total = jnp.zeros((3 * (ring + inner), grid_z), jnp.float32)
    for cells_ref, values_ref, shift in ((recv_cells, recv_values, 0), (bound_cells, bound_force, bits_z)):
        for begin in range(0, cells_ref.shape[-1], chunk):
            cells = cells_ref[0:1, begin : begin + chunk]
            across = cells >> shift
            depth = cells & (grid_z - 1) if shift else jnp.zeros_like(cells)
            cell_x = (across >> bits_y) - start_x
            cell_y = (across & (grid_y - 1)) - start_y
            near = (cell_x >= -2) & (cell_x < size_x + 2) & (cell_y >= -2) & (cell_y < size_y + 2)
            wrapped = jnp.where(cell_y < 0, cell_y + 24, cell_y)
            ring_row = jnp.where(near, (cell_x + 2) * 24 + wrapped, -1)
            inside = (cell_x >= 0) & (cell_x < size_x) & (cell_y >= 0) & (cell_y < size_y)
            inner_row = jnp.where(inside, cell_x * size_y + cell_y, -1)
            ring_hit = lax.broadcasted_iota(jnp.int32, (ring, chunk), 0) == ring_row
            inner_hit = lax.broadcasted_iota(jnp.int32, (inner, chunk), 0) == inner_row
            columns = lax.broadcasted_iota(jnp.int32, (grid_z, chunk), 0) == depth
            columns = jnp.where(columns, 1.0, 0.0).astype(jnp.bfloat16)
            pieces = []
            parts = []
            for step in range(2):
                value = values_ref[step : step + 1, begin : begin + chunk]
                split = []
                for _ in range(3):
                    top = value.astype(jnp.bfloat16).astype(jnp.float32)
                    split.append(top)
                    value = value - top
                parts.append(split)
            for number in range(3):
                pieces.append(jnp.where(ring_hit, parts[0][number], 0.0).astype(jnp.bfloat16))
                pieces.append(jnp.where(inner_hit, parts[1][number], 0.0).astype(jnp.bfloat16))
            total = total + lax.dot_general(
                jnp.concatenate(pieces, axis=0),
                columns,
                (((1,), (1,)), ((), ())),
                preferred_element_type=jnp.float32,
            )
    rows = ring + inner
    out[...] = total[0:rows] + total[rows : 2 * rows] + total[2 * rows : 3 * rows]


def fields_of(loc, far, near, odds, evens):
    size_x = loc.shape[0] // FIELDS
    high, low = from_both(evens, odds)
    half = WIDE * (size_x + 8) // 2
    wide_edge = cut(unpack(high[:half], low[:half], 2), size_x + 8)
    narrow_edge = cut(unpack(high[half:], low[half:], 4), size_x + 4)
    parts = [tiles_of(loc, near, far, size_x, part) for part in range(2)]
    wide = [[parts[0][0][n], parts[1][0][n], wide_edge[n]] for n in range(WIDE)]
    narrow = [[parts[0][1][n], parts[1][1][n], narrow_edge[n]] for n in range(NARROW)]
    return wide, narrow, wide_edge[2:4]


def first_step_kernel(grid_y, source, loc, far_x, near_x, odds, evens, normal, inject, grads, edge_normal):
    size_x, size_y = loc.shape[0] // FIELDS, loc.shape[1]
    count = size_x + 4
    wide, narrow, angles = fields_of(loc, far_x, near_x, odds, evens)
    fields = [[tile[2 : 2 + count] for tile in wide[n]] for n in range(2)]
    edge = normal_of(*angles)
    for axis in range(3):
        edge_normal[axis] = edge[axis]
    normals = [
        [normal[axis, 0, 2 : 2 + count], normal[axis, 1, 2 : 2 + count], edge[axis][2 : 2 + count]]
        for axis in range(3)
    ]
    products = [[normals[a][i] * normals[b][i] for i in range(3)] for a, b in PAIRS]
    mid = slice(2, 2 + size_x)
    p_next = adjoint(products, fields[0], size_x, 2, False)
    q_next = adjoint(products, fields[1], size_x, 2, True)
    inner = [[tile[mid] for tile in entry] for entry in products]
    images = [forward_image(inner, field, size_x) for field in narrow[5:7]]
    ring = inject[0 : count * 24].reshape(count, 24, 128)
    bits_y = grid_y.bit_length() - 1
    source_x = (source[0] >> bits_y) - lax.axis_index("gx") * size_x
    source_y = (source[0] & (grid_y - 1)) - lax.axis_index("gy") * size_y
    shape = (size_x, 8, 128)
    offset_x = lax.broadcasted_iota(jnp.int32, shape, 0) - source_x

    def block(field, ys):
        return loc[field * size_x : (field + 1) * size_x, ys, :]

    for i in range(2):
        ys = slice(8 * i, 8 * i + 8)
        offset_y = lax.broadcasted_iota(jnp.int32, shape, 1) + (8 * i - source_y)
        squared = (offset_x * offset_x + offset_y * offset_y).astype(jnp.float32)
        taper = jnp.minimum(squared * (1.0 / float(TAPER * TAPER)), 1.0)
        scale = taper * (2.0 * block(WIDE + 4, ys))
        image0, image1 = scale * images[0][i], scale * images[1][i]
        p_mid = block(WIDE, ys) + p_next[i] + ring[mid, ys, :]
        q_mid = block(WIDE + 1, ys) + q_next[i]
        grads[0, :, ys, :] = block(FIELDS - 2, ys) * image0 + p_mid * image1
        grads[1, :, ys, :] = block(FIELDS - 1, ys) * image0 + q_mid * image1
        f0, f1 = block(WIDE + 5, ys), block(WIDE + 6, ys)
        grads[2, :, ys, :] = f0 * f0 + f1 * f1


def second_step_kernel(loc, far_x, near_x, odds, evens, normal, edge_normal, inject, p_out, q_out):
    size_x, size_y = p_out.shape[0], p_out.shape[1]
    count = size_x + 4
    wide, narrow, _ = fields_of(loc, far_x, near_x, odds, evens)
    normals = [[normal[axis, 0], normal[axis, 1], edge_normal[axis]] for axis in range(3)]
    products = [[normals[a][i] * normals[b][i] for i in range(3)] for a, b in PAIRS]
    p_base, q_base, p_weight, q_weight, speed = narrow[:5]
    mid = slice(2, 2 + size_x)
    p_next = adjoint(products, wide[0], count, 3, False)
    q_next = adjoint(products, wide[1], count, 3, True)
    ring = inject[0 : count * 24].reshape(count, 24, 128)
    p_next = [p_base[i] + p_next[i] + ring[:, 8 * i : 8 * i + 8] for i in range(3)]
    q_next = [q_base[i] + q_next[i] for i in range(3)]
    source = [p_weight[i] * p_next[i] + q_weight[i] * q_next[i] for i in range(3)]
    mix = [speed[i] * (p_next[i] + q_next[i]) for i in range(3)]
    products = [[tile[2 : 2 + count] for tile in entry] for entry in products]
    p_last = adjoint(products, source, size_x, 2, False)
    q_last = adjoint(products, mix, size_x, 2, True)
    inner = inject[count * 24 :].reshape(size_x, size_y, 128)
    p = loc[(FIELDS - 2) * size_x : (FIELDS - 1) * size_x]
    q = loc[(FIELDS - 1) * size_x : FIELDS * size_x]
    for i in range(2):
        ys = slice(8 * i, 8 * i + 8)
        p_out[:, ys, :] = 2.0 * p_next[i][mid] - p[:, ys] + inner[:, ys] + p_last[i]
        q_out[:, ys, :] = 2.0 * q_next[i][mid] - q[:, ys] + q_last[i]


def finish_kernel(own, other, grad_e, grad_d):
    total = [own[i] + other[i] for i in range(3)]
    scale = 1.0 / jnp.sqrt(total[2] + 1.0)
    grad_e[...] = total[0] * scale
    grad_d[...] = total[1] * scale


def swap(part, axis, start):
    lows = range(start, lax.axis_size(axis) - 1, 2)
    return lax.ppermute(part, axis, [(i, i + 1) for i in lows] + [(i + 1, i) for i in lows])


def body(
    p_adjoint,
    q_adjoint,
    p_previous,
    q_previous,
    forward_p,
    courant,
    epsilon,
    delta_field,
    tilt_angle,
    azimuth,
    receiver_cells,
    receiver_values,
    boundary_cells,
    boundary_force,
    source_cells,
):
    _, size_x, size_y, size_z = p_adjoint.shape
    grid_y = size_y * lax.axis_size("gy")
    p, q, p_old, q_old, f = (
        entry[0] for entry in (p_adjoint, q_adjoint, p_previous, q_previous, forward_p)
    )
    message = WIDE * size_x + NARROW * 2
    inputs = (p, q, p_old, q_old, f, courant, epsilon, delta_field, tilt_angle, azimuth)
    loc, far, near = call(
        prepare_kernel,
        [(FIELDS * size_x, size_y, size_z)] + [(message, size_y, size_z)] * 2,
        inputs,
        scratch=[pltpu.VMEM(entry.shape, entry.dtype) for entry in inputs]
        + [pltpu.SemaphoreType.DMA((len(inputs),))],
        space=pltpu.HBM,
    )
    far = swap(far, "gx", 1)
    near = swap(near, "gx", 0)
    rows = (size_x + 4) * 24 + size_x * size_y
    (inject,) = call(
        functools.partial(inject_kernel, grid_y, size_z, size_x, size_y),
        [(rows, size_z)],
        (receiver_cells, receiver_values[0], boundary_cells[None], boundary_force[0]),
        flops=800_000_000,
    )
    edges = (loc, far, near)
    tiles = WIDE * (size_x + 8) // 2 + NARROW * (size_x + 4) // 4
    odds, evens = call(pack_kernel, [(tiles, 8, size_z)] * 2, edges)
    odds, evens = swap(odds, "gy", 1), swap(evens, "gy", 0)
    (normal,) = call(normal_kernel, [(3, 2, size_x + 8, 8, size_z)], edges)
    grads, edge_normal = call(
        functools.partial(first_step_kernel, grid_y),
        [(3, size_x, size_y, size_z), (3, size_x + 8, 8, size_z)],
        (source_cells, *edges, odds, evens, normal, inject),
        smem=(0,),
    )
    shots = range(lax.axis_size("shot"))
    grads = grads + lax.ppermute(grads, "shot", [(i, i ^ 1) for i in shots])
    other = lax.ppermute(grads, "shot", [(i, i ^ 3) for i in shots])
    p_final, q_final = call(
        second_step_kernel,
        [(size_x, size_y, size_z)] * 2,
        (*edges, odds, evens, normal, edge_normal, inject),
        flops=20_000_000,
    )
    grad_e, grad_d = call(finish_kernel, [(size_x, size_y, size_z)] * 2, (grads, other))
    return (p_final[None], q_final[None], grad_e, grad_d)


def solution(mesh):
    in_specs = (
        P("shot", "gx", "gy", None),
        P("shot", "gx", "gy", None),
        P("shot", "gx", "gy", None),
        P("shot", "gx", "gy", None),
        P("shot", None, "gx", "gy", None),
        P("gx", "gy", None),
        P("gx", "gy", None),
        P("gx", "gy", None),
        P("gx", "gy", None),
        P("gx", "gy", None),
        P("shot", None),
        P("shot", None, None),
        P(),
        P("shot", None, None),
        P("shot"),
    )
    out_specs = (
        P("shot", "gx", "gy", None),
        P("shot", "gx", "gy", None),
        P("gx", "gy", None),
        P("gx", "gy", None),
    )
    return jax.shard_map(body, mesh=mesh, in_specs=in_specs, out_specs=out_specs, check_vma=False)
```

```python
import functools

import jax
import jax.numpy as jnp
from jax import lax
from jax.experimental import pallas as pl
from jax.experimental.pallas import tpu as pltpu
from jax.sharding import PartitionSpec as P

TAPER = 32
WIDE = 4
NARROW = 7
FIELDS = WIDE + NARROW + 2
INPUTS = ("p", "q", "p_old", "q_old", "f", "c", "eps", "delta", "tilt", "azimuth")
PAIRS = ((0, 0), (1, 1), (2, 2), (0, 1), (0, 2), (1, 2))


def call(kernel, outs, args, scratch=(), smem=(), flops=2_000_000, space=pltpu.VMEM):
    specs = [
        pl.BlockSpec(memory_space=pltpu.SMEM if i in smem else space) for i in range(len(args))
    ]
    shapes = [jax.ShapeDtypeStruct(shape, jnp.float32) for shape in outs]
    return pl.pallas_call(
        kernel,
        out_shape=shapes,
        in_specs=specs,
        out_specs=[pl.BlockSpec(memory_space=pltpu.VMEM)] * len(outs),
        scratch_shapes=list(scratch),
        compiler_params=pltpu.CompilerParams(vmem_limit_bytes=24 * 1024 * 1024),
        cost_estimate=pl.CostEstimate(flops=flops, bytes_accessed=2_000_000, transcendentals=0),
    )(*(pltpu.with_memory_space_constraint(x, space) if space == pltpu.HBM else x for x in args))


def row_mask(shape, below):
    return lax.broadcasted_iota(jnp.int32, shape, len(shape) - 2) < below


def shift_y(tiles, step, keep=3):
    if step > 0:
        rolled = [pltpu.roll(tile, 8 - step, 1) for tile in tiles]
        mask = row_mask(tiles[0].shape, 8 - step)
        return [jnp.where(mask, rolled[i], rolled[(i + 1) % 3]) for i in range(keep)]
    rolled = [pltpu.roll(tile, -step, 1) for tile in tiles]
    mask = row_mask(tiles[0].shape, -step)
    return [jnp.where(mask, rolled[(i + 2) % 3], rolled[i]) for i in range(keep)]


def shift_z(tile, step):
    lane = lax.broadcasted_iota(jnp.int32, tile.shape, 2)
    rolled = pltpu.roll(tile, (-step) % 128, 2)
    inside = lane < 128 - step if step > 0 else lane >= -step
    return jnp.where(inside, rolled, 0.0)


def second(far_low, low, here, high, far_high):
    return (4.0 / 3.0) * (low + high) - (1.0 / 12.0) * (far_low + far_high) - 2.5 * here


def first(far_low, low, high, far_high):
    return (2.0 / 3.0) * (high - low) - (1.0 / 12.0) * (far_high - far_low)


def second_x(tile, count):
    return second(*[tile[i : i + count] for i in range(5)])


def first_x(tile, count):
    return first(*[tile[i : i + count] for i in (0, 1, 3, 4)])


def first_y(tiles, keep):
    low2, low1, high1, high2 = [shift_y(tiles, step, keep) for step in (-2, -1, 1, 2)]
    return [first(low2[i], low1[i], high1[i], high2[i]) for i in range(keep)]


def both(parts_second, parts_first):
    near_even = (4.0 / 3.0) * parts_second
    near_odd = (2.0 / 3.0) * parts_first
    far_even = (-1.0 / 12.0) * parts_second
    far_odd = (1.0 / 12.0) * parts_first
    return (far_even + far_odd, near_even - near_odd, near_even + near_odd, far_even - far_odd)


def adjoint(products, source, count, keep, plus):
    mid = slice(2, 2 + count)
    aa = []
    for axis in range(3):
        scaled = [products[axis][i] * source[i] for i in range(3)]
        aa.append(scaled if plus else [source[i] - scaled[i] for i in range(3)])
    factor = 2.0 if plus else -2.0
    doubled = [factor * tile for tile in source]
    n01 = [products[3][i] * doubled[i] for i in range(3)]
    n02 = [products[4][i] * doubled[i] for i in range(keep)]
    n12 = [products[5][i][mid] * doubled[i][mid] for i in range(3)]
    out = [second_x(aa[0][i], count) for i in range(keep)]
    second_y = [tile[mid] for tile in aa[1]]
    cross_y = [first_x(tile, count) for tile in n01]
    mixed = [both(second_y[i], cross_y[i]) for i in range(3)]
    out = [out[i] - 2.5 * second_y[i] for i in range(keep)]
    for number, step in enumerate((-2, -1, 1, 2)):
        moved = shift_y([mixed[i][number] for i in range(3)], step, keep)
        out = [out[i] + moved[i] for i in range(keep)]
    along_y = first_y(n12, keep)
    for i in range(keep):
        second_z = aa[2][i][mid]
        cross_z = first_x(n02[i], count) + along_y[i]
        terms = both(second_z, cross_z)
        out[i] = out[i] - 2.5 * second_z
        for number, step in enumerate((-2, -1, 1, 2)):
            out[i] = out[i] + shift_z(terms[number], step)
    return out


def forward_image(products, field, count):
    mid = slice(2, 2 + count)
    inner = [tile[mid] for tile in field]
    slope_x = [first_x(tile, count) for tile in field]
    moved = [shift_y(inner, step, 2) for step in (-2, -1, 1, 2)]
    cross = first_y(slope_x, 2)
    out = []
    for i in range(2):
        here = inner[i]
        along = [moved[k][i] for k in range(4)]
        curve_x = second_x(field[i], count)
        curve_y = second(along[0], along[1], here, along[2], along[3])
        slope_y = first(*along)
        depth = [shift_z(here, step) for step in (-2, -1, 1, 2)]
        curve_z = second(depth[0], depth[1], here, depth[2], depth[3])
        total = (1.0 - products[0][i]) * curve_x
        total = total + (1.0 - products[1][i]) * curve_y
        total = total + (1.0 - products[2][i]) * curve_z
        cross_z = []
        for slope in (slope_x[i], slope_y):
            cross_z.append(first(*[shift_z(slope, step) for step in (-2, -1, 1, 2)]))
        mixed = products[3][i] * cross[i] + products[4][i] * cross_z[0] + products[5][i] * cross_z[1]
        out.append(total - 2.0 * mixed)
    return out


def prepare_kernel(*refs):
    count = len(INPUTS)
    arrays, (loc, far, near), held, arrived = refs[:count], refs[count : count + 3], refs[-count - 1 : -1], refs[-1]
    copies = [pltpu.make_async_copy(arrays[i], held[i], arrived.at[i]) for i in range(count)]
    for copy in copies:
        copy.start()
    for copy in copies:
        copy.wait()
    p, q, p_old, q_old, f, c, eps, delta, tilt, azimuth = held
    size_x = p.shape[0]
    p_now, q_now, speed = p[...], q[...], c[...]
    p_weight = speed * (1.0 + 2.0 * eps[...])
    q_weight = speed * (1.0 + 2.0 * delta[...])
    wide = (
        p_weight * p_now + q_weight * q_now,
        speed * (p_now + q_now),
        tilt[...],
        azimuth[...],
    )
    narrow = (
        2.0 * p_now - p_old[...],
        2.0 * q_now - q_old[...],
        p_weight,
        q_weight,
        speed,
        f[0],
        f[1],
    )
    for number, cells in enumerate(wide):
        rows = slice(number * size_x, (number + 1) * size_x)
        loc[rows] = cells
        near[rows] = cells
        far[rows] = cells
    for number, cells in enumerate(narrow + (p_now, q_now)):
        start = (WIDE + number) * size_x
        loc[start : start + size_x] = cells
    odd = lax.rem(lax.axis_index("gx"), 2)
    upper, lower = (1 - odd) * (size_x - 2), odd * (size_x - 2)
    for number in range(NARROW):
        start = (WIDE + number) * size_x
        begin = WIDE * size_x + 2 * number
        near[begin : begin + 2] = loc[pl.ds(start + upper, 2)]
        far[begin : begin + 2] = loc[pl.ds(start + lower, 2)]


def tiles_of(loc, near, far, size_x, part):
    ys = slice(8 * part, 8 * part + 8)
    odd = lax.rem(lax.axis_index("gx"), 2) == 1
    first, second = near[:, ys, :], far[:, ys, :]
    below, above = jnp.where(odd, first, second), jnp.where(odd, second, first)
    wide, narrow = [], []
    for number in range(WIDE):
        rows = slice(number * size_x, (number + 1) * size_x)
        wide.append(jnp.concatenate([below[rows], loc[rows, ys, :], above[rows]], axis=0))
    for number in range(NARROW):
        start = (WIDE + number) * size_x
        begin = WIDE * size_x + 2 * number
        rows = slice(begin, begin + 2)
        here = loc[start : start + size_x, ys, :]
        narrow.append(jnp.concatenate([below[rows], here, above[rows]], axis=0))
    return wide, narrow


def turn(rows, by):
    by = by % 8
    return pltpu.roll(rows, by, 1) if by else rows


def pack(rows, part, groups):
    height, count = 8 // groups, rows.shape[0] // groups
    out = None
    for group in range(groups):
        piece = turn(rows[group * count : (group + 1) * count], height * (group - part * (groups - 1)))
        mask = row_mask(piece.shape, height * group)
        out = piece if out is None else jnp.where(mask, out, piece)
    return out


def unpack(high, low, groups):
    height = 8 // groups
    edges = []
    for group in range(groups):
        upper = turn(high, -height * group)
        lower = turn(low, height * (groups - 1 - group))
        edges.append(jnp.where(row_mask(high.shape, 4), upper, lower))
    return jnp.concatenate(edges, axis=0)


def send_both(parts, evens, odds, start):
    odd = lax.rem(lax.axis_index("gy"), 2) == 1
    rows = slice(start, start + parts[0].shape[0])
    evens[rows] = jnp.where(odd, parts[0], parts[1])
    odds[rows] = jnp.where(odd, parts[1], parts[0])


def from_both(evens, odds):
    odd = lax.rem(lax.axis_index("gy"), 2) == 1
    return jnp.where(odd, odds[...], evens[...]), jnp.where(odd, evens[...], odds[...])


def pack_kernel(loc, far, near, odds, evens):
    size_x = loc.shape[0] // FIELDS
    wides, narrows = [], []
    for part in range(2):
        wide, narrow = tiles_of(loc, near, far, size_x, part)
        wides.append(pack(jnp.concatenate(wide, axis=0), part, 2))
        narrows.append(pack(jnp.concatenate(narrow, axis=0), part, 4))
    send_both(wides, evens, odds, 0)
    send_both(narrows, evens, odds, wides[0].shape[0])


def normal_of(tilt, azimuth):
    sine = jnp.sin(tilt)
    return sine * jnp.cos(azimuth), sine * jnp.sin(azimuth), jnp.cos(tilt)


def normal_kernel(loc, far, near, out):
    size_x = loc.shape[0] // FIELDS
    for part in range(2):
        wide, _ = tiles_of(loc, near, far, size_x, part)
        for axis, cells in enumerate(normal_of(wide[2], wide[3])):
            out[axis, part] = cells


def cut(rows, count):
    return [rows[i : i + count] for i in range(0, rows.shape[0], count)]


def inject_kernel(grid_y, grid_z, size_x, size_y, recv_cells, recv_values, bound_cells, bound_force, out):
    bits_y, bits_z = grid_y.bit_length() - 1, grid_z.bit_length() - 1
    start_x = lax.axis_index("gx") * size_x
    start_y = lax.axis_index("gy") * size_y
    ring = (size_x + 4) * 24
    inner = size_x * size_y
    chunk = 512
    total = jnp.zeros((3 * (ring + inner), grid_z), jnp.float32)
    for cells_ref, values_ref, shift in ((recv_cells, recv_values, 0), (bound_cells, bound_force, bits_z)):
        for begin in range(0, cells_ref.shape[-1], chunk):
            cells = cells_ref[0:1, begin : begin + chunk]
            across = cells >> shift
            depth = cells & (grid_z - 1) if shift else jnp.zeros_like(cells)
            cell_x = (across >> bits_y) - start_x
            cell_y = (across & (grid_y - 1)) - start_y
            near = (cell_x >= -2) & (cell_x < size_x + 2) & (cell_y >= -2) & (cell_y < size_y + 2)
            wrapped = jnp.where(cell_y < 0, cell_y + 24, cell_y)
            ring_row = jnp.where(near, (cell_x + 2) * 24 + wrapped, -1)
            inside = (cell_x >= 0) & (cell_x < size_x) & (cell_y >= 0) & (cell_y < size_y)
            inner_row = jnp.where(inside, cell_x * size_y + cell_y, -1)
            ring_hit = lax.broadcasted_iota(jnp.int32, (ring, chunk), 0) == ring_row
            inner_hit = lax.broadcasted_iota(jnp.int32, (inner, chunk), 0) == inner_row
            columns = lax.broadcasted_iota(jnp.int32, (grid_z, chunk), 0) == depth
            columns = jnp.where(columns, 1.0, 0.0).astype(jnp.bfloat16)
            pieces = []
            parts = []
            for step in range(2):
                value = values_ref[step : step + 1, begin : begin + chunk]
                split = []
                for _ in range(3):
                    top = value.astype(jnp.bfloat16).astype(jnp.float32)
                    split.append(top)
                    value = value - top
                parts.append(split)
            for number in range(3):
                pieces.append(jnp.where(ring_hit, parts[0][number], 0.0).astype(jnp.bfloat16))
                pieces.append(jnp.where(inner_hit, parts[1][number], 0.0).astype(jnp.bfloat16))
            total = total + lax.dot_general(
                jnp.concatenate(pieces, axis=0),
                columns,
                (((1,), (1,)), ((), ())),
                preferred_element_type=jnp.float32,
            )
    rows = ring + inner
    out[...] = total[0:rows] + total[rows : 2 * rows] + total[2 * rows : 3 * rows]


def fields_of(loc, far, near, odds, evens):
    size_x = loc.shape[0] // FIELDS
    high, low = from_both(evens, odds)
    half = WIDE * (size_x + 8) // 2
    wide_edge = cut(unpack(high[:half], low[:half], 2), size_x + 8)
    narrow_edge = cut(unpack(high[half:], low[half:], 4), size_x + 4)
    parts = [tiles_of(loc, near, far, size_x, part) for part in range(2)]
    wide = [[parts[0][0][n], parts[1][0][n], wide_edge[n]] for n in range(WIDE)]
    narrow = [[parts[0][1][n], parts[1][1][n], narrow_edge[n]] for n in range(NARROW)]
    return wide, narrow, wide_edge[2:4]


def first_step_kernel(grid_y, source, loc, far_x, near_x, odds, evens, normal, inject, grads, edge_normal):
    size_x, size_y = loc.shape[0] // FIELDS, loc.shape[1]
    count = size_x + 4
    wide, narrow, angles = fields_of(loc, far_x, near_x, odds, evens)
    fields = [[tile[2 : 2 + count] for tile in wide[n]] for n in range(2)]
    edge = normal_of(*angles)
    for axis in range(3):
        edge_normal[axis] = edge[axis]
    normals = [
        [normal[axis, 0, 2 : 2 + count], normal[axis, 1, 2 : 2 + count], edge[axis][2 : 2 + count]]
        for axis in range(3)
    ]
    products = [[normals[a][i] * normals[b][i] for i in range(3)] for a, b in PAIRS]
    mid = slice(2, 2 + size_x)
    p_next = adjoint(products, fields[0], size_x, 2, False)
    q_next = adjoint(products, fields[1], size_x, 2, True)
    inner = [[tile[mid] for tile in entry] for entry in products]
    images = [forward_image(inner, field, size_x) for field in narrow[5:7]]
    ring = inject[0 : count * 24].reshape(count, 24, 128)
    bits_y = grid_y.bit_length() - 1
    source_x = (source[0] >> bits_y) - lax.axis_index("gx") * size_x
    source_y = (source[0] & (grid_y - 1)) - lax.axis_index("gy") * size_y
    shape = (size_x, 8, 128)
    offset_x = lax.broadcasted_iota(jnp.int32, shape, 0) - source_x

    def block(field, ys):
        return loc[field * size_x : (field + 1) * size_x, ys, :]

    for i in range(2):
        ys = slice(8 * i, 8 * i + 8)
        offset_y = lax.broadcasted_iota(jnp.int32, shape, 1) + (8 * i - source_y)
        squared = (offset_x * offset_x + offset_y * offset_y).astype(jnp.float32)
        taper = jnp.minimum(squared * (1.0 / float(TAPER * TAPER)), 1.0)
        scale = taper * (2.0 * block(WIDE + 4, ys))
        image0, image1 = scale * images[0][i], scale * images[1][i]
        p_mid = block(WIDE, ys) + p_next[i] + ring[mid, ys, :]
        q_mid = block(WIDE + 1, ys) + q_next[i]
        grads[0, :, ys, :] = block(FIELDS - 2, ys) * image0 + p_mid * image1
        grads[1, :, ys, :] = block(FIELDS - 1, ys) * image0 + q_mid * image1
        f0, f1 = block(WIDE + 5, ys), block(WIDE + 6, ys)
        grads[2, :, ys, :] = f0 * f0 + f1 * f1


def second_step_kernel(loc, far_x, near_x, odds, evens, normal, edge_normal, inject, p_out, q_out):
    size_x, size_y = p_out.shape[0], p_out.shape[1]
    count = size_x + 4
    wide, narrow, _ = fields_of(loc, far_x, near_x, odds, evens)
    normals = [[normal[axis, 0], normal[axis, 1], edge_normal[axis]] for axis in range(3)]
    products = [[normals[a][i] * normals[b][i] for i in range(3)] for a, b in PAIRS]
    p_base, q_base, p_weight, q_weight, speed = narrow[:5]
    mid = slice(2, 2 + size_x)
    p_next = adjoint(products, wide[0], count, 3, False)
    q_next = adjoint(products, wide[1], count, 3, True)
    ring = inject[0 : count * 24].reshape(count, 24, 128)
    p_next = [p_base[i] + p_next[i] + ring[:, 8 * i : 8 * i + 8] for i in range(3)]
    q_next = [q_base[i] + q_next[i] for i in range(3)]
    source = [p_weight[i] * p_next[i] + q_weight[i] * q_next[i] for i in range(3)]
    mix = [speed[i] * (p_next[i] + q_next[i]) for i in range(3)]
    products = [[tile[2 : 2 + count] for tile in entry] for entry in products]
    p_last = adjoint(products, source, size_x, 2, False)
    q_last = adjoint(products, mix, size_x, 2, True)
    inner = inject[count * 24 :].reshape(size_x, size_y, 128)
    p = loc[(FIELDS - 2) * size_x : (FIELDS - 1) * size_x]
    q = loc[(FIELDS - 1) * size_x : FIELDS * size_x]
    for i in range(2):
        ys = slice(8 * i, 8 * i + 8)
        p_out[:, ys, :] = 2.0 * p_next[i][mid] - p[:, ys] + inner[:, ys] + p_last[i]
        q_out[:, ys, :] = 2.0 * q_next[i][mid] - q[:, ys] + q_last[i]


def shot_round(part, even, odd):
    count = lax.axis_size("gx")
    pairs = []
    for shot in range(lax.axis_size("shot")):
        for place in range(count):
            other = shot ^ (odd if place % 2 else even)
            pairs.append((shot * count + place, other * count + place))
    return lax.ppermute(part, ("shot", "gx"), pairs)


def finish_kernel(own, other, grad_e, grad_d):
    total = [own[i] + other[i] for i in range(3)]
    scale = 1.0 / jnp.sqrt(total[2] + 1.0)
    grad_e[...] = total[0] * scale
    grad_d[...] = total[1] * scale


def swap(part, axis, start):
    lows = range(start, lax.axis_size(axis) - 1, 2)
    return lax.ppermute(part, axis, [(i, i + 1) for i in lows] + [(i + 1, i) for i in lows])


def body(
    p_adjoint,
    q_adjoint,
    p_previous,
    q_previous,
    forward_p,
    courant,
    epsilon,
    delta_field,
    tilt_angle,
    azimuth,
    receiver_cells,
    receiver_values,
    boundary_cells,
    boundary_force,
    source_cells,
):
    _, size_x, size_y, size_z = p_adjoint.shape
    grid_y = size_y * lax.axis_size("gy")
    p, q, p_old, q_old, f = (
        entry[0] for entry in (p_adjoint, q_adjoint, p_previous, q_previous, forward_p)
    )
    message = WIDE * size_x + NARROW * 2
    inputs = (p, q, p_old, q_old, f, courant, epsilon, delta_field, tilt_angle, azimuth)
    loc, far, near = call(
        prepare_kernel,
        [(FIELDS * size_x, size_y, size_z)] + [(message, size_y, size_z)] * 2,
        inputs,
        scratch=[pltpu.VMEM(entry.shape, entry.dtype) for entry in inputs]
        + [pltpu.SemaphoreType.DMA((len(inputs),))],
        space=pltpu.HBM,
    )
    far = swap(far, "gx", 1)
    near = swap(near, "gx", 0)
    rows = (size_x + 4) * 24 + size_x * size_y
    (inject,) = call(
        functools.partial(inject_kernel, grid_y, size_z, size_x, size_y),
        [(rows, size_z)],
        (receiver_cells, receiver_values[0], boundary_cells[None], boundary_force[0]),
        flops=800_000_000,
    )
    edges = (loc, far, near)
    tiles = WIDE * (size_x + 8) // 2 + NARROW * (size_x + 4) // 4
    odds, evens = call(pack_kernel, [(tiles, 8, size_z)] * 2, edges)
    odds, evens = swap(odds, "gy", 1), swap(evens, "gy", 0)
    (normal,) = call(normal_kernel, [(3, 2, size_x + 8, 8, size_z)], edges)
    grads, edge_normal = call(
        functools.partial(first_step_kernel, grid_y),
        [(3, size_x, size_y, size_z), (3, size_x + 8, 8, size_z)],
        (source_cells, *edges, odds, evens, normal, inject),
        smem=(0,),
    )
    grads = grads + shot_round(grads, 1, 3)
    other = shot_round(grads, 3, 1)
    p_final, q_final = call(
        second_step_kernel,
        [(size_x, size_y, size_z)] * 2,
        (*edges, odds, evens, normal, edge_normal, inject),
        flops=20_000_000,
    )
    grad_e, grad_d = call(finish_kernel, [(size_x, size_y, size_z)] * 2, (grads, other))
    return (p_final[None], q_final[None], grad_e, grad_d)


def solution(mesh):
    in_specs = (
        P("shot", "gx", "gy", None),
        P("shot", "gx", "gy", None),
        P("shot", "gx", "gy", None),
        P("shot", "gx", "gy", None),
        P("shot", None, "gx", "gy", None),
        P("gx", "gy", None),
        P("gx", "gy", None),
        P("gx", "gy", None),
        P("gx", "gy", None),
        P("gx", "gy", None),
        P("shot", None),
        P("shot", None, None),
        P(),
        P("shot", None, None),
        P("shot"),
    )
    out_specs = (
        P("shot", "gx", "gy", None),
        P("shot", "gx", "gy", None),
        P("gx", "gy", None),
        P("gx", "gy", None),
    )
    return jax.shard_map(body, mesh=mesh, in_specs=in_specs, out_specs=out_specs, check_vma=False)
```

```python
import functools

import jax
import jax.numpy as jnp
from jax import lax
from jax.experimental import pallas as pl
from jax.experimental.pallas import tpu as pltpu
from jax.sharding import PartitionSpec as P

TAPER = 32
WIDE = 4
NARROW = 7
FIELDS = WIDE + NARROW + 2
INPUTS = ("p", "q", "p_old", "q_old", "f", "c", "eps", "delta", "tilt", "azimuth")
PAIRS = ((0, 0), (1, 1), (2, 2), (0, 1), (0, 2), (1, 2))


def call(kernel, outs, args, scratch=(), smem=(), flops=2_000_000, space=pltpu.VMEM):
    specs = [
        pl.BlockSpec(memory_space=pltpu.SMEM if i in smem else space) for i in range(len(args))
    ]
    shapes = [jax.ShapeDtypeStruct(shape, jnp.float32) for shape in outs]
    return pl.pallas_call(
        kernel,
        out_shape=shapes,
        in_specs=specs,
        out_specs=[pl.BlockSpec(memory_space=pltpu.VMEM)] * len(outs),
        scratch_shapes=list(scratch),
        compiler_params=pltpu.CompilerParams(vmem_limit_bytes=24 * 1024 * 1024),
        cost_estimate=pl.CostEstimate(flops=flops, bytes_accessed=2_000_000, transcendentals=0),
    )(*(pltpu.with_memory_space_constraint(x, space) if space == pltpu.HBM else x for x in args))


def row_mask(shape, below):
    return lax.broadcasted_iota(jnp.int32, shape, len(shape) - 2) < below


def shift_y(tiles, step, keep=3):
    if step > 0:
        rolled = [pltpu.roll(tile, 8 - step, 1) for tile in tiles]
        mask = row_mask(tiles[0].shape, 8 - step)
        return [jnp.where(mask, rolled[i], rolled[(i + 1) % 3]) for i in range(keep)]
    rolled = [pltpu.roll(tile, -step, 1) for tile in tiles]
    mask = row_mask(tiles[0].shape, -step)
    return [jnp.where(mask, rolled[(i + 2) % 3], rolled[i]) for i in range(keep)]


def shift_z(tile, step):
    lane = lax.broadcasted_iota(jnp.int32, tile.shape, 2)
    rolled = pltpu.roll(tile, (-step) % 128, 2)
    inside = lane < 128 - step if step > 0 else lane >= -step
    return jnp.where(inside, rolled, 0.0)


def second(far_low, low, here, high, far_high):
    return (4.0 / 3.0) * (low + high) - (1.0 / 12.0) * (far_low + far_high) - 2.5 * here


def first(far_low, low, high, far_high):
    return (2.0 / 3.0) * (high - low) - (1.0 / 12.0) * (far_high - far_low)


def second_x(tile, count):
    return second(*[tile[i : i + count] for i in range(5)])


def first_x(tile, count):
    return first(*[tile[i : i + count] for i in (0, 1, 3, 4)])


def first_y(tiles, keep):
    low2, low1, high1, high2 = [shift_y(tiles, step, keep) for step in (-2, -1, 1, 2)]
    return [first(low2[i], low1[i], high1[i], high2[i]) for i in range(keep)]


def both(parts_second, parts_first):
    near_even = (4.0 / 3.0) * parts_second
    near_odd = (2.0 / 3.0) * parts_first
    far_even = (-1.0 / 12.0) * parts_second
    far_odd = (1.0 / 12.0) * parts_first
    return (far_even + far_odd, near_even - near_odd, near_even + near_odd, far_even - far_odd)


def adjoint(products, source, count, keep, plus):
    mid = slice(2, 2 + count)
    aa = []
    for axis in range(3):
        scaled = [products[axis][i] * source[i] for i in range(3)]
        aa.append(scaled if plus else [source[i] - scaled[i] for i in range(3)])
    factor = 2.0 if plus else -2.0
    doubled = [factor * tile for tile in source]
    n01 = [products[3][i] * doubled[i] for i in range(3)]
    n02 = [products[4][i] * doubled[i] for i in range(keep)]
    n12 = [products[5][i][mid] * doubled[i][mid] for i in range(3)]
    out = [second_x(aa[0][i], count) for i in range(keep)]
    second_y = [tile[mid] for tile in aa[1]]
    cross_y = [first_x(tile, count) for tile in n01]
    mixed = [both(second_y[i], cross_y[i]) for i in range(3)]
    out = [out[i] - 2.5 * second_y[i] for i in range(keep)]
    for number, step in enumerate((-2, -1, 1, 2)):
        moved = shift_y([mixed[i][number] for i in range(3)], step, keep)
        out = [out[i] + moved[i] for i in range(keep)]
    along_y = first_y(n12, keep)
    for i in range(keep):
        second_z = aa[2][i][mid]
        cross_z = first_x(n02[i], count) + along_y[i]
        terms = both(second_z, cross_z)
        out[i] = out[i] - 2.5 * second_z
        for number, step in enumerate((-2, -1, 1, 2)):
            out[i] = out[i] + shift_z(terms[number], step)
    return out


def forward_image(products, field, count):
    mid = slice(2, 2 + count)
    inner = [tile[mid] for tile in field]
    slope_x = [first_x(tile, count) for tile in field]
    moved = [shift_y(inner, step, 2) for step in (-2, -1, 1, 2)]
    cross = first_y(slope_x, 2)
    out = []
    for i in range(2):
        here = inner[i]
        along = [moved[k][i] for k in range(4)]
        curve_x = second_x(field[i], count)
        curve_y = second(along[0], along[1], here, along[2], along[3])
        slope_y = first(*along)
        depth = [shift_z(here, step) for step in (-2, -1, 1, 2)]
        curve_z = second(depth[0], depth[1], here, depth[2], depth[3])
        total = (1.0 - products[0][i]) * curve_x
        total = total + (1.0 - products[1][i]) * curve_y
        total = total + (1.0 - products[2][i]) * curve_z
        cross_z = []
        for slope in (slope_x[i], slope_y):
            cross_z.append(first(*[shift_z(slope, step) for step in (-2, -1, 1, 2)]))
        mixed = products[3][i] * cross[i] + products[4][i] * cross_z[0] + products[5][i] * cross_z[1]
        out.append(total - 2.0 * mixed)
    return out


def prepare_kernel(*refs):
    count = len(INPUTS)
    arrays, (loc, far, near), held, arrived = refs[:count], refs[count : count + 3], refs[-count - 1 : -1], refs[-1]
    copies = [pltpu.make_async_copy(arrays[i], held[i], arrived.at[i]) for i in range(count)]
    for copy in copies:
        copy.start()
    for copy in copies:
        copy.wait()
    p, q, p_old, q_old, f, c, eps, delta, tilt, azimuth = held
    size_x = p.shape[0]
    p_now, q_now, speed = p[...], q[...], c[...]
    p_weight = speed * (1.0 + 2.0 * eps[...])
    q_weight = speed * (1.0 + 2.0 * delta[...])
    wide = (
        p_weight * p_now + q_weight * q_now,
        speed * (p_now + q_now),
        tilt[...],
        azimuth[...],
    )
    narrow = (
        2.0 * p_now - p_old[...],
        2.0 * q_now - q_old[...],
        p_weight,
        q_weight,
        speed,
        f[0],
        f[1],
    )
    for number, cells in enumerate(wide):
        rows = slice(number * size_x, (number + 1) * size_x)
        loc[rows] = cells
        near[rows] = cells
        far[rows] = cells
    for number, cells in enumerate(narrow + (p_now, q_now)):
        start = (WIDE + number) * size_x
        loc[start : start + size_x] = cells
    odd = lax.rem(lax.axis_index("gx"), 2)
    upper, lower = (1 - odd) * (size_x - 2), odd * (size_x - 2)
    for number in range(NARROW):
        start = (WIDE + number) * size_x
        begin = WIDE * size_x + 2 * number
        near[begin : begin + 2] = loc[pl.ds(start + upper, 2)]
        far[begin : begin + 2] = loc[pl.ds(start + lower, 2)]


def tiles_of(loc, near, far, size_x, part):
    ys = slice(8 * part, 8 * part + 8)
    odd = lax.rem(lax.axis_index("gx"), 2) == 1
    first, second = near[:, ys, :], far[:, ys, :]
    below, above = jnp.where(odd, first, second), jnp.where(odd, second, first)
    wide, narrow = [], []
    for number in range(WIDE):
        rows = slice(number * size_x, (number + 1) * size_x)
        wide.append(jnp.concatenate([below[rows], loc[rows, ys, :], above[rows]], axis=0))
    for number in range(NARROW):
        start = (WIDE + number) * size_x
        begin = WIDE * size_x + 2 * number
        rows = slice(begin, begin + 2)
        here = loc[start : start + size_x, ys, :]
        narrow.append(jnp.concatenate([below[rows], here, above[rows]], axis=0))
    return wide, narrow


def turn(rows, by):
    by = by % 8
    return pltpu.roll(rows, by, 1) if by else rows


def pack(rows, part, groups):
    height, count = 8 // groups, rows.shape[0] // groups
    out = None
    for group in range(groups):
        piece = turn(rows[group * count : (group + 1) * count], height * (group - part * (groups - 1)))
        mask = row_mask(piece.shape, height * group)
        out = piece if out is None else jnp.where(mask, out, piece)
    return out


def unpack(high, low, groups):
    height = 8 // groups
    edges = []
    for group in range(groups):
        upper = turn(high, -height * group)
        lower = turn(low, height * (groups - 1 - group))
        edges.append(jnp.where(row_mask(high.shape, 4), upper, lower))
    return jnp.concatenate(edges, axis=0)


def send_both(parts, evens, odds, start):
    odd = lax.rem(lax.axis_index("gx") + lax.axis_index("gy"), 2) == 1
    rows = slice(start, start + parts[0].shape[0])
    evens[rows] = jnp.where(odd, parts[0], parts[1])
    odds[rows] = jnp.where(odd, parts[1], parts[0])


def from_both(evens, odds):
    odd = lax.rem(lax.axis_index("gx") + lax.axis_index("gy"), 2) == 1
    return jnp.where(odd, odds[...], evens[...]), jnp.where(odd, evens[...], odds[...])


def pack_kernel(loc, far, near, odds, evens):
    size_x = loc.shape[0] // FIELDS
    wides, narrows = [], []
    for part in range(2):
        wide, narrow = tiles_of(loc, near, far, size_x, part)
        wides.append(pack(jnp.concatenate(wide, axis=0), part, 2))
        narrows.append(pack(jnp.concatenate(narrow, axis=0), part, 4))
    send_both(wides, evens, odds, 0)
    send_both(narrows, evens, odds, wides[0].shape[0])


def normal_of(tilt, azimuth):
    sine = jnp.sin(tilt)
    return sine * jnp.cos(azimuth), sine * jnp.sin(azimuth), jnp.cos(tilt)


def normal_kernel(loc, far, near, out):
    size_x = loc.shape[0] // FIELDS
    for part in range(2):
        wide, _ = tiles_of(loc, near, far, size_x, part)
        for axis, cells in enumerate(normal_of(wide[2], wide[3])):
            out[axis, part] = cells


def cut(rows, count):
    return [rows[i : i + count] for i in range(0, rows.shape[0], count)]


def inject_kernel(grid_y, grid_z, size_x, size_y, recv_cells, recv_values, bound_cells, bound_force, out):
    bits_y, bits_z = grid_y.bit_length() - 1, grid_z.bit_length() - 1
    start_x = lax.axis_index("gx") * size_x
    start_y = lax.axis_index("gy") * size_y
    ring = (size_x + 4) * 24
    inner = size_x * size_y
    chunk = 512
    total = jnp.zeros((3 * (ring + inner), grid_z), jnp.float32)
    for cells_ref, values_ref, shift in ((recv_cells, recv_values, 0), (bound_cells, bound_force, bits_z)):
        for begin in range(0, cells_ref.shape[-1], chunk):
            cells = cells_ref[0:1, begin : begin + chunk]
            across = cells >> shift
            depth = cells & (grid_z - 1) if shift else jnp.zeros_like(cells)
            cell_x = (across >> bits_y) - start_x
            cell_y = (across & (grid_y - 1)) - start_y
            near = (cell_x >= -2) & (cell_x < size_x + 2) & (cell_y >= -2) & (cell_y < size_y + 2)
            wrapped = jnp.where(cell_y < 0, cell_y + 24, cell_y)
            ring_row = jnp.where(near, (cell_x + 2) * 24 + wrapped, -1)
            inside = (cell_x >= 0) & (cell_x < size_x) & (cell_y >= 0) & (cell_y < size_y)
            inner_row = jnp.where(inside, cell_x * size_y + cell_y, -1)
            ring_hit = lax.broadcasted_iota(jnp.int32, (ring, chunk), 0) == ring_row
            inner_hit = lax.broadcasted_iota(jnp.int32, (inner, chunk), 0) == inner_row
            columns = lax.broadcasted_iota(jnp.int32, (grid_z, chunk), 0) == depth
            columns = jnp.where(columns, 1.0, 0.0).astype(jnp.bfloat16)
            pieces = []
            parts = []
            for step in range(2):
                value = values_ref[step : step + 1, begin : begin + chunk]
                split = []
                for _ in range(3):
                    top = value.astype(jnp.bfloat16).astype(jnp.float32)
                    split.append(top)
                    value = value - top
                parts.append(split)
            for number in range(3):
                pieces.append(jnp.where(ring_hit, parts[0][number], 0.0).astype(jnp.bfloat16))
                pieces.append(jnp.where(inner_hit, parts[1][number], 0.0).astype(jnp.bfloat16))
            total = total + lax.dot_general(
                jnp.concatenate(pieces, axis=0),
                columns,
                (((1,), (1,)), ((), ())),
                preferred_element_type=jnp.float32,
            )
    rows = ring + inner
    out[...] = total[0:rows] + total[rows : 2 * rows] + total[2 * rows : 3 * rows]


def fields_of(loc, far, near, odds, evens):
    size_x = loc.shape[0] // FIELDS
    high, low = from_both(evens, odds)
    half = WIDE * (size_x + 8) // 2
    wide_edge = cut(unpack(high[:half], low[:half], 2), size_x + 8)
    narrow_edge = cut(unpack(high[half:], low[half:], 4), size_x + 4)
    parts = [tiles_of(loc, near, far, size_x, part) for part in range(2)]
    wide = [[parts[0][0][n], parts[1][0][n], wide_edge[n]] for n in range(WIDE)]
    narrow = [[parts[0][1][n], parts[1][1][n], narrow_edge[n]] for n in range(NARROW)]
    return wide, narrow, wide_edge[2:4]


def first_step_kernel(grid_y, source, loc, far_x, near_x, odds, evens, normal, inject, grads, edge_normal):
    size_x, size_y = loc.shape[0] // FIELDS, loc.shape[1]
    count = size_x + 4
    wide, narrow, angles = fields_of(loc, far_x, near_x, odds, evens)
    fields = [[tile[2 : 2 + count] for tile in wide[n]] for n in range(2)]
    edge = normal_of(*angles)
    for axis in range(3):
        edge_normal[axis] = edge[axis]
    normals = [
        [normal[axis, 0, 2 : 2 + count], normal[axis, 1, 2 : 2 + count], edge[axis][2 : 2 + count]]
        for axis in range(3)
    ]
    products = [[normals[a][i] * normals[b][i] for i in range(3)] for a, b in PAIRS]
    mid = slice(2, 2 + size_x)
    p_next = adjoint(products, fields[0], size_x, 2, False)
    q_next = adjoint(products, fields[1], size_x, 2, True)
    inner = [[tile[mid] for tile in entry] for entry in products]
    images = [forward_image(inner, field, size_x) for field in narrow[5:7]]
    ring = inject[0 : count * 24].reshape(count, 24, 128)
    bits_y = grid_y.bit_length() - 1
    source_x = (source[0] >> bits_y) - lax.axis_index("gx") * size_x
    source_y = (source[0] & (grid_y - 1)) - lax.axis_index("gy") * size_y
    shape = (size_x, 8, 128)
    offset_x = lax.broadcasted_iota(jnp.int32, shape, 0) - source_x

    def block(field, ys):
        return loc[field * size_x : (field + 1) * size_x, ys, :]

    for i in range(2):
        ys = slice(8 * i, 8 * i + 8)
        offset_y = lax.broadcasted_iota(jnp.int32, shape, 1) + (8 * i - source_y)
        squared = (offset_x * offset_x + offset_y * offset_y).astype(jnp.float32)
        taper = jnp.minimum(squared * (1.0 / float(TAPER * TAPER)), 1.0)
        scale = taper * (2.0 * block(WIDE + 4, ys))
        image0, image1 = scale * images[0][i], scale * images[1][i]
        p_mid = block(WIDE, ys) + p_next[i] + ring[mid, ys, :]
        q_mid = block(WIDE + 1, ys) + q_next[i]
        grads[0, :, ys, :] = block(FIELDS - 2, ys) * image0 + p_mid * image1
        grads[1, :, ys, :] = block(FIELDS - 1, ys) * image0 + q_mid * image1
        f0, f1 = block(WIDE + 5, ys), block(WIDE + 6, ys)
        grads[2, :, ys, :] = f0 * f0 + f1 * f1


def second_step_kernel(loc, far_x, near_x, odds, evens, normal, edge_normal, inject, p_out, q_out):
    size_x, size_y = p_out.shape[0], p_out.shape[1]
    count = size_x + 4
    wide, narrow, _ = fields_of(loc, far_x, near_x, odds, evens)
    normals = [[normal[axis, 0], normal[axis, 1], edge_normal[axis]] for axis in range(3)]
    products = [[normals[a][i] * normals[b][i] for i in range(3)] for a, b in PAIRS]
    p_base, q_base, p_weight, q_weight, speed = narrow[:5]
    mid = slice(2, 2 + size_x)
    p_next = adjoint(products, wide[0], count, 3, False)
    q_next = adjoint(products, wide[1], count, 3, True)
    ring = inject[0 : count * 24].reshape(count, 24, 128)
    p_next = [p_base[i] + p_next[i] + ring[:, 8 * i : 8 * i + 8] for i in range(3)]
    q_next = [q_base[i] + q_next[i] for i in range(3)]
    source = [p_weight[i] * p_next[i] + q_weight[i] * q_next[i] for i in range(3)]
    mix = [speed[i] * (p_next[i] + q_next[i]) for i in range(3)]
    products = [[tile[2 : 2 + count] for tile in entry] for entry in products]
    p_last = adjoint(products, source, size_x, 2, False)
    q_last = adjoint(products, mix, size_x, 2, True)
    inner = inject[count * 24 :].reshape(size_x, size_y, 128)
    p = loc[(FIELDS - 2) * size_x : (FIELDS - 1) * size_x]
    q = loc[(FIELDS - 1) * size_x : FIELDS * size_x]
    for i in range(2):
        ys = slice(8 * i, 8 * i + 8)
        p_out[:, ys, :] = 2.0 * p_next[i][mid] - p[:, ys] + inner[:, ys] + p_last[i]
        q_out[:, ys, :] = 2.0 * q_next[i][mid] - q[:, ys] + q_last[i]


def swap_y(part, start):
    count = lax.axis_size("gy")
    pairs = []
    for place in range(lax.axis_size("gx")):
        for low in range((start + place) % 2, count - 1, 2):
            low = place * count + low
            pairs += [(low, low + 1), (low + 1, low)]
    return lax.ppermute(part, ("gx", "gy"), pairs)


def shot_round(part, even, odd):
    count = lax.axis_size("gx")
    pairs = []
    for shot in range(lax.axis_size("shot")):
        for place in range(count):
            other = shot ^ (odd if place % 2 else even)
            pairs.append((shot * count + place, other * count + place))
    return lax.ppermute(part, ("shot", "gx"), pairs)


def finish_kernel(own, other, grad_e, grad_d):
    total = [own[i] + other[i] for i in range(3)]
    scale = 1.0 / jnp.sqrt(total[2] + 1.0)
    grad_e[...] = total[0] * scale
    grad_d[...] = total[1] * scale


def swap(part, axis, start):
    lows = range(start, lax.axis_size(axis) - 1, 2)
    return lax.ppermute(part, axis, [(i, i + 1) for i in lows] + [(i + 1, i) for i in lows])


def body(
    p_adjoint,
    q_adjoint,
    p_previous,
    q_previous,
    forward_p,
    courant,
    epsilon,
    delta_field,
    tilt_angle,
    azimuth,
    receiver_cells,
    receiver_values,
    boundary_cells,
    boundary_force,
    source_cells,
):
    _, size_x, size_y, size_z = p_adjoint.shape
    grid_y = size_y * lax.axis_size("gy")
    p, q, p_old, q_old, f = (
        entry[0] for entry in (p_adjoint, q_adjoint, p_previous, q_previous, forward_p)
    )
    message = WIDE * size_x + NARROW * 2
    inputs = (p, q, p_old, q_old, f, courant, epsilon, delta_field, tilt_angle, azimuth)
    loc, far, near = call(
        prepare_kernel,
        [(FIELDS * size_x, size_y, size_z)] + [(message, size_y, size_z)] * 2,
        inputs,
        scratch=[pltpu.VMEM(entry.shape, entry.dtype) for entry in inputs]
        + [pltpu.SemaphoreType.DMA((len(inputs),))],
        space=pltpu.HBM,
    )
    far = swap(far, "gx", 1)
    near = swap(near, "gx", 0)
    rows = (size_x + 4) * 24 + size_x * size_y
    (inject,) = call(
        functools.partial(inject_kernel, grid_y, size_z, size_x, size_y),
        [(rows, size_z)],
        (receiver_cells, receiver_values[0], boundary_cells[None], boundary_force[0]),
        flops=800_000_000,
    )
    edges = (loc, far, near)
    tiles = WIDE * (size_x + 8) // 2 + NARROW * (size_x + 4) // 4
    odds, evens = call(pack_kernel, [(tiles, 8, size_z)] * 2, edges)
    odds, evens = swap_y(odds, 1), swap_y(evens, 0)
    (normal,) = call(normal_kernel, [(3, 2, size_x + 8, 8, size_z)], edges)
    grads, edge_normal = call(
        functools.partial(first_step_kernel, grid_y),
        [(3, size_x, size_y, size_z), (3, size_x + 8, 8, size_z)],
        (source_cells, *edges, odds, evens, normal, inject),
        smem=(0,),
    )
    grads = grads + shot_round(grads, 1, 3)
    other = shot_round(grads, 3, 1)
    p_final, q_final = call(
        second_step_kernel,
        [(size_x, size_y, size_z)] * 2,
        (*edges, odds, evens, normal, edge_normal, inject),
        flops=20_000_000,
    )
    grad_e, grad_d = call(finish_kernel, [(size_x, size_y, size_z)] * 2, (grads, other))
    return (p_final[None], q_final[None], grad_e, grad_d)


def solution(mesh):
    in_specs = (
        P("shot", "gx", "gy", None),
        P("shot", "gx", "gy", None),
        P("shot", "gx", "gy", None),
        P("shot", "gx", "gy", None),
        P("shot", None, "gx", "gy", None),
        P("gx", "gy", None),
        P("gx", "gy", None),
        P("gx", "gy", None),
        P("gx", "gy", None),
        P("gx", "gy", None),
        P("shot", None),
        P("shot", None, None),
        P(),
        P("shot", None, None),
        P("shot"),
    )
    out_specs = (
        P("shot", "gx", "gy", None),
        P("shot", "gx", "gy", None),
        P("gx", "gy", None),
        P("gx", "gy", None),
    )
    return jax.shard_map(body, mesh=mesh, in_specs=in_specs, out_specs=out_specs, check_vma=False)
```
